128 devices in a mesh: wide: 16 (over y, x_hi, core), narrow: 8 (over x_lo, z).
Axes of the slice: x: 4 (x_hi: 2, x_lo: 2; x = x_hi * 2 + x_lo), y: 4, z: 4, core: 2. Of those that a mesh axis runs over, the one named last changes fastest.
Arguments:
- patches: bfloat16 [31360, 1024], P(('wide', 'narrow')), may hold values from -6 to 6
- keep: int32 [640, 49], P(('wide', 'narrow')), may hold values from 0 to 1, as said below
- cotangent: bfloat16 [31360, 1024], P(('wide', 'narrow')), may hold values from -6 to 6
- owner_table: int32 [768], replicated, may hold values from 0 to 767, as said below
- master: float32 [768, 128, 128], P(('wide', 'narrow')), may hold values from -0.1875 to 0.1875
- left_stats: float32 [768, 128, 128], P(('wide', 'narrow'))
- right_stats: float32 [768, 128, 128], P(('wide', 'narrow'))
- left_root: float32 [768, 128, 128], P(('wide', 'narrow'))
- right_root: float32 [768, 128, 128], P(('wide', 'narrow'))
- vectors: float32 [12, 1024], P(None, ('wide', 'narrow'))
- vec_accum: float32 [12, 1024], P(None, ('wide', 'narrow'))
Outputs:
- output: bfloat16 [31360, 1024], P(('wide', 'narrow'))
- input_grad: bfloat16 [31360, 1024], P(('wide', 'narrow'))
- block_grads: float32 [768, 128, 128], P(('wide', 'narrow'))
- new_left: float32 [768, 128, 128], P(('wide', 'narrow'))
- new_right: float32 [768, 128, 128], P(('wide', 'narrow'))
- new_master: float32 [768, 128, 128], P(('wide', 'narrow'))
- new_copy: bfloat16 [768, 128, 128], P(('wide', 'narrow'))
- vec_grads: float32 [12, 1024], P(None, ('wide', 'narrow'))
- vec_accum_new: float32 [12, 1024], P(None, ('wide', 'narrow'))
- vec_new: float32 [12, 1024], P(None, ('wide', 'narrow'))
- grad_norm: float32 [], replicated
The draws below stay inside these ranges and needn't reach their ends.
Inputs may be any that keep to these rules, and one draw needn't show every extreme that they name: `keep`: each image keeps between 25 and 49 of its patches; the first image keeps exactly 25, the last keeps all. `owner_table`: every block number appears in exactly one slot. A block's class is k * 8 // m, with k its block column and m the block columns of its matrix for Wq, Wk, Wv and W_in, and k its block row and m the block rows of its matrix for Wo and W_out. Slot s holds a block of class (s // 6) % 8.
All inputs are finite; a program needn't handle non-finite values.
Results may differ from the reference program's by a relative error of at most 0.017.
Values may be sent and summed in bfloat16 or wider, within the bound.
A program may use at most 448 MiB of HBM per device.

```python
import math
import jax
import jax.numpy as jnp
from jax import lax

D = 1024
HEADS = 16
HEAD_DIM = 64
FF = 4096
PATCHES = 49
MIN_KEEP = 25
BLOCK = 128
IMG_DEV = 5
GROUP = 8
IMAGES = 640
TOKENS = 31360
NBLK = 768
SLOTS = 6
NV = 12
N_WIDE = 16
N_NARROW = 8


def statistic(raw, diag_key, base, side):
    identity = jnp.eye(side, dtype=jnp.float32)
    diagonal = base * jnp.exp(jax.random.uniform(diag_key, (raw.shape[0], side, 1), jnp.float32, 0.0, math.log(4.0)))
    sym_part = (raw + jnp.swapaxes(raw, 1, 2)) * 0.7071
    return identity * diagonal + (1.0 - identity) * sym_part * (0.3 * base / math.sqrt(side))


def root_matrix(raw, diag_key, level, side):
    identity = jnp.eye(side, dtype=jnp.float32)
    diagonal = jnp.exp(jax.random.uniform(diag_key, (raw.shape[0], side, 1), jnp.float32, math.log(0.7), math.log(1.4)))
    sym_part = (raw + jnp.swapaxes(raw, 1, 2)) * 0.7071
    return level * (identity * diagonal + (1.0 - identity) * sym_part * (0.25 / math.sqrt(side)))


def block_layout():
    labels_list = []
    place_list = []
    gained_list = []
    layout_list = [(D // BLOCK, D // BLOCK, True, True)] * 3 + [(D // BLOCK, D // BLOCK, False, False), (D // BLOCK, FF // BLOCK, True, True), (FF // BLOCK, D // BLOCK, False, False)]
    for row_count, col_count, by_column, gained in layout_list:
        row_index = jnp.arange(row_count, dtype=jnp.int32)[:, None]
        col_index = jnp.arange(col_count, dtype=jnp.int32)[None, :]
        if by_column:
            labels = jnp.broadcast_to(col_index * GROUP // col_count, (row_count, col_count))
        else:
            labels = jnp.broadcast_to(row_index * GROUP // row_count, (row_count, col_count))
        place = jnp.broadcast_to(row_index * NBLK // row_count, (row_count, col_count))
        labels_list.append(labels.reshape(-1))
        place_list.append(place.reshape(-1))
        gained_list.append(jnp.full((row_count * col_count,), 1 if gained else 0, jnp.int32))
    return (jnp.concatenate(labels_list, 0), jnp.concatenate(place_list, 0), jnp.concatenate(gained_list, 0))


def draw_owner_table(key, part):
    key = jax.random.fold_in(key, 7)
    shuffle = jax.random.permutation(key, NBLK).astype(jnp.int32)
    classes, place, gained = block_layout()
    fraction = jnp.where(gained > 0, place, shuffle)
    scores = classes * (NBLK * NBLK) + fraction * NBLK + shuffle
    ranked = jnp.argsort(scores, stable=True).astype(jnp.int32)
    slot_index = jnp.arange(NBLK, dtype=jnp.int32)
    device_index = slot_index // SLOTS
    wide_index = device_index // GROUP
    lane_index = device_index % GROUP
    position = lane_index * (NBLK // GROUP) + wide_index * SLOTS + slot_index % SLOTS
    return jnp.take(ranked, position).astype(jnp.int32)


def draw_keep(key, part):
    key = jax.random.fold_in(key, 5)
    first_key, second_key = jax.random.split(key)
    counts = jax.random.randint(first_key, (IMAGES,), MIN_KEEP, PATCHES + 1)
    counts = counts.at[0].set(MIN_KEEP).at[IMAGES - 1].set(PATCHES)
    scores = jax.random.randint(second_key, (IMAGES, PATCHES), 0, 1 << 20) * 64 + jnp.arange(PATCHES, dtype=jnp.int32)[None, :]
    ranks = jnp.argsort(jnp.argsort(scores, axis=1), axis=1)
    return (ranks < counts[:, None]).astype(jnp.int32)


def draw_left_stats(key, part):
    key = jax.random.fold_in(key, 21)
    first_key, second_key = jax.random.split(key)
    base = BLOCK / (4.0 * D * D + 2.0 * D * FF)
    raw = jax.random.normal(first_key, (NBLK, BLOCK, BLOCK), jnp.float32)
    return statistic(raw, second_key, base, BLOCK)


def draw_right_stats(key, part):
    key = jax.random.fold_in(key, 22)
    first_key, second_key = jax.random.split(key)
    base = BLOCK / (4.0 * D * D + 2.0 * D * FF)
    raw = jax.random.normal(first_key, (NBLK, BLOCK, BLOCK), jnp.float32)
    return statistic(raw, second_key, base, BLOCK)


def draw_left_root(key, part):
    key = jax.random.fold_in(key, 31)
    first_key, second_key = jax.random.split(key)
    level = ((4.0 * D * D + 2.0 * D * FF) / BLOCK) ** 0.25
    raw = jax.random.normal(first_key, (NBLK, BLOCK, BLOCK), jnp.float32)
    return root_matrix(raw, second_key, level, BLOCK)


def draw_right_root(key, part):
    key = jax.random.fold_in(key, 32)
    first_key, second_key = jax.random.split(key)
    level = ((4.0 * D * D + 2.0 * D * FF) / BLOCK) ** 0.25
    raw = jax.random.normal(first_key, (NBLK, BLOCK, BLOCK), jnp.float32)
    return root_matrix(raw, second_key, level, BLOCK)


def draw_vectors(key, part):
    key = jax.random.fold_in(key, 41)
    first_key, second_key = jax.random.split(key)
    position = jnp.arange(D, dtype=jnp.float32)[None, :] / (D - 1.0)
    jitter = jax.random.uniform(second_key, (NV, D), jnp.float32, 0.8, 1.2)
    noise = jax.random.normal(first_key, (NV, D), jnp.float32)
    gains = 0.6 * jnp.exp(position * math.log(3.0)) * jitter
    row_index = jnp.arange(NV)[:, None]
    is_gain = (row_index == 0) | (row_index == 5)
    return jnp.where(is_gain, gains, 0.3 * noise)


def draw_vec_accum(key, part):
    key = jax.random.fold_in(key, 51)
    base = 1.0 / (4.0 * D * D + 2.0 * D * FF)
    factor = jnp.exp(jax.random.uniform(key, (NV, D), jnp.float32, 0.0, math.log(4.0)))
    return base * factor


def block_scale(own_key, shape, pieces, least, largest):
    def one(dim, shards_of):
        heights = jax.random.uniform(jax.random.fold_in(jax.random.fold_in(own_key, 6), dim), (shards_of,), jnp.float32, least / len(pieces), largest / len(pieces))
        return jnp.repeat(jnp.exp(heights), shape[dim] // shards_of).reshape((-1,) + (1,) * (len(shape) - dim - 1))

    level = one(*pieces[0])
    for cut in pieces[1:]:
        level = level * one(*cut)
    return level


def normal_values(key, shape, deviation, most, shards=(), held_as=jnp.bfloat16):
    entries = deviation * jax.random.normal(key, shape, jnp.float32)
    if shards:
        entries = entries * block_scale(key, shape, shards, -0.22, 0.18)
    return jnp.clip(entries, -most, most).astype(held_as)


def setup_inputs(seed: int = 0) -> dict:
    key_list = jax.random.split(jax.random.key(seed), 12)
    return {
        "patches": normal_values(key_list[0], (TOKENS, D), 1.0, 6.0, ((0, 128),)),
        "keep": draw_keep(jax.random.fold_in(key_list[11], 71), 0),
        "cotangent": normal_values(key_list[2], (TOKENS, D), 1.0, 6.0, ((0, 128),)),
        "owner_table": draw_owner_table(jax.random.fold_in(key_list[11], 71), 0),
        "master": normal_values(key_list[4], (NBLK, BLOCK, BLOCK), D ** -0.5, 0.1875, ((0, 128),), jnp.float32),
        "left_stats": draw_left_stats(jax.random.fold_in(key_list[11], 71), 0),
        "right_stats": draw_right_stats(jax.random.fold_in(key_list[11], 71), 0),
        "left_root": draw_left_root(jax.random.fold_in(key_list[11], 71), 0),
        "right_root": draw_right_root(jax.random.fold_in(key_list[11], 71), 0),
        "vectors": draw_vectors(jax.random.fold_in(key_list[11], 71), 0),
        "vec_accum": draw_vec_accum(jax.random.fold_in(key_list[11], 71), 0),
    }


@jax.custom_vjp
def low(v):
    return lax.optimization_barrier(v.astype(jnp.bfloat16)).astype(jnp.float32)

@jax.custom_vjp
def low_back(v):
    return v

def low_keep(v):
    return (low(v), None)

def low_pass(kept, grad):
    return (grad,)

def back_keep(v):
    return (v, None)

def back_low(kept, grad):
    return (low(grad),)
low.defvjp(low_keep, low_pass)
low_back.defvjp(back_keep, back_low)
highest = lax.Precision.HIGHEST
layer_eps = 1e-05
masked_score = -1000000000.0
decay = 0.5
matrix_rate = 0.5
vector_rate = 0.5
vector_eps = 1e-08

def both_round(value):
    return low(low_back(value))

def exact_dot(left, right):
    return jnp.dot(left, right, precision=highest, preferred_element_type=jnp.float32)

def layer_norm(values, gain, shift):
    centre = lax.optimization_barrier(jnp.mean(values, -1, keepdims=True))
    centred = values - centre
    spread = lax.optimization_barrier(jnp.mean(centred * centred, -1, keepdims=True))
    return centred * lax.rsqrt(spread + layer_eps) * gain + shift

def matrix_shapes(width, hidden):
    return [(width, width)] * 4 + [(width, hidden), (hidden, width)]

def from_blocks(ordered, width, hidden, side):
    matrices = []
    offset = 0
    for row_count, col_count in matrix_shapes(width, hidden):
        number = row_count // side * (col_count // side)
        segment = ordered[offset:offset + number].reshape(row_count // side, col_count // side, side, side)
        matrices.append(segment.transpose(0, 2, 1, 3).reshape(row_count, col_count))
        offset += number
    return matrices

def to_blocks(matrices, side):
    segments = []
    for matrix in matrices:
        row_count, col_count = matrix.shape
        segments.append(matrix.reshape(row_count // side, side, col_count // side, side).transpose(0, 2, 1, 3).reshape(-1, side, side))
    return jnp.concatenate(segments, 0)

def block_forward(matrices, vector_rows, tokens, mask):
    w_query, w_key, w_value, w_output, w_in, w_out = matrices
    images = mask.shape[0]
    scale = HEAD_DIM ** (-0.5)
    head_shape = (images, PATCHES, HEADS, HEAD_DIM)
    a_first = low(layer_norm(tokens, vector_rows[0], vector_rows[1]))
    queries = both_round(exact_dot(a_first, w_query) + vector_rows[2])
    keys = both_round(exact_dot(a_first, w_key))
    values = both_round(exact_dot(a_first, w_value) + vector_rows[3])
    raw = low_back(jnp.einsum('iqhd,ikhd->ihqk', queries.reshape(head_shape), keys.reshape(head_shape), precision=highest))
    masked = jnp.where(mask[:, None, None, :] > 0, raw * scale, masked_score)
    probs = low(jax.nn.softmax(masked, axis=-1))
    attended = jnp.einsum('ihqk,ikhd->iqhd', probs, values.reshape(head_shape), precision=highest)
    attended = both_round(attended.reshape(tokens.shape))
    middle = tokens + low_back(exact_dot(attended, w_output) + vector_rows[4])
    a_second = low(layer_norm(middle, vector_rows[5], vector_rows[6]))
    pre_act = low_back(exact_dot(a_second, w_in) + vector_rows[8:].reshape(-1))
    activated = low(jax.nn.gelu(pre_act, approximate=False))
    return middle + low_back(exact_dot(activated, w_out) + vector_rows[7])

def reference(patches, keep, cotangent, owner_table, master, left_stats, right_stats, left_root, right_root, vectors, vec_accum):
    order_back = jnp.argsort(owner_table).astype(jnp.int32)
    ordered = jnp.take(low(master), order_back, axis=0)
    matrices = from_blocks(ordered, D, FF, BLOCK)
    vector_low = low(vectors)
    group_images = IMG_DEV * N_NARROW * 2
    groups = N_WIDE // 2
    token_groups = patches.astype(jnp.float32).reshape(groups, group_images * PATCHES, D)
    keep_groups = keep.reshape(groups, group_images, PATCHES)
    step_fn = jax.checkpoint(block_forward)

    def whole(mats_in, vecs_in, toks_in):

        def scan_body(carry, inputs):
            return (carry, step_fn(mats_in, vecs_in, inputs[0], inputs[1]))
        _, results = lax.scan(scan_body, None, (toks_in, keep_groups))
        return results
    result, pullback = jax.vjp(whole, matrices, vector_low, token_groups)
    grad_mats, vec_raw, grad_tokens = pullback(cotangent.astype(jnp.float32).reshape(groups, group_images * PATCHES, D))
    output = result.reshape(TOKENS, D).astype(jnp.bfloat16)
    input_grad = grad_tokens.reshape(TOKENS, D).astype(jnp.bfloat16)
    block_raw = jnp.take(to_blocks(grad_mats, BLOCK), owner_table, axis=0)
    grad_norm = jnp.sqrt(jnp.sum(block_raw * block_raw) + jnp.sum(vec_raw * vec_raw))
    clip = 1.0 / jnp.maximum(grad_norm, 1.0)
    block_grads = clip * block_raw
    vec_grads = clip * vec_raw
    new_left = decay * left_stats + (1.0 - decay) * jnp.einsum('sij,skj->sik', block_grads, block_grads, precision=highest)
    new_right = decay * right_stats + (1.0 - decay) * jnp.einsum('sji,sjk->sik', block_grads, block_grads, precision=highest)
    step_left = jnp.einsum('sij,sjk->sik', left_root, block_grads, precision=highest)
    direction = jnp.einsum('sij,sjk->sik', step_left, right_root, precision=highest)
    new_master = master - matrix_rate * direction
    new_copy = new_master.astype(jnp.bfloat16)
    vec_accum_new = decay * vec_accum + (1.0 - decay) * vec_grads * vec_grads
    vec_new = vectors - vector_rate * vec_grads / (jnp.sqrt(vec_accum_new) + vector_eps)
    return (output, input_grad, block_grads, new_left, new_right, new_master, new_copy, vec_grads, vec_accum_new, vec_new, grad_norm)
```

```python
import functools
import math

import jax
import jax.numpy as jnp
import numpy as np
from jax import lax
from jax.experimental import pallas as pl
from jax.experimental.pallas import tpu as pltpu
from jax.sharding import PartitionSpec as P

MESH = pl.DeviceIdType.MESH
BOTH = ("wide", "narrow")
F32, BF16 = jnp.float32, jnp.bfloat16
MIB = 2**20

D = 1024
FF = 4096
HEADS = 16
HEAD_DIM = 64
PATCHES = 49
IMAGES = 5
TOKENS = IMAGES * PATCHES
ROWS = 256
SIDE = 128
NBLK = 768
NV = 12
LAYER_EPS = 1e-05
MASKED = -1000000000.0
OUTSIDE = -3.0e38
SCALE = HEAD_DIM**-0.5

ORDERS = ((0, 1, 2), (1, 2, 0), (2, 0, 1))
SHARE = (16, 16, 17)
SHARE_FROM = (0, 16, 32)
PART_FROM = (0, 128 * 16, 128 * 32)
ALL_ROWS = 128 * 49
NEXT = (0, 3, 1, 2)

FIRST = (0, 64, 128, 192, 256, 512)
WIDTH = (8, 8, 8, 8, 32, 8)
LEFT_AT = (0, 0, 0, 8, 16, 24)
RIGHT_AT = (0, 8, 16, 24, 32, 64)


def slot_places():
    block_at, vector_at = np.zeros(NBLK, np.int32), np.zeros(128, np.int32)
    for dev in range(128):
        wide, narrow = dev // 8, dev % 8
        core = wide % 2
        pos = (wide // 2 % 2 * 2 + narrow // 4, wide // 4, narrow % 4)
        for p, (a, b, c) in enumerate(ORDERS):
            at = PART_FROM[p] + (((core * 4 + pos[c]) * 4 + pos[b]) * 4 + pos[a]) * SHARE[p]
            block_at[dev * 6 + 2 * p] = at
            block_at[dev * 6 + 2 * p + 1] = at + 8
            if p == 2:
                vector_at[dev] = at + 16
    return block_at, vector_at


BLOCK_AT, VECTOR_AT = slot_places()


def place():
    wide, narrow = lax.axis_index("wide"), lax.axis_index("narrow")
    x = (wide // 2) % 2 * 2 + narrow // 4
    return (x, wide // 4, narrow % 4), wide % 2


def device(pos, core):
    x, y, z = pos
    return ((y * 2 + x // 2) * 2 + core, x % 2 * 4 + z)


def moved(pos, axis, by):
    return tuple((c + by) % 4 if a == axis else c for a, c in enumerate(pos))


def greet(partners):
    barrier = pltpu.get_barrier_semaphore()
    for partner in partners:
        pl.semaphore_signal(barrier, inc=1, device_id=partner, device_id_type=MESH)
    pl.semaphore_wait(barrier, len(partners))


def loop(count, body):
    lax.fori_loop(0, count, lambda i, _: (body(i), None)[1], None)


def dot(left, right):
    return jnp.dot(left, right, preferred_element_type=F32)


def dot_nt(left, right):
    return lax.dot_general(left, right, (((1,), (1,)), ((), ())), preferred_element_type=F32)


def dot_tn(left, right):
    return lax.dot_general(left, right, (((0,), (0,)), ((), ())), preferred_element_type=F32)


def gather_weights(shard, g, local_sem, send_sem, recv_sem):
    pos, core = place()
    twin = device(pos, 1 - core)
    near = {(a, s): device(moved(pos, a, s), core) for a in range(3) for s in (1, -1)}
    greet([twin] + list(near.values()))
    sends = []

    def copy_of(src, dst, p, slot, to):
        return pltpu.make_async_remote_copy(
            src_ref=src, dst_ref=dst, send_sem=send_sem.at[p, slot],
            recv_sem=recv_sem.at[p, slot], device_id=to, device_id_type=MESH,
        )

    def send(src, dst, p, slot, to):
        copy = copy_of(src, dst, p, slot, to)
        copy.start()
        sends.append(copy)

    def arrived(dst, p, slot):
        copy_of(dst, dst, p, slot, twin).wait_recv()

    def at(p, of_core, c, b, a=0, count=4, skip=0, rows=None):
        start = PART_FROM[p] + (((of_core * 4 + c % 4) * 4 + b % 4) * 4 + a % 4) * SHARE[p] + skip
        return g.at[pl.ds(start, count * SHARE[p] if rows is None else rows)]

    def spot(p):
        a, b, c = ORDERS[p]
        return pos[a], pos[b], pos[c]

    def row(p, ci, bi):
        _, b, c = spot(p)
        return at(p, core, c + ci, b + bi)

    def half_row(p, ci, bi, second):
        _, b, c = spot(p)
        return at(p, core, c + ci, b + bi, 2 if second else 0, 2)

    def chunk(p, ai):
        a, b, c = spot(p)
        return at(p, core, c, b, a + ai, 1)

    def half_chunk(p, ai, second):
        a, b, c = spot(p)
        return at(p, core, c, b, a + ai, 1, 8 if second else 0, SHARE[p] - 8 if second else 8)

    def to_twin(p, ci, bi):
        r = row(p, ci, bi)
        send(r, r, p, 24 + 4 * (ci % 4) + bi % 4, twin)

    def onward(p, base, axis, half):
        first, second = half(False), half(True)
        return (
            lambda: send(first, first, p, base + 2, near[axis, 1]),
            lambda: send(second, second, p, base + 3, near[axis, -1]),
        )

    def both(p, base, axis, src, dst):
        send(src, dst, p, base, near[axis, 1])
        send(src, dst, p, base + 1, near[axis, -1])

    parts = range(3)
    held = []
    for p in parts:
        own = shard.at[pl.ds(SHARE_FROM[p], SHARE[p])]
        both(p, 0, ORDERS[p][0], own, chunk(p, 0))
        copy = pltpu.make_async_copy(own, chunk(p, 0), local_sem.at[p])
        copy.start()
        held.append(copy)
    for p in parts:
        axis = ORDERS[p][0]
        arrived(chunk(p, -1), p, 0)
        onward(p, 0, axis, lambda second: half_chunk(p, -1, second))[0]()
        arrived(chunk(p, 1), p, 1)
        onward(p, 0, axis, lambda second: half_chunk(p, 1, second))[1]()
    for p in parts:
        held[p].wait()
        arrived(half_chunk(p, 2, False), p, 2)
        arrived(half_chunk(p, 2, True), p, 3)
        r = row(p, 0, 0)
        both(p, 4, ORDERS[p][1], r, r)
        both(p, 8, ORDERS[p][2], r, r)
        to_twin(p, 0, 0)
    for p in parts:
        for bi, i in ((-1, 1), (1, 2)):
            r = row(p, 0, bi)
            arrived(r, p, 4 + (i - 1))
            onward(p, 4, ORDERS[p][1], lambda second: half_row(p, 0, bi, second))[i - 1]()
            both(p, 8 + 4 * i, ORDERS[p][2], r, r)
            to_twin(p, 0, bi)

    def sides(p, i):
        bi = NEXT[i]
        for ci, j in ((-1, 0), (1, 1)):
            arrived(row(p, ci, bi), p, 8 + 4 * i + j)
            onward(p, 8 + 4 * i, ORDERS[p][2], lambda second: half_row(p, ci, bi, second))[j]()
            to_twin(p, ci, bi)

    def opposite(p, i):
        bi = NEXT[i]
        arrived(half_row(p, 2, bi, False), p, 8 + 4 * i + 2)
        arrived(half_row(p, 2, bi, True), p, 8 + 4 * i + 3)
        to_twin(p, 2, bi)

    for p in parts:
        sides(p, 0)
    for p in parts:
        arrived(half_row(p, 0, 2, False), p, 6)
        arrived(half_row(p, 0, 2, True), p, 7)
        r = row(p, 0, 2)
        both(p, 8 + 12, ORDERS[p][2], r, r)
        to_twin(p, 0, 2)
    for p in parts:
        sides(p, 1)
        sides(p, 2)
    for p in parts:
        opposite(p, 0)
    for p in parts:
        sides(p, 3)
    for p in parts:
        opposite(p, 1)
        opposite(p, 2)
    for p in parts:
        opposite(p, 3)
    for p in parts:
        _, b, c = spot(p)
        for ci in range(4):
            for bi in range(4):
                arrived(at(p, 1 - core, c + ci, b + bi), p, 24 + 4 * ci + bi)
    return sends


def normal(values):
    centre = jnp.mean(values, -1, keepdims=True)
    centred = values - centre
    spread = jnp.mean(centred * centred, -1, keepdims=True)
    scale = lax.rsqrt(spread + LAYER_EPS)
    return centred * scale, scale


def by_eights(values):
    return jnp.sum(values.reshape(values.shape[0] // 8, 8, values.shape[1]), 0)


def pass_kernel(
    block_at, shard, patches, keep, cotangent,
    output, input_grad, left_out, right_out, vec_out,
    g, left, right, q, k, v, att, a_low, d_att, probs, tokens, mid, d_mid, d_a, act, wall, sums, vec,
    local_sem, send_sem, recv_sem, out_sem,
):
    sends = gather_weights(shard, g, local_sem, send_sem, recv_sem)

    def block(n):
        return g[pl.ds(block_at[n], 8)].reshape(SIDE, SIDE)

    def columns(m, j, count):
        rows = (256 if m == 4 else 64 if m < 4 else 256) // WIDTH[m]
        return jnp.concatenate(
            [
                jnp.concatenate([block(FIRST[m] + r * WIDTH[m] + j + i) for i in range(count)], 1)
                for r in range(rows)
            ],
            0,
        )

    def rows_of(m, i, count):
        return jnp.concatenate(
            [
                jnp.concatenate([block(FIRST[m] + (i + r) * WIDTH[m] + c) for c in range(WIDTH[m])], 1)
                for r in range(count)
            ],
            0,
        )

    def lanes(i, width):
        return pl.ds(pl.multiple_of(i * width, width), width)

    def strip(i):
        return pl.ds(pl.multiple_of(i * 32, 32), 32)

    def stack(first, count):
        return jnp.concatenate([right[first + i] for i in range(count)], 1)

    def line(i):
        return vec[i : i + 1, :]

    def add_sums(i, value, where=slice(None)):
        sums[i, :, where] += by_eights(value)

    for w in range(8):
        window = sum(
            g[int(VECTOR_AT[16 * w + i])].astype(F32) for i in range(16)
        )
        vec[:, w * 128 : (w + 1) * 128] = window
    sums[...] = jnp.zeros_like(sums)

    tokens[0:TOKENS, :] = patches[...].astype(F32)
    tokens[TOKENS:ROWS, :] = jnp.zeros((ROWS - TOKENS, D), F32)
    d_mid[0:TOKENS, :] = cotangent[...].astype(F32)
    d_mid[TOKENS:ROWS, :] = jnp.zeros((ROWS - TOKENS, D), F32)

    row_at = lax.broadcasted_iota(jnp.int32, (ROWS, ROWS), 0)
    col_at = lax.broadcasted_iota(jnp.int32, (ROWS, ROWS), 1)

    def image(at):
        return sum((at >= PATCHES * (i + 1)).astype(jnp.int32) for i in range(IMAGES))

    kept = jnp.broadcast_to(keep[...], (ROWS, ROWS))
    wall[...] = jnp.where(
        image(row_at) == image(col_at), jnp.where(kept > 0, 0.0, MASKED), OUTSIDE
    )

    def first_norm(i):
        n, _ = normal(tokens[strip(i), :])
        a_low[strip(i), :] = (n * line(0) + line(1)).astype(BF16)
        cot = d_mid[strip(i), :]
        for c in range(8):
            right[64 + c, strip(i), :] = cot[:, c * 128 : (c + 1) * 128].astype(BF16)
        add_sums(7, cot)

    loop(8, first_norm)

    def project(j):
        left[pl.ds(2 * j, 2)] = a_low[:, lanes(j, 256)].T.reshape(2, 128, ROWS)
        at = lanes(j, 256)
        q[:, at] = (dot(a_low[...], columns(0, 2 * j, 2)) + vec[2:3, at]).astype(BF16)
        k[:, at] = dot(a_low[...], columns(1, 2 * j, 2)).astype(BF16)
        v[:, at] = (dot(a_low[...], columns(2, 2 * j, 2)) + vec[3:4, at]).astype(BF16)

    loop(4, project)

    low_half = lax.broadcasted_iota(jnp.int32, (ROWS, 128), 1) < HEAD_DIM

    def split(pair):
        nothing = jnp.zeros_like(pair)
        return jnp.where(low_half, pair, nothing), jnp.where(low_half, nothing, pair)

    def attend(j):
        at = lanes(j, 128)
        kp = k[:, at]
        weights = []
        for h, qh in enumerate(split(q[:, at])):
            raw = dot_nt(qh, kp)
            masked = jnp.where(wall[...] == 0.0, raw * SCALE, wall[...])
            e = jnp.exp(masked - jnp.max(masked, -1, keepdims=True))
            p = e / jnp.sum(e, -1, keepdims=True)
            probs[2 * j + h] = p
            weights.append(p.astype(BF16))
        pair = dot(jnp.concatenate(weights, 1), jnp.concatenate(split(v[:, at]), 0)).astype(BF16)
        att[:, at] = pair
        left[8 + j] = pair.T

    loop(8, attend)

    def to_mid(j):
        at = lanes(j, 256)
        mid[:, at] = tokens[:, at] + (dot(att[...], columns(3, 2 * j, 2)) + vec[4:5, at])

    loop(4, to_mid)

    def second_norm(i):
        n, _ = normal(mid[strip(i), :])
        a_low[strip(i), :] = (n * line(5) + line(6)).astype(BF16)

    loop(8, second_norm)

    def hidden(j):
        pre = dot(a_low[...], columns(4, 2 * j, 2)) + vec[pl.ds(8 + j // 4, 1), lanes(j % 4, 256)]
        half = 0.5 * (1.0 + lax.erf(pre * math.sqrt(0.5)))
        slope = half + pre * (jnp.exp(-0.5 * pre * pre) * (1.0 / math.sqrt(2.0 * math.pi)))
        low = (pre * half).astype(BF16)
        act[:, lanes(j, 256)] = low
        left[pl.ds(24 + 2 * j, 2)] = low.T.reshape(2, 128, ROWS)
        d_pre = (dot_nt(stack(64, 8), rows_of(5, 2 * j, 2)) * slope).astype(BF16)
        right[32 + 2 * j] = d_pre[:, :128]
        right[33 + 2 * j] = d_pre[:, 128:]
        add_sums(8 + j // 4, d_pre.astype(F32), lanes(j % 4, 256))

    loop(16, hidden)

    def second_back(j):
        at = lanes(j, 256)
        left[pl.ds(16 + 2 * j, 2)] = a_low[:, at].T.reshape(2, 128, ROWS)
        d_a[:, at] = dot_nt(stack(32, 32), rows_of(4, 2 * j, 2))

    loop(4, second_back)

    def mid_back(i):
        rows = strip(i)
        n, scale = normal(mid[rows, :])
        d = d_a[rows, :]
        e = d * line(5)
        inner = e - jnp.mean(e, -1, keepdims=True) - n * jnp.mean(e * n, -1, keepdims=True)
        whole = d_mid[rows, :] + inner * scale
        d_mid[rows, :] = whole
        low = whole.astype(BF16)
        for c in range(8):
            right[24 + c, rows, :] = low[:, c * 128 : (c + 1) * 128]
        add_sums(5, d * n)
        add_sums(6, d)
        add_sums(4, low.astype(F32))

    loop(8, mid_back)

    def att_back(j):
        d_att[:, lanes(j, 256)] = dot_nt(stack(24, 8), rows_of(3, 2 * j, 2)).astype(BF16)

    loop(4, att_back)

    def heads_back(j):
        at = lanes(j, 128)
        vp = v[:, at]
        q_parts, k_parts, da_parts = split(q[:, at]), split(k[:, at]), split(d_att[:, at])
        d_raws, weights = [], []
        for h in range(2):
            p = probs[2 * j + h]
            d_p = dot_nt(da_parts[h], vp)
            d_m = p * (d_p - jnp.sum(p * d_p, -1, keepdims=True))
            d_raws.append(jnp.where(wall[...] == 0.0, d_m * SCALE, 0.0).astype(BF16))
            weights.append(p.astype(BF16))
        d_q = dot(jnp.concatenate(d_raws, 1), jnp.concatenate(k_parts, 0)).astype(BF16)
        d_k = dot_tn(jnp.concatenate(d_raws, 0), jnp.concatenate(q_parts, 0)).astype(BF16)
        d_v = dot_tn(jnp.concatenate(weights, 0), jnp.concatenate(da_parts, 0)).astype(BF16)
        right[j] = d_q
        right[8 + j] = d_k
        right[16 + j] = d_v
        add_sums(2, d_q.astype(F32), at)
        add_sums(3, d_v.astype(F32), at)

    loop(8, heads_back)

    copies = [
        pltpu.make_async_copy(left, left_out, out_sem.at[0]),
        pltpu.make_async_copy(right, right_out, out_sem.at[1]),
    ]
    for copy in copies:
        copy.start()

    def first_back(j):
        weights = jnp.concatenate([rows_of(m, 2 * j, 2) for m in range(3)], 1)
        d_a[:, lanes(j, 256)] = dot_nt(stack(0, 24), weights)

    loop(4, first_back)

    def token_back(i):
        rows = strip(i)
        n, scale = normal(tokens[rows, :])
        d = d_a[rows, :]
        e = d * line(0)
        inner = e - jnp.mean(e, -1, keepdims=True) - n * jnp.mean(e * n, -1, keepdims=True)
        d_mid[rows, :] = d_mid[rows, :] + inner * scale
        add_sums(0, d * n)
        add_sums(1, d)

    loop(8, token_back)
    input_grad[...] = d_mid[0:TOKENS, :].astype(BF16)

    def last(j):
        at = lanes(j, 256)
        d_a[:, at] = mid[:, at] + (dot(act[...], columns(5, 2 * j, 2)) + vec[7:8, at])

    loop(4, last)
    output[...] = d_a[0:TOKENS, :].astype(BF16)
    vec_out[0:NV, :] = jnp.sum(sums[...], 1)
    vec_out[NV:, :] = jnp.zeros((16 - NV, D), F32)
    for copy in copies:
        copy.wait()
    for copy in sends:
        copy.wait_send()


def forward_backward(block_at, shard, patches, keep, cotangent):
    anywhere, vmem = pl.BlockSpec(memory_space=pl.ANY), pl.BlockSpec(memory_space=pltpu.VMEM)
    flat = (ROWS, D)
    return pl.pallas_call(
        pass_kernel,
        out_shape=[
            jax.ShapeDtypeStruct((TOKENS, D), BF16),
            jax.ShapeDtypeStruct((TOKENS, D), BF16),
            jax.ShapeDtypeStruct((56, 128, ROWS), BF16),
            jax.ShapeDtypeStruct((72, ROWS, 128), BF16),
            jax.ShapeDtypeStruct((16, D), F32),
        ],
        in_specs=[pl.BlockSpec(memory_space=pltpu.SMEM), anywhere, vmem, vmem, vmem],
        out_specs=[vmem, vmem, anywhere, anywhere, vmem],
        scratch_shapes=[
            pltpu.VMEM((ALL_ROWS, 16, 128), BF16),
            pltpu.VMEM((56, 128, ROWS), BF16),
            pltpu.VMEM((72, ROWS, 128), BF16),
            pltpu.VMEM(flat, BF16),
            pltpu.VMEM(flat, BF16),
            pltpu.VMEM(flat, BF16),
            pltpu.VMEM(flat, BF16),
            pltpu.VMEM(flat, BF16),
            pltpu.VMEM(flat, BF16),
            pltpu.VMEM((HEADS, ROWS, ROWS), F32),
            pltpu.VMEM(flat, F32),
            pltpu.VMEM(flat, F32),
            pltpu.VMEM(flat, F32),
            pltpu.VMEM(flat, F32),
            pltpu.VMEM((ROWS, FF), BF16),
            pltpu.VMEM((ROWS, ROWS), F32),
            pltpu.VMEM((NV, 8, D), F32),
            pltpu.VMEM((16, D), F32),
            pltpu.SemaphoreType.DMA((3,)),
            pltpu.SemaphoreType.DMA((3, 40)),
            pltpu.SemaphoreType.DMA((3, 40)),
            pltpu.SemaphoreType.DMA((2,)),
        ],
        compiler_params=pltpu.CompilerParams(
            collective_id=0, has_side_effects=True, vmem_limit_bytes=62 * MIB
        ),
        cost_estimate=pl.CostEstimate(
            flops=13_000_000_000, bytes_accessed=60_000_000, transcendentals=3_000_000
        ),
        name="forward_backward",
    )(block_at, shard, patches, keep, cotangent)


AHEAD = 3


def scatter_kernel(
    left_at, right_at, left, right, vec_in,
    total, window, norm_tile,
    tw_out, tw_in, c_out, c_in, c_half, b_out, b_in, b_half, a_out, a_in, a_half, kept, vec, vec_in_buf, tiles, mask,
    tw_send, tw_recv, c_send, c_recv, b_send, b_recv, a_send, a_recv, v_send, v_recv, n_send, n_recv,
):
    pos, core = place()
    twin = device(pos, 1 - core)
    axes = [[device(moved(pos, a, s), core) for s in (1, 2, 3)] for a in range(3)]
    greet([twin] + [to for three in axes for to in three])

    def pick(options, i):
        value = options[-1]
        for n in range(len(options) - 2, -1, -1):
            value = jnp.where(i == n, options[n], value)
        return value

    def axis_of(p, which):
        return lax.rem(p + which, 3)

    def neighbour(p, which, by):
        axis = axis_of(p, which)
        if isinstance(by, int):
            return tuple(pick([axes[a][by - 1][n] for a in range(3)], axis) for n in range(2))
        ahead, back = neighbour(p, which, 1), neighbour(p, which, 3)
        return tuple(jnp.where(by == 1, ahead[n], back[n]) for n in range(2))

    def along(p, which, by):
        return lax.rem(pick(pos, axis_of(p, which)) + by, 4)

    def pair(p, ci, bi, ai, of_core):
        spots = [along(p, 0, ai), along(p, 1, bi), along(p, 2, ci)]
        x, y, z = (pick([spots[(a - s) % 3] for s in range(3)], p) for a in range(3))
        wide, narrow = device((x, y, z), of_core)
        slot = (wide * 8 + narrow) * 6 + 2 * p
        made = []
        for i in range(2):
            made.append(dot(left[left_at[slot + i]], right[right_at[slot + i]]))
        return jnp.concatenate(made, 0)

    def order(i):
        return pick([2, 1, 3, 0], i)

    def step(s):
        quarter, p = s // 3, lax.rem(s, 3)
        ci = jnp.where(quarter < 4, 2, jnp.where(quarter < 12, jnp.where(lax.rem(quarter, 2) == 0, 1, 3), 0))
        i = jnp.where(quarter < 4, quarter, jnp.where(quarter < 12, (quarter - 4) // 2, quarter - 12))
        return p, ci, order(i)

    def remote(src, dst, send_sem, recv_sem, to):
        return pltpu.make_async_remote_copy(
            src_ref=src, dst_ref=dst, send_sem=send_sem, recv_sem=recv_sem, device_id=to, device_id_type=MESH
        )

    def twin_copy(p, ci, bi):
        n = p * 16 + ci * 4 + bi
        return remote(tw_out.at[n], tw_in.at[n], tw_send.at[n], tw_recv.at[n], twin)

    def for_twin(s):
        p, ci, bi = step(s)
        for ai in range(4):
            tw_out[p * 16 + ci * 4 + bi, ai] = pair(p, ci, bi, ai, 1 - core).astype(BF16)
        twin_copy(p, ci, bi).start()

    def chip_sum(p, ci, bi, ai):
        return pair(p, ci, bi, ai, core) + tw_in[p * 16 + ci * 4 + bi, ai].astype(F32)

    def c_half_copy(p, bi, second):
        n = p * 4 + bi
        part = pl.ds(2 if second else 0, 2)
        return remote(
            c_out.at[n, part], c_half.at[n, part], c_send.at[2 * n + second], c_recv.at[2 * n + second],
            neighbour(p, 2, 3 if second else 1),
        )

    def c_whole_copy(p, bi, leftward):
        n = p * 4 + bi
        return remote(
            c_out.at[12 + 12 * leftward + n], c_in.at[12 * leftward + n], c_send.at[24 + 12 * leftward + n],
            c_recv.at[24 + 12 * leftward + n], neighbour(p, 2, 1 + 2 * leftward),
        )

    def b_half_copy(p, second):
        part = pl.ds(2 if second else 0, 2)
        return remote(
            b_out.at[p, 0, part], b_half.at[p, part], b_send.at[4 * p + second], b_recv.at[4 * p + second],
            neighbour(p, 1, 3 if second else 1),
        )

    def b_whole_copy(p, leftward):
        return remote(
            b_out.at[p, 1 + leftward], b_in.at[p, leftward], b_send.at[4 * p + 2 + leftward],
            b_recv.at[4 * p + 2 + leftward], neighbour(p, 1, 3 if leftward else 1),
        )

    def a_half_copy(p, second):
        part = pl.ds(128 if second else 0, 128)
        return remote(
            a_out.at[p, 0, part], a_half.at[p, part], a_send.at[4 * p + second], a_recv.at[4 * p + second],
            neighbour(p, 0, 3 if second else 1),
        )

    def a_whole_copy(p, leftward):
        return remote(
            a_out.at[p, 1 + leftward], a_in.at[p, leftward], a_send.at[4 * p + 2 + leftward],
            a_recv.at[4 * p + 2 + leftward], neighbour(p, 0, 3 if leftward else 1),
        )

    def vec_twin():
        return remote(vec.at[0], vec_in_buf.at[0], v_send.at[0], v_recv.at[0], twin)

    def vec_copy(axis, by):
        n = 1 + 3 * axis + by - 1
        return remote(vec.at[1 + axis], vec_in_buf.at[n], v_send.at[n], v_recv.at[n], axes[axis][by - 1])

    def vec_axis(axis):
        if axis == 0:
            vec_twin().wait_recv()
            vec[1] = vec[0] + vec_in_buf[0]
        else:
            vec[1 + axis] = vec_done(axis - 1)
        for by in (1, 2, 3):
            vec_copy(axis, by).start()

    def vec_done(axis):
        whole = vec[1 + axis]
        for by in (1, 2, 3):
            vec_copy(axis, by).wait_recv()
            whole = whole + vec_in_buf[3 * axis + by]
        return whole

    vec[0] = vec_in[...]
    vec_twin().start()

    loop(AHEAD, for_twin)

    def opposite_step(s):
        for_twin(s + AHEAD)
        p, ci, bi = step(s)
        n = p * 4 + bi
        twin_copy(p, ci, bi).wait_recv()
        for ai in range(4):
            c_out[n, ai] = chip_sum(p, ci, bi, ai).astype(BF16)
        c_half_copy(p, bi, 0).start()
        c_half_copy(p, bi, 1).start()

    loop(12, opposite_step)
    vec_axis(0)

    def side_step(s):
        p, ci, bi = step(s)
        leftward = jnp.where(ci == 3, 1, 0)
        n = p * 4 + bi
        out = 12 + 12 * leftward + n
        twin_copy(p, ci, bi).wait_recv()
        remote(
            c_out.at[n, pl.ds(0, 2)], c_half.at[n, pl.ds(2 * leftward, 2)], c_send.at[2 * n + leftward],
            c_recv.at[2 * n + leftward], twin,
        ).wait_recv()
        for i in range(2):
            ai = 2 * leftward + i
            c_out[out, ai] = (chip_sum(p, ci, bi, ai) + c_half[n, ai].astype(F32)).astype(BF16)
        for i in range(2):
            ai = 2 - 2 * leftward + i
            c_out[out, ai] = chip_sum(p, ci, bi, ai).astype(BF16)
        c_whole_copy(p, bi, leftward).start()

    def side_ahead(i):
        for_twin(12 + i + AHEAD)
        side_step(12 + i)

    loop(24, side_ahead)
    vec_axis(1)

    def own_sum(p, bi, ai):
        n = p * 4 + bi
        return chip_sum(p, 0, bi, ai) + c_in[n, ai].astype(F32) + c_in[12 + n, ai].astype(F32)

    def own_arrived(p, bi):
        twin_copy(p, 0, bi).wait_recv()
        c_whole_copy(p, bi, 0).wait_recv()
        c_whole_copy(p, bi, 1).wait_recv()

    def b_opposite(p):
        for_twin(36 + p + AHEAD)
        own_arrived(p, 2)
        for ai in range(4):
            b_out[p, 0, ai] = own_sum(p, 2, ai).astype(BF16)
        b_half_copy(p, 0).start()
        b_half_copy(p, 1).start()

    loop(3, b_opposite)

    def b_side(leftward):
        def body(p):
            for_twin(39 + 3 * leftward + p + AHEAD)
            bi = 3 if leftward else 1
            own_arrived(p, bi)
            b_half_copy(p, leftward).wait_recv()
            for ai in range(4):
                value = own_sum(p, bi, ai)
                if ai // 2 == leftward:
                    value = value + b_half[p, ai].astype(F32)
                b_out[p, 1 + leftward, ai] = value.astype(BF16)
            b_whole_copy(p, leftward).start()

        return body

    loop(3, b_side(0))
    loop(3, b_side(1))

    def b_own(p):
        own_arrived(p, 0)
        for ai in range(4):
            kept[p, ai] = own_sum(p, 0, ai)

    loop(3, b_own)

    def row_sum(p, ai):
        return kept[p, ai] + b_in[p, 0, ai].astype(F32) + b_in[p, 1, ai].astype(F32)

    def a_opposite(p):
        b_whole_copy(p, 0).wait_recv()
        b_whole_copy(p, 1).wait_recv()
        a_out[p, 0] = row_sum(p, 2).astype(BF16)
        a_half_copy(p, 0).start()
        a_half_copy(p, 1).start()

    loop(3, a_opposite)
    vec_axis(2)

    def a_sides(p):
        for leftward in (0, 1):
            a_half_copy(p, leftward).wait_recv()
            value = row_sum(p, 3 if leftward else 1)
            at = slice(128, 256) if leftward else slice(0, 128)
            other = slice(0, 128) if leftward else slice(128, 256)
            a_out[p, 1 + leftward, at] = (value[at] + a_half[p, at].astype(F32)).astype(BF16)
            a_out[p, 1 + leftward, other] = value[other].astype(BF16)
            a_whole_copy(p, leftward).start()

    loop(3, a_sides)

    squares = jnp.zeros((8, 128), F32)
    for p in range(3):
        a_whole_copy(p, 0).wait_recv()
        a_whole_copy(p, 1).wait_recv()
        value = row_sum(p, 0) + a_in[p, 0].astype(F32) + a_in[p, 1].astype(F32)
        total[2 * p] = value[:128]
        total[2 * p + 1] = value[128:]
        squares = squares + by_eights(value * value)

    wide, narrow = lax.axis_index("wide"), lax.axis_index("narrow")
    vec[4] = vec_done(2)
    mine = vec[4, :, pl.ds(pl.multiple_of((wide // 2) * 128, 128), 128)]
    window[...] = mine
    lane = lax.broadcasted_iota(jnp.int32, (16, 128), 1) // 8
    own = jnp.where(lane == lax.rem(wide, 2) * 8 + narrow, mine, 0.0)
    squares = squares + by_eights(own * own)

    tiles[0] = squares

    def norm_copy(stage, by):
        n = 1 + 3 * (stage - 1) + by - 1 if stage else 0
        to = axes[stage - 1][by - 1] if stage else twin
        return remote(tiles.at[stage], tiles.at[5 + n], n_send.at[n], n_recv.at[n], to)

    for stage in range(4):
        partners = (1, 2, 3) if stage else (1,)
        for by in partners:
            norm_copy(stage, by).start()
        whole = tiles[stage]
        for by in partners:
            norm_copy(stage, by).wait_recv()
            whole = whole + tiles[5 + (1 + 3 * (stage - 1) + by - 1 if stage else 0)]
        tiles[stage + 1] = whole
    norm_tile[...] = tiles[4]

    def sent(s):
        p, ci, bi = step(s)
        twin_copy(p, ci, bi).wait_send()

    loop(48, sent)

    def sent_along(p):
        for bi in range(4):
            for side in (0, 1):
                c_half_copy(p, bi, side).wait_send()
                c_whole_copy(p, bi, side).wait_send()
        for side in (0, 1):
            b_half_copy(p, side).wait_send()
            b_whole_copy(p, side).wait_send()
            a_half_copy(p, side).wait_send()
            a_whole_copy(p, side).wait_send()

    loop(3, sent_along)
    vec_twin().wait_send()
    norm_copy(0, 1).wait_send()
    for axis in range(3):
        for by in (1, 2, 3):
            vec_copy(axis, by).wait_send()
            norm_copy(axis + 1, by).wait_send()


def sum_gradients(left_at, right_at, left, right, vec):
    smem, vmem = pl.BlockSpec(memory_space=pltpu.SMEM), pl.BlockSpec(memory_space=pltpu.VMEM)
    row = (4, 256, 128)
    dma = pltpu.SemaphoreType.DMA
    return pl.pallas_call(
        scatter_kernel,
        out_shape=[
            jax.ShapeDtypeStruct((6, SIDE, SIDE), F32),
            jax.ShapeDtypeStruct((16, 128), F32),
            jax.ShapeDtypeStruct((8, 128), F32),
        ],
        in_specs=[smem, smem, vmem, vmem, vmem],
        out_specs=[vmem, vmem, vmem],
        scratch_shapes=[
            pltpu.VMEM((48, *row), BF16),
            pltpu.VMEM((48, *row), BF16),
            pltpu.VMEM((36, *row), BF16),
            pltpu.VMEM((24, *row), BF16),
            pltpu.VMEM((12, *row), BF16),
            pltpu.VMEM((3, 3, *row), BF16),
            pltpu.VMEM((3, 2, *row), BF16),
            pltpu.VMEM((3, *row), BF16),
            pltpu.VMEM((3, 3, 256, 128), BF16),
            pltpu.VMEM((3, 2, 256, 128), BF16),
            pltpu.VMEM((3, 256, 128), BF16),
            pltpu.VMEM((3, *row), F32),
            pltpu.VMEM((5, 16, D), F32),
            pltpu.VMEM((10, 16, D), F32),
            pltpu.VMEM((15, 8, 128), F32),
            pltpu.VMEM((8, 128), F32),
            dma((48,)), dma((48,)), dma((48,)), dma((48,)), dma((12,)), dma((12,)), dma((12,)), dma((12,)),
            dma((10,)), dma((10,)), dma((10,)), dma((10,)),
        ],
        compiler_params=pltpu.CompilerParams(
            collective_id=1, has_side_effects=True, vmem_limit_bytes=62 * MIB
        ),
        cost_estimate=pl.CostEstimate(
            flops=6_500_000_000, bytes_accessed=10_000_000, transcendentals=0
        ),
        name="sum_gradients",
    )(left_at, right_at, left, right, vec)


def exact(left, right, over):
    return lax.dot_general(
        left, right, (over, ((), ())), precision=lax.Precision.HIGHEST, preferred_element_type=F32
    )


def step_kernel(
    raw, window, norm_tile, place_ref, master, left_stats, right_stats, left_root, right_root, vectors, vec_accum,
    block_grads, new_left, new_right, new_master, new_copy, vec_grads, vec_accum_new, vec_new, grad_norm,
):
    norm = jnp.sqrt(jnp.sum(norm_tile[...], keepdims=True))
    clip = 1.0 / jnp.maximum(norm, 1.0)
    for i in range(raw.shape[0]):
        grads = raw[i] * clip
        block_grads[i] = grads
        new_left[i] = 0.5 * left_stats[i] + 0.5 * exact(grads, grads, ((1,), (1,)))
        new_right[i] = 0.5 * right_stats[i] + 0.5 * exact(grads, grads, ((0,), (0,)))
        way = exact(exact(left_root[i], grads, ((1,), (0,))), right_root[i], ((1,), (0,)))
        master_now = master[i] - 0.5 * way
        new_master[i] = master_now
        new_copy[i] = master_now.astype(BF16)

    @pl.when(pl.program_id(0) == 0)
    def _():
        grad_norm[...] = norm
        mine = pltpu.roll(window[...], place_ref[0], 1)[:NV, :8]
        grads = clip * mine
        vec_grads[...] = grads
        accum = 0.5 * vec_accum[...] + 0.5 * grads * grads
        vec_accum_new[...] = accum
        vec_new[...] = vectors[...] - 0.5 * grads / (jnp.sqrt(accum) + 1e-08)


def update(raw, window, norm_tile, shift, master, left_stats, right_stats, left_root, right_root, vectors, vec_accum):
    per = 2
    blocks = pl.BlockSpec((per, SIDE, SIDE), lambda i: (i, 0, 0))

    def whole(*shape):
        return pl.BlockSpec(shape, lambda i: (0,) * len(shape))

    f32_blocks = jax.ShapeDtypeStruct((6, SIDE, SIDE), F32)
    f32_vecs = jax.ShapeDtypeStruct((NV, 8), F32)
    return pl.pallas_call(
        step_kernel,
        grid=(6 // per,),
        out_shape=[f32_blocks] * 4
        + [jax.ShapeDtypeStruct((6, SIDE, SIDE), BF16)]
        + [f32_vecs] * 3
        + [jax.ShapeDtypeStruct((1, 1), F32)],
        in_specs=[blocks, whole(16, 128), whole(8, 128), pl.BlockSpec(memory_space=pltpu.SMEM)]
        + [blocks] * 5
        + [whole(NV, 8)] * 2,
        out_specs=[blocks] * 5 + [whole(NV, 8)] * 3 + [whole(1, 1)],
        compiler_params=pltpu.CompilerParams(vmem_limit_bytes=32 * MIB),
        name="update",
    )(raw, window, norm_tile, shift, master, left_stats, right_stats, left_root, right_root, vectors, vec_accum)


def body(
    patches, keep, cotangent, owner_table, master, left_stats, right_stats, left_root, right_root, vectors, vec_accum,
):
    wide, narrow = lax.axis_index("wide"), lax.axis_index("narrow")
    lane = ((wide % 2) * 8 + narrow) * 8
    vec_tile = lax.dynamic_update_slice(jnp.zeros((16, 128), BF16), vectors.astype(BF16), (0, lane))
    shard = jnp.concatenate([master.astype(BF16).reshape(48, 16, SIDE), vec_tile[None]], 0)

    numbers = jnp.arange(NBLK, dtype=jnp.int32)
    held = owner_table[None, :] == numbers[:, None]
    block_at = jnp.sum(jnp.where(held, jnp.asarray(BLOCK_AT)[None, :], 0), 1)
    matrix = sum((owner_table >= first).astype(jnp.int32) for first in FIRST[1:])

    def by_matrix(values):
        return sum(jnp.where(matrix == m, value, 0) for m, value in enumerate(values))

    inner = owner_table - by_matrix(FIRST)
    block_row = jnp.where(matrix == 4, inner // 32, inner // 8)
    block_column = jnp.where(matrix == 4, inner % 32, inner % 8)
    left_at = by_matrix(LEFT_AT) + block_row
    right_at = by_matrix(RIGHT_AT) + block_column

    kept = jnp.pad(keep.reshape(1, TOKENS), ((0, 0), (0, ROWS - TOKENS)), constant_values=1)
    output, input_grad, left, right, vec = forward_backward(block_at, shard, patches, kept, cotangent)
    raw, window, norm_tile = sum_gradients(left_at, right_at, left, right, vec)
    shift = jnp.reshape((128 - lane) % 128, (1,)).astype(jnp.int32)
    *rest, grad_norm = update(
        raw, window, norm_tile, shift, master, left_stats, right_stats, left_root, right_root, vectors, vec_accum
    )
    return (output, input_grad, *rest, grad_norm.reshape(()))


def solution(mesh):
    rows, blocks, vecs = P(BOTH, None), P(BOTH, None, None), P(None, BOTH)
    return jax.shard_map(
        body,
        mesh=mesh,
        in_specs=(rows, rows, rows, P(), blocks, blocks, blocks, blocks, blocks, vecs, vecs),
        out_specs=(rows, rows, blocks, blocks, blocks, blocks, blocks, vecs, vecs, vecs, P()),
        check_vma=False,
    )
```

```python
import functools
import math

import jax
import jax.numpy as jnp
import numpy as np
from jax import lax
from jax.experimental import pallas as pl
from jax.experimental.pallas import tpu as pltpu
from jax.sharding import PartitionSpec as P

MESH = pl.DeviceIdType.MESH
BOTH = ("wide", "narrow")
F32, BF16 = jnp.float32, jnp.bfloat16
MIB = 2**20

D = 1024
FF = 4096
HEADS = 16
HEAD_DIM = 64
PATCHES = 49
IMAGES = 5
TOKENS = IMAGES * PATCHES
ROWS = 256
SIDE = 128
NBLK = 768
NV = 12
LAYER_EPS = 1e-05
MASKED = -1000000000.0
OUTSIDE = -3.0e38
SCALE = HEAD_DIM**-0.5

ORDERS = ((0, 1, 2), (1, 2, 0), (2, 0, 1))
SHARE = (16, 16, 17)
PART_FROM = (0, 128 * 16, 128 * 32)
ALL_ROWS = 128 * 49
NEXT = (0, 3, 1, 2)

FIRST = (0, 64, 128, 192, 256, 512)
WIDTH = (8, 8, 8, 8, 32, 8)
LEFT_AT = (0, 0, 0, 8, 16, 24)
RIGHT_AT = (0, 8, 16, 24, 32, 64)


def slot_places():
    block_at, vector_at = np.zeros(NBLK, np.int32), np.zeros(128, np.int32)
    for dev in range(128):
        wide, narrow = dev // 8, dev % 8
        core = wide % 2
        pos = (wide // 2 % 2 * 2 + narrow // 4, wide // 4, narrow % 4)
        for p, (a, b, c) in enumerate(ORDERS):
            at = PART_FROM[p] + (((core * 4 + pos[c]) * 4 + pos[b]) * 4 + pos[a]) * SHARE[p]
            block_at[dev * 6 + 2 * p] = at
            block_at[dev * 6 + 2 * p + 1] = at + 8
            if p == 2:
                vector_at[dev] = at + 16
    return block_at, vector_at


BLOCK_AT, VECTOR_AT = slot_places()


def place():
    wide, narrow = lax.axis_index("wide"), lax.axis_index("narrow")
    x = (wide // 2) % 2 * 2 + narrow // 4
    return (x, wide // 4, narrow % 4), wide % 2


def device(pos, core):
    x, y, z = pos
    return ((y * 2 + x // 2) * 2 + core, x % 2 * 4 + z)


def moved(pos, axis, by):
    return tuple((c + by) % 4 if a == axis else c for a, c in enumerate(pos))


def partners():
    pos, core = place()
    plane = [device(moved(moved(pos, 0, i), 1, j), core) for i in range(4) for j in range(4) if i or j]
    column = [
        device(moved(pos, 2, i), core if j == 0 else 1 - core) for j in range(2) for i in range(4) if i or j
    ]
    return plane, column


def announce(semaphore):
    plane, column = partners()
    for partner in plane + column:
        pl.semaphore_signal(semaphore, inc=1, device_id=partner, device_id_type=MESH)


def all_announced(semaphore):
    plane, column = partners()
    pl.semaphore_wait(semaphore, len(plane + column))


def loop(count, body):
    lax.fori_loop(0, count, lambda i, _: (body(i), None)[1], None)


def dot(left, right):
    return jnp.dot(left, right, preferred_element_type=F32)


def dot_nt(left, right):
    return lax.dot_general(left, right, (((1,), (1,)), ((), ())), preferred_element_type=F32)


def dot_tn(left, right):
    return lax.dot_general(left, right, (((0,), (0,)), ((), ())), preferred_element_type=F32)


def gather_weights(master, vectors, loads, g, send_sem, recv_sem, meanwhile):
    pos, core = place()
    twin = device(pos, 1 - core)
    near = {(a, s): device(moved(pos, a, s), core) for a in range(3) for s in (1, -1)}

    for load in loads:
        load.wait()

    for p in range(3):
        a, b, c = (pos[axis] for axis in ORDERS[p])
        start = PART_FROM[p] + (((core * 4 + c) * 4 + b) * 4 + a) * SHARE[p]
        g[pl.ds(start, 16)] = master[2 * p : 2 * p + 2].astype(BF16).reshape(16, 16, SIDE)
        if p == 2:
            wide, narrow = lax.axis_index("wide"), lax.axis_index("narrow")
            first_lane = (lax.rem(wide, 2) * 8 + narrow) * 8
            spread = lax.broadcasted_iota(jnp.int32, (8, 128), 1) == (
                lax.broadcasted_iota(jnp.int32, (8, 128), 0) + first_lane
            )
            tile = dot_tn(vectors[...].astype(BF16), spread.astype(BF16)).astype(BF16)
            g[start + 16] = jnp.concatenate([tile, jnp.zeros((16 - NV, 128), BF16)], 0)

    sends = []

    def copy_of(src, dst, p, slot, to):
        return pltpu.make_async_remote_copy(
            src_ref=src, dst_ref=dst, send_sem=send_sem.at[p, slot],
            recv_sem=recv_sem.at[p, slot], device_id=to, device_id_type=MESH,
        )

    def send(src, dst, p, slot, to):
        copy = copy_of(src, dst, p, slot, to)
        copy.start()
        sends.append(copy)

    def arrived(dst, p, slot):
        copy_of(dst, dst, p, slot, twin).wait_recv()

    def at(p, of_core, c, b, a=0, count=4, skip=0, rows=None):
        start = PART_FROM[p] + (((of_core * 4 + c % 4) * 4 + b % 4) * 4 + a % 4) * SHARE[p] + skip
        return g.at[pl.ds(start, count * SHARE[p] if rows is None else rows)]

    def spot(p):
        a, b, c = ORDERS[p]
        return pos[a], pos[b], pos[c]

    def row(p, ci, bi):
        _, b, c = spot(p)
        return at(p, core, c + ci, b + bi)

    def half_row(p, ci, bi, second):
        _, b, c = spot(p)
        return at(p, core, c + ci, b + bi, 2 if second else 0, 2)

    def chunk(p, ai):
        a, b, c = spot(p)
        return at(p, core, c, b, a + ai, 1)

    def half_chunk(p, ai, second):
        a, b, c = spot(p)
        return at(p, core, c, b, a + ai, 1, 8 if second else 0, SHARE[p] - 8 if second else 8)

    def to_twin(p, ci, bi):
        r = row(p, ci, bi)
        send(r, r, p, 24 + 4 * (ci % 4) + bi % 4, twin)

    def onward(p, base, axis, half):
        first, second = half(False), half(True)
        return (
            lambda: send(first, first, p, base + 2, near[axis, 1]),
            lambda: send(second, second, p, base + 3, near[axis, -1]),
        )

    def both(p, base, axis, src, dst):
        send(src, dst, p, base, near[axis, 1])
        send(src, dst, p, base + 1, near[axis, -1])

    parts = range(3)
    for p in parts:
        both(p, 0, ORDERS[p][0], chunk(p, 0), chunk(p, 0))
    for p in parts:
        axis = ORDERS[p][0]
        arrived(chunk(p, -1), p, 0)
        onward(p, 0, axis, lambda second: half_chunk(p, -1, second))[0]()
        arrived(chunk(p, 1), p, 1)
        onward(p, 0, axis, lambda second: half_chunk(p, 1, second))[1]()
    for p in parts:
        arrived(half_chunk(p, 2, False), p, 2)
        arrived(half_chunk(p, 2, True), p, 3)
        r = row(p, 0, 0)
        both(p, 4, ORDERS[p][1], r, r)
        both(p, 8, ORDERS[p][2], r, r)
        to_twin(p, 0, 0)
    for p in parts:
        for bi, i in ((-1, 1), (1, 2)):
            r = row(p, 0, bi)
            arrived(r, p, 4 + (i - 1))
            onward(p, 4, ORDERS[p][1], lambda second: half_row(p, 0, bi, second))[i - 1]()
            both(p, 8 + 4 * i, ORDERS[p][2], r, r)
            to_twin(p, 0, bi)

    meanwhile()

    def sides(p, i):
        bi = NEXT[i]
        for ci, j in ((-1, 0), (1, 1)):
            arrived(row(p, ci, bi), p, 8 + 4 * i + j)
            onward(p, 8 + 4 * i, ORDERS[p][2], lambda second: half_row(p, ci, bi, second))[j]()
            to_twin(p, ci, bi)

    def opposite(p, i):
        bi = NEXT[i]
        arrived(half_row(p, 2, bi, False), p, 8 + 4 * i + 2)
        arrived(half_row(p, 2, bi, True), p, 8 + 4 * i + 3)
        to_twin(p, 2, bi)

    for p in parts:
        sides(p, 0)
    for p in parts:
        arrived(half_row(p, 0, 2, False), p, 6)
        arrived(half_row(p, 0, 2, True), p, 7)
        r = row(p, 0, 2)
        both(p, 8 + 12, ORDERS[p][2], r, r)
        to_twin(p, 0, 2)
    for p in parts:
        sides(p, 1)
        sides(p, 2)
    for p in parts:
        opposite(p, 0)
    for p in parts:
        sides(p, 3)
    for p in parts:
        opposite(p, 1)
        opposite(p, 2)
    for p in parts:
        opposite(p, 3)
    for p in parts:
        _, b, c = spot(p)
        for ci in range(4):
            for bi in range(4):
                arrived(at(p, 1 - core, c + ci, b + bi), p, 24 + 4 * ci + bi)
    return sends


def normal(values):
    centre = jnp.mean(values, -1, keepdims=True)
    centred = values - centre
    spread = jnp.mean(centred * centred, -1, keepdims=True)
    scale = lax.rsqrt(spread + LAYER_EPS)
    return centred * scale, scale


def by_eights(values):
    return jnp.sum(values.reshape(values.shape[0] // 8, 8, values.shape[1]), 0)


def pass_kernel(
    block_at, master_in, vectors_in, patches, keep_in, cotangent, output, input_grad, vec_out,
    g, left, right, flats, q, k, v, att, a_low, probs, act, w_out, wall, sums, vec,
    master, vectors, keep, send_sem, recv_sem, held_sem, ready,
):
    tokens, d_mid, mid, d_a = (flats.at[i] for i in range(4))
    loads = [
        pltpu.make_async_copy(src, to, held_sem.at[i])
        for i, (src, to) in enumerate(
            ((master_in, master), (vectors_in, vectors), (patches, output), (cotangent, input_grad), (keep_in, keep))
        )
    ]
    for load in loads:
        load.start()

    def block(n):
        return g[pl.ds(block_at[n], 8)].reshape(SIDE, SIDE)

    def columns(m, j, count):
        rows = (256 if m == 4 else 64 if m < 4 else 256) // WIDTH[m]
        return jnp.concatenate(
            [
                jnp.concatenate([block(FIRST[m] + r * WIDTH[m] + j + i) for i in range(count)], 1)
                for r in range(rows)
            ],
            0,
        )

    def rows_of(m, i, count):
        return jnp.concatenate(
            [
                jnp.concatenate([block(FIRST[m] + (i + r) * WIDTH[m] + c) for c in range(WIDTH[m])], 1)
                for r in range(count)
            ],
            0,
        )

    def lanes(i, width):
        return pl.ds(pl.multiple_of(i * width, width), width)

    def strip(i):
        return pl.ds(pl.multiple_of(i * 32, 32), 32)

    def stack(first, count):
        return jnp.concatenate([right[first + i] for i in range(count)], 1)

    def line(i):
        return vec[i : i + 1, :]

    def add_sums(i, value, where=slice(None)):
        sums[i, :, where] += by_eights(value)

    def first_normal(i):
        n, _ = normal(tokens[strip(i), :])
        d_a[strip(i), :] = n
        cot = d_mid[strip(i), :]
        for c in range(8):
            right[64 + c, strip(i), :] = cot[:, c * 128 : (c + 1) * 128].astype(BF16)
        add_sums(7, cot)

    def meanwhile():
        sums[...] = jnp.zeros_like(sums)
        for load in loads[2:]:
            load.wait()
        for came, to in ((output, tokens), (input_grad, d_mid)):
            to[0:TOKENS, :] = came[...].astype(F32)
            to[TOKENS:ROWS, :] = jnp.zeros((ROWS - TOKENS, D), F32)
        row_at = lax.broadcasted_iota(jnp.int32, (ROWS, ROWS), 0)
        col_at = lax.broadcasted_iota(jnp.int32, (ROWS, ROWS), 1)

        def image(at):
            return sum((at >= PATCHES * (i + 1)).astype(jnp.int32) for i in range(IMAGES))

        spread = (
            lax.broadcasted_iota(jnp.int32, (PATCHES, ROWS), 1)
            - PATCHES * image(lax.broadcasted_iota(jnp.int32, (PATCHES, ROWS), 1))
            == lax.broadcasted_iota(jnp.int32, (PATCHES, ROWS), 0)
        )
        kept = dot(keep[...].astype(F32).astype(BF16), spread.astype(F32).astype(BF16))
        own = lax.broadcasted_iota(jnp.int32, (IMAGES, ROWS), 0) == image(
            lax.broadcasted_iota(jnp.int32, (IMAGES, ROWS), 1)
        )
        dropped = jnp.sum(jnp.where(own & (kept < 0.5), 1.0, 0.0), 0, keepdims=True)
        wall[...] = jnp.where(
            image(row_at) == image(col_at), jnp.broadcast_to(dropped, (ROWS, ROWS)) * MASKED, OUTSIDE
        )
        loop(8, first_normal)

    barrier = pltpu.get_barrier_semaphore()
    announce(barrier)
    all_announced(barrier)
    sends = gather_weights(master, vectors, loads[:2], g, send_sem, recv_sem, meanwhile)

    for w in range(8):
        window = sum(g[int(VECTOR_AT[16 * w + i])].astype(F32) for i in range(16))
        vec[:, w * 128 : (w + 1) * 128] = window

    def first_norm(i):
        a_low[strip(i), :] = (d_a[strip(i), :] * line(0) + line(1)).astype(BF16)

    loop(8, first_norm)

    def project(j):
        left[pl.ds(2 * j, 2)] = a_low[:, lanes(j, 256)].T.reshape(2, 128, ROWS)
        at = lanes(j, 256)
        q[:, at] = (dot(a_low[...], columns(0, 2 * j, 2)) + vec[2:3, at]).astype(BF16)
        k[:, at] = dot(a_low[...], columns(1, 2 * j, 2)).astype(BF16)
        v[:, at] = (dot(a_low[...], columns(2, 2 * j, 2)) + vec[3:4, at]).astype(BF16)

    loop(4, project)

    low_half = lax.broadcasted_iota(jnp.int32, (ROWS, 128), 1) < HEAD_DIM

    def split(pair):
        nothing = jnp.zeros_like(pair)
        return jnp.where(low_half, pair, nothing), jnp.where(low_half, nothing, pair)

    def attend(j):
        at = lanes(j, 128)
        kp = k[:, at]
        weights = []
        for h, qh in enumerate(split(q[:, at])):
            raw = dot_nt(qh, kp)
            masked = jnp.where(wall[...] == 0.0, raw * SCALE, wall[...])
            e = jnp.exp(masked - jnp.max(masked, -1, keepdims=True))
            p = e / jnp.sum(e, -1, keepdims=True)
            low = p.astype(BF16)
            probs[2 * j + h] = low
            weights.append(low)
        pair = dot(jnp.concatenate(weights, 1), jnp.concatenate(split(v[:, at]), 0)).astype(BF16)
        att[:, at] = pair
        left[8 + j] = pair.T

    loop(8, attend)

    def to_mid(j):
        at = lanes(j, 256)
        mid[:, at] = tokens[:, at] + (dot(att[...], columns(3, 2 * j, 2)) + vec[4:5, at])

    loop(4, to_mid)

    def second_norm(i):
        n, _ = normal(mid[strip(i), :])
        a_low[strip(i), :] = (n * line(5) + line(6)).astype(BF16)

    loop(8, second_norm)

    def hidden(j):
        pre = dot(a_low[...], columns(4, 2 * j, 2)) + vec[pl.ds(8 + j // 4, 1), lanes(j % 4, 256)]
        half = 0.5 * (1.0 + lax.erf(pre * math.sqrt(0.5)))
        slope = half + pre * (jnp.exp(-0.5 * pre * pre) * (1.0 / math.sqrt(2.0 * math.pi)))
        low = (pre * half).astype(BF16)
        act[:, lanes(j, 256)] = low
        left[pl.ds(24 + 2 * j, 2)] = low.T.reshape(2, 128, ROWS)
        weights = rows_of(5, 2 * j, 2)
        w_out[lanes(j, 256), :] = weights
        d_pre = (dot_nt(stack(64, 8), weights) * slope).astype(BF16)
        right[32 + 2 * j] = d_pre[:, :128]
        right[33 + 2 * j] = d_pre[:, 128:]
        add_sums(8 + j // 4, d_pre.astype(F32), lanes(j % 4, 256))

    loop(16, hidden)

    def second_back(j):
        at = lanes(j, 256)
        left[pl.ds(16 + 2 * j, 2)] = a_low[:, at].T.reshape(2, 128, ROWS)
        d_a[:, at] = dot_nt(stack(32, 32), rows_of(4, 2 * j, 2))

    loop(4, second_back)

    def mid_back(i):
        rows = strip(i)
        n, scale = normal(mid[rows, :])
        d = d_a[rows, :]
        e = d * line(5)
        inner = e - jnp.mean(e, -1, keepdims=True) - n * jnp.mean(e * n, -1, keepdims=True)
        whole = d_mid[rows, :] + inner * scale
        d_mid[rows, :] = whole
        low = whole.astype(BF16)
        for c in range(8):
            right[24 + c, rows, :] = low[:, c * 128 : (c + 1) * 128]
        add_sums(5, d * n)
        add_sums(6, d)
        add_sums(4, low.astype(F32))

    loop(8, mid_back)

    def att_back(j):
        att[:, lanes(j, 256)] = dot_nt(stack(24, 8), rows_of(3, 2 * j, 2)).astype(BF16)

    loop(4, att_back)

    def heads_back(j):
        at = lanes(j, 128)
        vp = v[:, at]
        q_parts, k_parts, da_parts = split(q[:, at]), split(k[:, at]), split(att[:, at])
        d_raws, weights = [], []
        for h in range(2):
            low = probs[2 * j + h]
            p = low.astype(F32)
            d_p = dot_nt(da_parts[h], vp)
            d_m = p * (d_p - jnp.sum(p * d_p, -1, keepdims=True))
            d_raws.append(jnp.where(wall[...] == 0.0, d_m * SCALE, 0.0).astype(BF16))
            weights.append(low)
        d_q = dot(jnp.concatenate(d_raws, 1), jnp.concatenate(k_parts, 0)).astype(BF16)
        d_k = dot_tn(jnp.concatenate(d_raws, 0), jnp.concatenate(q_parts, 0)).astype(BF16)
        d_v = dot_tn(jnp.concatenate(weights, 0), jnp.concatenate(da_parts, 0)).astype(BF16)
        right[j] = d_q
        right[8 + j] = d_k
        right[16 + j] = d_v
        add_sums(2, d_q.astype(F32), at)
        add_sums(3, d_v.astype(F32), at)

    loop(8, heads_back)

    def first_back(j):
        weights = jnp.concatenate([rows_of(m, 2 * j, 2) for m in range(3)], 1)
        d_a[:, lanes(j, 256)] = dot_nt(stack(0, 24), weights)

    loop(4, first_back)

    def token_back(i):
        rows = strip(i)
        n, scale = normal(tokens[rows, :])
        d = d_a[rows, :]
        e = d * line(0)
        inner = e - jnp.mean(e, -1, keepdims=True) - n * jnp.mean(e * n, -1, keepdims=True)
        d_mid[rows, :] = d_mid[rows, :] + inner * scale
        add_sums(0, d * n)
        add_sums(1, d)

    for copy in sends:
        copy.wait_send()
    announce(ready)
    loop(8, token_back)
    input_grad[...] = d_mid[0:TOKENS, :].astype(BF16)
    folded = jnp.sum(sums[...], 1)
    vec_out[0] = folded[:8]
    vec_out[1, 0 : NV - 8] = folded[8:]
    vec_out[1, NV - 8 :] = jnp.zeros((16 - NV, D), F32)

    def last(j):
        at = lanes(j, 256)
        d_a[:, at] = mid[:, at] + (dot(act[...], w_out[:, at]) + vec[7:8, at])

    return last


ROUNDS = (
    (2, 2), (2, 1), (1, 2), (3, 2), (2, 3), (1, 1), (3, 1), (0, 2), (2, 0), (1, 3), (3, 3), (0, 1), (1, 0), (3, 0), (0, 3), (0, 0),
)
AHEAD = 1
RING = 2 * AHEAD + 2


VMEM_LIMIT = 62 * MIB


class Rows:
    def __init__(self, buffer, first):
        self.buffer, self.first = buffer, first

    def row(self, n):
        return self.buffer.at[pl.ds(64 * (self.first + n), 64)]

    def half(self, n, second):
        return self.buffer.at[pl.ds(64 * (self.first + n) + 32 * second, 32)]

    def get(self, n, ai):
        return self.buffer[pl.ds(64 * (self.first + n) + 16 * ai, 16)].reshape(256, SIDE).astype(F32)

    def put(self, n, ai, value):
        self.buffer[pl.ds(64 * (self.first + n) + 16 * ai, 16)] = value.astype(BF16).reshape(16, 16, SIDE)


def scatter_kernel(
    left_at, right_at, left, right, vec_in,
    total, window, norm_tile,
    g, kept, b_out, b_in, b_half, a_out, a_in,
    vec_y, vec_y_in, vec_x, vec_x_in, vec_z, vec_z_in, vec_t, tiles,
    tw_send, tw_recv, c_send, c_recv, b_send, b_recv, a_send, a_recv, v_send, v_recv, n_send, n_recv,
    between,
):
    pos, core = place()
    twin = device(pos, 1 - core)
    axes = [[device(moved(pos, a, s), core) for s in (1, 2, 3)] for a in range(3)]
    plane, column = partners()
    tw_out, tw_in, c_out, c_in, c_half = (Rows(g, at) for at in (0, 3 * RING, 6 * RING, 6 * RING + 36, 6 * RING + 60))

    def pick(options, i):
        value = options[-1]
        for n in range(len(options) - 2, -1, -1):
            value = jnp.where(i == n, options[n], value)
        return value

    def axis_of(p, which):
        return lax.rem(p + which, 3)

    def neighbour(p, which, by):
        axis = axis_of(p, which)
        return tuple(pick([axes[a][by - 1][n] for a in range(3)], axis) for n in range(2))

    def along(p, which, by):
        return lax.rem(pick(pos, axis_of(p, which)) + by, 4)

    def pair(p, ci, bi, ai, of_core):
        spots = [along(p, 0, ai), along(p, 1, bi), along(p, 2, ci)]
        x, y, z = (pick([spots[(a - s) % 3] for s in range(3)], p) for a in range(3))
        wide, narrow = device((x, y, z), of_core)
        slot = (wide * 8 + narrow) * 6 + 2 * p
        made = []
        for i in range(2):
            made.append(dot(left[left_at[slot + i]], right[right_at[slot + i]]))
        return jnp.concatenate(made, 0)

    def remote(src, dst, send_sem, recv_sem, to):
        return pltpu.make_async_remote_copy(
            src_ref=src, dst_ref=dst, send_sem=send_sem, recv_sem=recv_sem, device_id=to, device_id_type=MESH
        )

    def twin_copy(k, p):
        n = 3 * (k % RING) + p
        return remote(tw_out.row(n), tw_in.row(n), tw_send.at[3 * k + p], tw_recv.at[3 * k + p], twin)

    def for_twin(k, p):
        if k >= len(ROUNDS):
            return
        if k >= RING:
            twin_copy(k - RING, p).wait_send()
        ci, bi = ROUNDS[k]
        for ai in range(4):
            tw_out.put(3 * (k % RING) + p, ai, pair(p, ci, bi, ai, 1 - core))
        twin_copy(k, p).start()

    def chip_sum(k, p, ai):
        ci, bi = ROUNDS[k]
        return pair(p, ci, bi, ai, core) + tw_in.get(3 * (k % RING) + p, ai)

    def c_half_copy(p, bi, second):
        n = p * 4 + bi
        return remote(
            c_out.half(n, second), c_half.half(n, second), c_send.at[2 * n + second], c_recv.at[2 * n + second],
            neighbour(p, 2, 3 if second else 1),
        )

    def c_whole_copy(p, bi, leftward):
        n = 12 * leftward + p * 4 + bi
        return remote(
            c_out.row(12 + n), c_in.row(n), c_send.at[24 + n], c_recv.at[24 + n], neighbour(p, 2, 3 if leftward else 1)
        )

    def b_half_copy(p, second):
        part = pl.ds(2 * second, 2)
        return remote(
            b_out.at[p, 0, part], b_half.at[p, part], b_send.at[4 * p + second], b_recv.at[4 * p + second],
            neighbour(p, 1, 3 if second else 1),
        )

    def b_whole_copy(p, leftward):
        return remote(
            b_out.at[p, 1 + leftward], b_in.at[p, leftward], b_send.at[4 * p + 2 + leftward],
            b_recv.at[4 * p + 2 + leftward], neighbour(p, 1, 3 if leftward else 1),
        )

    def a_copy(p, by):
        n = 3 * p + by - 1
        return remote(a_out.at[n], a_in.at[n], a_send.at[n], a_recv.at[n], neighbour(p, 0, by))

    def opposite_row(k, p):
        _, bi = ROUNDS[k]
        for ai in range(4):
            c_out.put(p * 4 + bi, ai, chip_sum(k, p, ai))
            if ai % 2:
                c_half_copy(p, bi, ai // 2).start()

    def side_row(k, p):
        ci, bi = ROUNDS[k]
        leftward = ci // 2
        n = p * 4 + bi
        c_half_copy(p, bi, leftward).wait_recv()
        for ai in range(4):
            value = chip_sum(k, p, ai)
            if ai // 2 == leftward:
                value = value + c_half.get(n, ai)
            c_out.put(12 + 12 * leftward + n, ai, value)
        c_whole_copy(p, bi, leftward).start()

    def own_row(k, p):
        _, bi = ROUNDS[k]
        n = p * 4 + bi
        leftward = bi // 2
        c_whole_copy(p, bi, 0).wait_recv()
        c_whole_copy(p, bi, 1).wait_recv()
        if bi % 2:
            b_half_copy(p, leftward).wait_recv()
        for ai in range(4):
            value = chip_sum(k, p, ai) + c_in.get(n, ai) + c_in.get(12 + n, ai)
            if bi == 0:
                kept[p, :, ai * 128 : (ai + 1) * 128] = value
                continue
            if bi % 2 and ai // 2 == leftward:
                value = value + b_half[p, ai].astype(F32)
            b_out[p, 0 if bi == 2 else 1 + leftward, ai] = value.astype(BF16)
            if bi == 2 and ai % 2:
                b_half_copy(p, ai // 2).start()
        if bi % 2:
            b_whole_copy(p, leftward).start()

    def vec_twin():
        return remote(vec_in.at[1 - core], vec_t.at[0], v_send.at[0], v_recv.at[0], twin)

    def vec_copy(axis, by):
        src, dst = ((vec_x, vec_x_in), (vec_y, vec_y_in), (vec_z, vec_z_in))[axis]
        n = 1 + 3 * axis + by - 1
        there = lax.rem(pos[axis] + by, 4)
        piece = src.at[there] if axis == 1 else src.at[there // 2] if axis == 0 else src
        return remote(piece, dst.at[by - 1], v_send.at[n], v_recv.at[n], axes[axis][by - 1])

    def vec_start(axis):
        for by in (1, 2, 3):
            vec_copy(axis, by).start()

    def vec_sum(axis, whole):
        dst = (vec_x_in, vec_y_in, vec_z_in)[axis]
        for by in (1, 2, 3):
            vec_copy(axis, by).wait_recv()
            whole = whole + dst[by - 1]
        return whole

    def vec_last():
        return remote(window.at[core], window.at[core], v_send.at[10], v_recv.at[10], twin)

    def vec_stage(stage):
        if stage == 0:
            vec_twin().wait_recv()
            whole = vec_in[core] + vec_t[0]
            for i in range(4):
                vec_y[i] = whole[:, 256 * i : 256 * i + 256]
            vec_start(1)
        elif stage == 1:
            whole = vec_sum(1, vec_y[pos[1]])
            for i in range(2):
                vec_x[i] = whole[:, 128 * i : 128 * i + 128]
            vec_start(0)
        elif stage == 2:
            vec_z[...] = vec_sum(0, vec_x[pos[0] // 2])
            vec_start(2)
        elif stage == 3:
            window[core] = vec_sum(2, vec_z[...])
            vec_last().start()

    vec_twin().start()
    for k in range(AHEAD):
        loop(3, lambda p: for_twin(k, p))
    for k, (ci, _) in enumerate(ROUNDS):

        def one_round(p):
            for_twin(k + AHEAD, p)
            twin_copy(k, p).wait_recv()
            (own_row if ci == 0 else opposite_row if ci == 2 else side_row)(k, p)

        loop(3, one_round)
        if k % 3 == 2:
            vec_stage(k // 3)
        between(k)

    def row_sum(p, ai):
        return kept[p, :, ai * 128 : (ai + 1) * 128] + b_in[p, 0, ai].astype(F32) + b_in[p, 1, ai].astype(F32)

    def last_axis(p):
        b_whole_copy(p, 0).wait_recv()
        b_whole_copy(p, 1).wait_recv()
        for by in (2, 1, 3):
            a_out[3 * p + by - 1] = row_sum(p, by).astype(BF16)
            a_copy(p, by).start()

    loop(3, last_axis)

    wide, narrow = lax.axis_index("wide"), lax.axis_index("narrow")
    remote(window.at[1 - core], window.at[1 - core], v_send.at[10], v_recv.at[10], twin).wait_recv()
    lane = lax.broadcasted_iota(jnp.int32, (8, 128), 1) // 8
    own_lanes = lane == lax.rem(wide, 2) * 8 + narrow
    squares = jnp.zeros((8, 128), F32)
    for i in range(2):
        own = jnp.where(own_lanes, window[i], 0.0)
        squares = squares + own * own

    for p in range(3):
        value = row_sum(p, 0)
        for by in (1, 3, 2):
            a_copy(p, by).wait_recv()
            value = value + a_in[3 * p + by - 1].astype(F32)
        total[2 * p] = value[:128]
        total[2 * p + 1] = value[128:]
        squares = squares + by_eights(value * value)

    def norm_copy(stage, i):
        n = 15 * stage + i
        to = (column if stage else plane)[i]
        return remote(tiles.at[stage], tiles.at[2 + n], n_send.at[n], n_recv.at[n], to)

    whole = squares
    for stage, count in ((0, 15), (1, 7)):
        tiles[stage] = whole
        for i in range(count):
            norm_copy(stage, i).start()
        for i in range(count):
            norm_copy(stage, i).wait_recv()
            whole = whole + tiles[2 + 15 * stage + i]
    norm_tile[...] = whole

    def sent(p):
        for k in range(len(ROUNDS) - RING, len(ROUNDS)):
            twin_copy(k, p).wait_send()
        for side in (0, 1):
            for bi in range(4):
                c_half_copy(p, bi, side).wait_send()
                c_whole_copy(p, bi, side).wait_send()
            b_half_copy(p, side).wait_send()
            b_whole_copy(p, side).wait_send()
        for by in (1, 2, 3):
            a_copy(p, by).wait_send()

    loop(3, sent)
    vec_twin().wait_send()
    vec_last().wait_send()
    for axis in range(3):
        for by in (1, 2, 3):
            vec_copy(axis, by).wait_send()
    for stage, count in ((0, 15), (1, 7)):
        for i in range(count):
            norm_copy(stage, i).wait_send()


def whole_kernel(
    block_at, left_at, right_at, master_in, vectors_in, patches, keep_in, cotangent,
    output, input_grad, total, window, norm_tile, *scratch,
):
    gathered, scattered = scratch[:PASS_SCRATCH], scratch[PASS_SCRATCH:]
    g, left, right, flats = gathered[:4]
    vec_in, *scattered = scattered
    ready = gathered[-1]
    last = pass_kernel(
        block_at, master_in, vectors_in, patches, keep_in, cotangent, output, input_grad, vec_in, *gathered
    )
    all_announced(ready)

    def between(k):
        if 1 <= k <= 4:
            last(k - 1)

    scatter_kernel(left_at, right_at, left, right, vec_in, total, window, norm_tile, g, flats, *scattered, between)
    output[...] = flats[3, 0:TOKENS, :].astype(BF16)


PASS_SCRATCH = 22


def forward_backward(block_at, left_at, right_at, master, vectors, patches, keep, cotangent):
    vmem = pl.BlockSpec(memory_space=pltpu.VMEM)
    flat, row = (ROWS, D), (4, 256, 128)
    dma = pltpu.SemaphoreType.DMA
    pass_scratch = [
        pltpu.VMEM((ALL_ROWS, 16, 128), BF16),
        pltpu.VMEM((56, 128, ROWS), BF16),
        pltpu.VMEM((72, ROWS, 128), BF16),
        pltpu.VMEM((4, *flat), F32),
        *[pltpu.VMEM(flat, BF16)] * 5,
        pltpu.VMEM((HEADS, ROWS, ROWS), BF16),
        pltpu.VMEM((ROWS, FF), BF16),
        pltpu.VMEM((FF, D), BF16),
        pltpu.VMEM((ROWS, ROWS), F32),
        pltpu.VMEM((NV, 8, D), F32),
        pltpu.VMEM((16, D), F32),
        pltpu.VMEM((6, SIDE, SIDE), F32),
        pltpu.VMEM((8, NV), F32),
        pltpu.VMEM((IMAGES, PATCHES), jnp.int32),
        dma((3, 40)),
        dma((3, 40)),
        dma((5,)),
        pltpu.SemaphoreType.REGULAR,
    ]
    assert len(pass_scratch) == PASS_SCRATCH
    return pl.pallas_call(
        whole_kernel,
        out_shape=[
            jax.ShapeDtypeStruct((TOKENS, D), BF16),
            jax.ShapeDtypeStruct((TOKENS, D), BF16),
            jax.ShapeDtypeStruct((6, SIDE, SIDE), F32),
            jax.ShapeDtypeStruct((2, 8, 128), F32),
            jax.ShapeDtypeStruct((8, 128), F32),
        ],
        in_specs=[pl.BlockSpec(memory_space=pltpu.SMEM)] * 3 + [pl.BlockSpec(memory_space=pltpu.HBM)] * 5,
        out_specs=[vmem] * 5,
        scratch_shapes=pass_scratch
        + [
            pltpu.VMEM((2, 8, D), F32),
            pltpu.VMEM((3, 3, *row), BF16),
            pltpu.VMEM((3, 2, *row), BF16),
            pltpu.VMEM((3, *row), BF16),
            pltpu.VMEM((9, 256, 128), BF16),
            pltpu.VMEM((9, 256, 128), BF16),
            pltpu.VMEM((4, 8, 256), F32),
            pltpu.VMEM((3, 8, 256), F32),
            pltpu.VMEM((2, 8, 128), F32),
            pltpu.VMEM((3, 8, 128), F32),
            pltpu.VMEM((8, 128), F32),
            pltpu.VMEM((3, 8, 128), F32),
            pltpu.VMEM((1, 8, D), F32),
            pltpu.VMEM((24, 8, 128), F32),
            dma((48,)), dma((48,)), dma((48,)), dma((48,)), dma((12,)), dma((12,)), dma((9,)), dma((9,)),
            dma((11,)), dma((11,)), dma((22,)), dma((22,)),
        ],
        compiler_params=pltpu.CompilerParams(
            collective_id=0, has_side_effects=True, vmem_limit_bytes=VMEM_LIMIT
        ),
        cost_estimate=pl.CostEstimate(
            flops=19_000_000_000, bytes_accessed=10_000_000, transcendentals=3_000_000
        ),
        name="forward_backward",
    )(block_at, left_at, right_at, master, vectors, patches, keep, cotangent)


def rounded_dot(left, right, over):
    return lax.dot_general(
        left.astype(BF16), right.astype(BF16), (over, ((), ())), preferred_element_type=F32
    )


def step_kernel(
    raw, window, norm_tile, shift, master, left_stats, right_stats, left_root, right_root, vectors, vec_accum,
    output_in, input_grad_in,
    block_grads, new_left, new_right, new_master, new_copy, vec_grads, vec_accum_new, vec_new, grad_norm,
    output, input_grad, sem,
):
    def copies():
        pairs = ((output_in, output), (input_grad_in, input_grad))
        return [pltpu.make_async_copy(src, dst, sem.at[i]) for i, (src, dst) in enumerate(pairs)]

    norm = jnp.sqrt(jnp.sum(norm_tile[...], keepdims=True))
    clip = 1.0 / jnp.maximum(norm, 1.0)

    @pl.when(pl.program_id(0) == 0)
    def _():
        for copy in copies():
            copy.start()
        grad_norm[...] = norm
        lanes = pltpu.roll(window[...].reshape(16, 128), shift[0], 1)
        grads = clip * lanes.T[:8, :NV]
        vec_grads[...] = grads
        accum = 0.5 * vec_accum[...] + 0.5 * grads * grads
        vec_accum_new[...] = accum
        vec_new[...] = vectors[...] - 0.5 * grads / (jnp.sqrt(accum) + 1e-08)

    for i in range(raw.shape[0]):
        grads = raw[i] * clip
        block_grads[i] = grads
        new_left[i] = 0.5 * left_stats[i] + 0.5 * rounded_dot(grads, grads, ((1,), (1,)))
        new_right[i] = 0.5 * right_stats[i] + 0.5 * rounded_dot(grads, grads, ((0,), (0,)))
        way = rounded_dot(rounded_dot(left_root[i], grads, ((1,), (0,))), right_root[i], ((1,), (0,)))
        master_now = master[i] - 0.5 * way
        new_master[i] = master_now
        new_copy[i] = master_now.astype(BF16)

    @pl.when(pl.program_id(0) == pl.num_programs(0) - 1)
    def _():
        for copy in copies():
            copy.wait()


def update(raw, window, norm_tile, shift, blocks_in, vectors, vec_accum, output, input_grad):
    per = 2
    blocks = pl.BlockSpec((per, SIDE, SIDE), lambda i: (i, 0, 0))
    anywhere = pl.BlockSpec(memory_space=pl.ANY)

    def whole(*shape):
        return pl.BlockSpec(shape, lambda i: (0,) * len(shape))

    f32_blocks = jax.ShapeDtypeStruct((6, SIDE, SIDE), F32)
    f32_vecs = jax.ShapeDtypeStruct((8, NV), F32)
    tokens = jax.ShapeDtypeStruct((TOKENS, D), BF16)
    return pl.pallas_call(
        step_kernel,
        grid=(6 // per,),
        out_shape=[f32_blocks] * 4
        + [jax.ShapeDtypeStruct((6, SIDE, SIDE), BF16)]
        + [f32_vecs] * 3
        + [jax.ShapeDtypeStruct((1, 1), F32)]
        + [tokens] * 2,
        in_specs=[blocks, whole(2, 8, 128), whole(8, 128), pl.BlockSpec(memory_space=pltpu.SMEM)]
        + [blocks] * 5
        + [whole(8, NV)] * 2
        + [anywhere] * 2,
        out_specs=[blocks] * 5 + [whole(8, NV)] * 3 + [whole(1, 1)] + [anywhere] * 2,
        scratch_shapes=[pltpu.SemaphoreType.DMA((2,))],
        compiler_params=pltpu.CompilerParams(vmem_limit_bytes=32 * MIB),
        name="update",
    )(raw, window, norm_tile, shift, *blocks_in, vectors, vec_accum, output, input_grad)


def body(
    patches, keep, cotangent, owner_table, master, left_stats, right_stats, left_root, right_root, vectors, vec_accum,
):
    wide, narrow = lax.axis_index("wide"), lax.axis_index("narrow")
    numbers = jnp.arange(NBLK, dtype=jnp.int32)
    held = owner_table[None, :] == numbers[:, None]
    block_at = jnp.sum(jnp.where(held, jnp.asarray(BLOCK_AT)[None, :], 0), 1)
    matrix = sum((owner_table >= first).astype(jnp.int32) for first in FIRST[1:])

    def by_matrix(values):
        return sum(jnp.where(matrix == m, value, 0) for m, value in enumerate(values))

    inner = owner_table - by_matrix(FIRST)
    block_row = jnp.where(matrix == 4, inner // 32, inner // 8)
    block_column = jnp.where(matrix == 4, inner % 32, inner % 8)
    left_at = by_matrix(LEFT_AT) + block_row
    right_at = by_matrix(RIGHT_AT) + block_column

    output, input_grad, raw, window, norm_tile = forward_backward(
        block_at, left_at, right_at, master, vectors.T, patches, keep, cotangent
    )
    lane = ((wide % 2) * 8 + narrow) * 8
    shift = jnp.reshape((128 - lane) % 128, (1,)).astype(jnp.int32)
    blocks_in = (master, left_stats, right_stats, left_root, right_root)
    *of_blocks, vec_grads, vec_accum_new, vec_new, grad_norm, output, input_grad = update(
        raw, window, norm_tile, shift, blocks_in, vectors.T, vec_accum.T, output, input_grad
    )
    return (output, input_grad, *of_blocks, vec_grads.T, vec_accum_new.T, vec_new.T, grad_norm.reshape(()))


def solution(mesh):
    rows, blocks, vecs = P(BOTH, None), P(BOTH, None, None), P(None, BOTH)
    return jax.shard_map(
        body,
        mesh=mesh,
        in_specs=(rows, rows, rows, P(), blocks, blocks, blocks, blocks, blocks, vecs, vecs),
        out_specs=(rows, rows, blocks, blocks, blocks, blocks, blocks, vecs, vecs, vecs, P()),
        check_vma=False,
    )
```

```python
import functools
import math

import jax
import jax.numpy as jnp
import numpy as np
from jax import lax
from jax.experimental import pallas as pl
from jax.experimental.pallas import tpu as pltpu
from jax.sharding import PartitionSpec as P

MESH = pl.DeviceIdType.MESH
BOTH = ("wide", "narrow")
F32, BF16 = jnp.float32, jnp.bfloat16
MIB = 2**20

D = 1024
FF = 4096
HEADS = 16
HEAD_DIM = 64
PATCHES = 49
IMAGES = 5
TOKENS = IMAGES * PATCHES
ROWS = 256
SIDE = 128
NBLK = 768
NV = 12
LAYER_EPS = 1e-05
MASKED = -1000000000.0
OUTSIDE = -3.0e38
SCALE = HEAD_DIM**-0.5

ORDERS = ((0, 1, 2), (1, 2, 0), (2, 0, 1))
SHARE = (16, 16, 17)
PART_FROM = (0, 128 * 16, 128 * 32)
ALL_ROWS = 128 * 49
NEXT = (0, 3, 1, 2)

FIRST = (0, 64, 128, 192, 256, 512)
WIDTH = (8, 8, 8, 8, 32, 8)
LEFT_AT = (0, 0, 0, 8, 16, 24)
RIGHT_AT = (0, 8, 16, 24, 32, 64)


def slot_places():
    block_at, vector_at = np.zeros(NBLK, np.int32), np.zeros(128, np.int32)
    for dev in range(128):
        wide, narrow = dev // 8, dev % 8
        core = wide % 2
        pos = (wide // 2 % 2 * 2 + narrow // 4, wide // 4, narrow % 4)
        for p, (a, b, c) in enumerate(ORDERS):
            at = PART_FROM[p] + (((core * 4 + pos[c]) * 4 + pos[b]) * 4 + pos[a]) * SHARE[p]
            block_at[dev * 6 + 2 * p] = at
            block_at[dev * 6 + 2 * p + 1] = at + 8
            if p == 2:
                vector_at[dev] = at + 16
    return block_at, vector_at


BLOCK_AT, VECTOR_AT = slot_places()


def place():
    wide, narrow = lax.axis_index("wide"), lax.axis_index("narrow")
    x = (wide // 2) % 2 * 2 + narrow // 4
    return (x, wide // 4, narrow % 4), wide % 2


def device(pos, core):
    x, y, z = pos
    return ((y * 2 + x // 2) * 2 + core, x % 2 * 4 + z)


def moved(pos, axis, by):
    return tuple((c + by) % 4 if a == axis else c for a, c in enumerate(pos))


def partners():
    pos, core = place()
    plane = [device(moved(moved(pos, 0, i), 1, j), core) for i in range(4) for j in range(4) if i or j]
    column = [
        device(moved(pos, 2, i), core if j == 0 else 1 - core) for j in range(2) for i in range(4) if i or j
    ]
    return plane, column


def announce(semaphore):
    plane, column = partners()
    for partner in plane + column:
        pl.semaphore_signal(semaphore, inc=1, device_id=partner, device_id_type=MESH)


def all_announced(semaphore):
    plane, column = partners()
    pl.semaphore_wait(semaphore, len(plane + column))


def loop(count, body, together=1):
    lax.fori_loop(0, count, lambda i, _: (body(i), None)[1], None, unroll=together)


def dot(left, right):
    return jnp.dot(left, right, preferred_element_type=F32)


def dot_nt(left, right):
    return lax.dot_general(left, right, (((1,), (1,)), ((), ())), preferred_element_type=F32)


def dot_tn(left, right):
    return lax.dot_general(left, right, (((0,), (0,)), ((), ())), preferred_element_type=F32)


def gather_weights(master, vectors, loads, g, send_sem, recv_sem, meanwhile):
    pos, core = place()
    twin = device(pos, 1 - core)
    near = {(a, s): device(moved(pos, a, s), core) for a in range(3) for s in (1, -1)}

    for load in loads:
        load.wait()

    for p in range(3):
        a, b, c = (pos[axis] for axis in ORDERS[p])
        start = PART_FROM[p] + (((core * 4 + c) * 4 + b) * 4 + a) * SHARE[p]
        g[pl.ds(start, 16)] = master[2 * p : 2 * p + 2].astype(BF16).reshape(16, 16, SIDE)
        if p == 2:
            wide, narrow = lax.axis_index("wide"), lax.axis_index("narrow")
            first_lane = (lax.rem(wide, 2) * 8 + narrow) * 8
            spread = lax.broadcasted_iota(jnp.int32, (8, 128), 1) == (
                lax.broadcasted_iota(jnp.int32, (8, 128), 0) + first_lane
            )
            tile = dot_tn(vectors[...].astype(BF16), spread.astype(BF16)).astype(BF16)
            g[start + 16] = jnp.concatenate([tile, jnp.zeros((16 - NV, 128), BF16)], 0)

    sends = []

    def copy_of(src, dst, p, slot, to):
        return pltpu.make_async_remote_copy(
            src_ref=src, dst_ref=dst, send_sem=send_sem.at[p, slot],
            recv_sem=recv_sem.at[p, slot], device_id=to, device_id_type=MESH,
        )

    def send(src, dst, p, slot, to):
        copy = copy_of(src, dst, p, slot, to)
        copy.start()
        sends.append(copy)

    def arrived(dst, p, slot):
        copy_of(dst, dst, p, slot, twin).wait_recv()

    def at(p, of_core, c, b, a=0, count=4, skip=0, rows=None):
        start = PART_FROM[p] + (((of_core * 4 + c % 4) * 4 + b % 4) * 4 + a % 4) * SHARE[p] + skip
        return g.at[pl.ds(start, count * SHARE[p] if rows is None else rows)]

    def spot(p):
        a, b, c = ORDERS[p]
        return pos[a], pos[b], pos[c]

    def row(p, ci, bi):
        _, b, c = spot(p)
        return at(p, core, c + ci, b + bi)

    def half_row(p, ci, bi, second):
        _, b, c = spot(p)
        return at(p, core, c + ci, b + bi, 2 if second else 0, 2)

    def chunk(p, ai):
        a, b, c = spot(p)
        return at(p, core, c, b, a + ai, 1)

    def half_chunk(p, ai, second):
        a, b, c = spot(p)
        return at(p, core, c, b, a + ai, 1, 8 if second else 0, SHARE[p] - 8 if second else 8)

    def to_twin(p, ci, bi):
        r = row(p, ci, bi)
        send(r, r, p, 24 + 4 * (ci % 4) + bi % 4, twin)

    def onward(p, base, axis, half):
        first, second = half(False), half(True)
        return (
            lambda: send(first, first, p, base + 2, near[axis, 1]),
            lambda: send(second, second, p, base + 3, near[axis, -1]),
        )

    def both(p, base, axis, src, dst):
        send(src, dst, p, base, near[axis, 1])
        send(src, dst, p, base + 1, near[axis, -1])

    parts = range(3)
    for p in parts:
        both(p, 0, ORDERS[p][0], chunk(p, 0), chunk(p, 0))
    for p in parts:
        axis = ORDERS[p][0]
        arrived(chunk(p, -1), p, 0)
        onward(p, 0, axis, lambda second: half_chunk(p, -1, second))[0]()
        arrived(chunk(p, 1), p, 1)
        onward(p, 0, axis, lambda second: half_chunk(p, 1, second))[1]()
    for p in parts:
        arrived(half_chunk(p, 2, False), p, 2)
        arrived(half_chunk(p, 2, True), p, 3)
        r = row(p, 0, 0)
        both(p, 4, ORDERS[p][1], r, r)
        both(p, 8, ORDERS[p][2], r, r)
        to_twin(p, 0, 0)
    for p in parts:
        for bi, i in ((-1, 1), (1, 2)):
            r = row(p, 0, bi)
            arrived(r, p, 4 + (i - 1))
            onward(p, 4, ORDERS[p][1], lambda second: half_row(p, 0, bi, second))[i - 1]()
            both(p, 8 + 4 * i, ORDERS[p][2], r, r)
            to_twin(p, 0, bi)

    meanwhile()

    def sides(p, i):
        bi = NEXT[i]
        for ci, j in ((-1, 0), (1, 1)):
            arrived(row(p, ci, bi), p, 8 + 4 * i + j)
            onward(p, 8 + 4 * i, ORDERS[p][2], lambda second: half_row(p, ci, bi, second))[j]()
            to_twin(p, ci, bi)

    def opposite(p, i):
        bi = NEXT[i]
        arrived(half_row(p, 2, bi, False), p, 8 + 4 * i + 2)
        arrived(half_row(p, 2, bi, True), p, 8 + 4 * i + 3)
        to_twin(p, 2, bi)

    for p in parts:
        sides(p, 0)
    for p in parts:
        arrived(half_row(p, 0, 2, False), p, 6)
        arrived(half_row(p, 0, 2, True), p, 7)
        r = row(p, 0, 2)
        both(p, 8 + 12, ORDERS[p][2], r, r)
        to_twin(p, 0, 2)
    for p in parts:
        sides(p, 1)
        sides(p, 2)
    for p in parts:
        opposite(p, 0)
    for p in parts:
        sides(p, 3)
    for p in parts:
        opposite(p, 1)
        opposite(p, 2)
    for p in parts:
        opposite(p, 3)
    for p in parts:
        _, b, c = spot(p)
        for ci in range(4):
            for bi in range(4):
                arrived(at(p, 1 - core, c + ci, b + bi), p, 24 + 4 * ci + bi)
    return sends


def normal(values):
    centre = jnp.mean(values, -1, keepdims=True)
    centred = values - centre
    spread = jnp.mean(centred * centred, -1, keepdims=True)
    scale = lax.rsqrt(spread + LAYER_EPS)
    return centred * scale, scale


def by_eights(values):
    return jnp.sum(values.reshape(values.shape[0] // 8, 8, values.shape[1]), 0)


def pass_kernel(
    owner_in, places_in, master_in, vectors_in, patches, keep_in, cotangent, output, input_grad, master, vec_out,
    g, left, right, flats, q, k, v, att, a_low, probs, act, w_out, wall, sums, vec,
    vectors, keep, owner, places, made, tables, send_sem, recv_sem, held_sem, ready,
):
    tokens, d_mid, mid, d_a = (flats.at[i] for i in range(4))
    loads = [
        pltpu.make_async_copy(src, to, held_sem.at[i])
        for i, (src, to) in enumerate(
            (
                (master_in, master), (vectors_in, vectors), (patches, output), (cotangent, input_grad), (keep_in, keep),
                (owner_in, owner), (places_in, places),
            )
        )
    ]
    for load in loads:
        load.start()

    def block(n):
        return g[pl.ds(tables[lax.div(n, 128), lax.rem(n, 128)], 8)].reshape(SIDE, SIDE)

    def columns(m, j, count):
        rows = (256 if m == 4 else 64 if m < 4 else 256) // WIDTH[m]
        return jnp.concatenate(
            [
                jnp.concatenate([block(FIRST[m] + r * WIDTH[m] + j + i) for i in range(count)], 1)
                for r in range(rows)
            ],
            0,
        )

    def rows_of(m, i, count):
        return jnp.concatenate(
            [
                jnp.concatenate([block(FIRST[m] + (i + r) * WIDTH[m] + c) for c in range(WIDTH[m])], 1)
                for r in range(count)
            ],
            0,
        )

    def lanes(i, width):
        return pl.ds(pl.multiple_of(i * width, width), width)

    def strip(i):
        return pl.ds(pl.multiple_of(i * 32, 32), 32)

    def stack(first, count):
        return jnp.concatenate([right[first + i] for i in range(count)], 1)

    def line(i):
        return vec[i : i + 1, :]

    def add_sums(i, value, where=slice(None)):
        sums[i, :, where] += by_eights(value)

    def first_normal(i):
        n, _ = normal(tokens[strip(i), :])
        d_a[strip(i), :] = n
        cot = d_mid[strip(i), :]
        for c in range(8):
            right[64 + c, strip(i), :] = cot[:, c * 128 : (c + 1) * 128].astype(BF16)
        add_sums(7, cot)

    def make_tables():
        number = owner[...]
        matrix = sum((number >= first).astype(jnp.int32) for first in FIRST[1:])

        def by_matrix(values):
            return sum(jnp.where(matrix == m, value, 0) for m, value in enumerate(values))

        inner = number - by_matrix(FIRST)
        wide_one = matrix == 4
        made[8:14, :] = by_matrix(LEFT_AT) + jnp.where(wide_one, inner >> 5, inner >> 3)
        made[16:22, :] = by_matrix(RIGHT_AT) + jnp.where(wide_one, inner & 31, inner & 7)
        lane = lax.broadcasted_iota(jnp.int32, (128, 128), 1)
        found = [jnp.zeros((8, 128), F32)] * 6
        for i in range(6):
            held_by = jnp.broadcast_to(number[i : i + 1].astype(F32), (128, 128)).T
            lies_at = jnp.broadcast_to(places[i : i + 1, :].astype(F32), (128, 128)).T
            for j in range(6):
                hit = held_by == (lane + 128 * j).astype(F32)
                found[j] = found[j] + by_eights(jnp.where(hit, lies_at, 0.0))
        for j in range(6):
            at = jnp.sum(found[j], 0, keepdims=True).astype(jnp.int32)
            made[j : j + 1, :] = jnp.clip(at, 0, ALL_ROWS - 8)

    def meanwhile():
        for load in loads[5:]:
            load.wait()
        make_tables()
        to_scalars = pltpu.make_async_copy(made, tables, held_sem.at[7])
        to_scalars.start()
        sums[...] = jnp.zeros_like(sums)
        for load in loads[2:5]:
            load.wait()
        for came, to in ((output, tokens), (input_grad, d_mid)):
            to[0:TOKENS, :] = came[...].astype(F32)
            to[TOKENS:ROWS, :] = jnp.zeros((ROWS - TOKENS, D), F32)
        row_at = lax.broadcasted_iota(jnp.int32, (ROWS, ROWS), 0)
        col_at = lax.broadcasted_iota(jnp.int32, (ROWS, ROWS), 1)

        def image(at):
            return sum((at >= PATCHES * (i + 1)).astype(jnp.int32) for i in range(IMAGES))

        spread = (
            lax.broadcasted_iota(jnp.int32, (PATCHES, ROWS), 1)
            - PATCHES * image(lax.broadcasted_iota(jnp.int32, (PATCHES, ROWS), 1))
            == lax.broadcasted_iota(jnp.int32, (PATCHES, ROWS), 0)
        )
        kept = dot(keep[...].astype(F32).astype(BF16), spread.astype(F32).astype(BF16))
        own = lax.broadcasted_iota(jnp.int32, (IMAGES, ROWS), 0) == image(
            lax.broadcasted_iota(jnp.int32, (IMAGES, ROWS), 1)
        )
        dropped = jnp.sum(jnp.where(own & (kept < 0.5), 1.0, 0.0), 0, keepdims=True)
        wall[...] = jnp.where(
            image(row_at) == image(col_at), jnp.broadcast_to(dropped, (ROWS, ROWS)) * MASKED, OUTSIDE
        )
        loop(8, first_normal, 2)
        to_scalars.wait()

    barrier = pltpu.get_barrier_semaphore()
    announce(barrier)
    all_announced(barrier)
    sends = gather_weights(master, vectors, loads[:2], g, send_sem, recv_sem, meanwhile)

    for w in range(8):
        window = sum(g[int(VECTOR_AT[16 * w + i])].astype(F32) for i in range(16))
        vec[:, w * 128 : (w + 1) * 128] = window

    def first_norm(i):
        a_low[strip(i), :] = (d_a[strip(i), :] * line(0) + line(1)).astype(BF16)

    loop(8, first_norm, 4)

    def project(j):
        left[pl.ds(2 * j, 2)] = a_low[:, lanes(j, 256)].T.reshape(2, 128, ROWS)
        at = lanes(j, 256)
        q[:, at] = (dot(a_low[...], columns(0, 2 * j, 2)) + vec[2:3, at]).astype(BF16)
        k[:, at] = dot(a_low[...], columns(1, 2 * j, 2)).astype(BF16)
        v[:, at] = (dot(a_low[...], columns(2, 2 * j, 2)) + vec[3:4, at]).astype(BF16)

    loop(4, project, 4)

    low_half = lax.broadcasted_iota(jnp.int32, (ROWS, 128), 1) < HEAD_DIM

    def split(pair):
        nothing = jnp.zeros_like(pair)
        return jnp.where(low_half, pair, nothing), jnp.where(low_half, nothing, pair)

    def attend(j):
        at = lanes(j, 128)
        kp = k[:, at]
        weights = []
        for h, qh in enumerate(split(q[:, at])):
            raw = dot_nt(qh, kp)
            masked = jnp.where(wall[...] == 0.0, raw * SCALE, wall[...])
            e = jnp.exp(masked - jnp.max(masked, -1, keepdims=True))
            p = e / jnp.sum(e, -1, keepdims=True)
            low = p.astype(BF16)
            probs[2 * j + h] = low
            weights.append(low)
        pair = dot(jnp.concatenate(weights, 1), jnp.concatenate(split(v[:, at]), 0)).astype(BF16)
        att[:, at] = pair
        left[8 + j] = pair.T

    loop(8, attend, 4)

    def to_mid(j):
        at = lanes(j, 256)
        mid[:, at] = tokens[:, at] + (dot(att[...], columns(3, 2 * j, 2)) + vec[4:5, at])

    loop(4, to_mid, 4)

    def second_norm(i):
        n, _ = normal(mid[strip(i), :])
        a_low[strip(i), :] = (n * line(5) + line(6)).astype(BF16)

    loop(8, second_norm, 8)

    def hidden(j):
        pre = dot(a_low[...], columns(4, 2 * j, 2)) + vec[pl.ds(8 + j // 4, 1), lanes(j % 4, 256)]
        half = 0.5 * (1.0 + lax.erf(pre * math.sqrt(0.5)))
        slope = half + pre * (jnp.exp(-0.5 * pre * pre) * (1.0 / math.sqrt(2.0 * math.pi)))
        low = (pre * half).astype(BF16)
        act[:, lanes(j, 256)] = low
        left[pl.ds(24 + 2 * j, 2)] = low.T.reshape(2, 128, ROWS)
        weights = rows_of(5, 2 * j, 2)
        w_out[lanes(j, 256), :] = weights
        d_pre = (dot_nt(stack(64, 8), weights) * slope).astype(BF16)
        right[32 + 2 * j] = d_pre[:, :128]
        right[33 + 2 * j] = d_pre[:, 128:]
        add_sums(8 + j // 4, d_pre.astype(F32), lanes(j % 4, 256))

    loop(16, hidden, 4)

    def second_back(j):
        at = lanes(j, 256)
        left[pl.ds(16 + 2 * j, 2)] = a_low[:, at].T.reshape(2, 128, ROWS)
        d_a[:, at] = dot_nt(stack(32, 32), rows_of(4, 2 * j, 2))

    loop(4, second_back, 4)

    def mid_back(i):
        rows = strip(i)
        n, scale = normal(mid[rows, :])
        d = d_a[rows, :]
        e = d * line(5)
        inner = e - jnp.mean(e, -1, keepdims=True) - n * jnp.mean(e * n, -1, keepdims=True)
        whole = d_mid[rows, :] + inner * scale
        d_mid[rows, :] = whole
        low = whole.astype(BF16)
        for c in range(8):
            right[24 + c, rows, :] = low[:, c * 128 : (c + 1) * 128]
        add_sums(5, d * n)
        add_sums(6, d)
        add_sums(4, low.astype(F32))

    loop(8, mid_back, 8)

    def att_back(j):
        att[:, lanes(j, 256)] = dot_nt(stack(24, 8), rows_of(3, 2 * j, 2)).astype(BF16)

    loop(4, att_back, 4)

    def heads_back(j):
        at = lanes(j, 128)
        vp = v[:, at]
        q_parts, k_parts, da_parts = split(q[:, at]), split(k[:, at]), split(att[:, at])
        d_raws, weights = [], []
        for h in range(2):
            low = probs[2 * j + h]
            p = low.astype(F32)
            d_p = dot_nt(da_parts[h], vp)
            d_m = p * (d_p - jnp.sum(p * d_p, -1, keepdims=True))
            d_raws.append(jnp.where(wall[...] == 0.0, d_m * SCALE, 0.0).astype(BF16))
            weights.append(low)
        d_q = dot(jnp.concatenate(d_raws, 1), jnp.concatenate(k_parts, 0)).astype(BF16)
        d_k = dot_tn(jnp.concatenate(d_raws, 0), jnp.concatenate(q_parts, 0)).astype(BF16)
        d_v = dot_tn(jnp.concatenate(weights, 0), jnp.concatenate(da_parts, 0)).astype(BF16)
        right[j] = d_q
        right[8 + j] = d_k
        right[16 + j] = d_v
        add_sums(2, d_q.astype(F32), at)
        add_sums(3, d_v.astype(F32), at)

    loop(8, heads_back, 4)

    def first_back(j):
        weights = jnp.concatenate([rows_of(m, 2 * j, 2) for m in range(3)], 1)
        d_a[:, lanes(j, 256)] = dot_nt(stack(0, 24), weights)

    loop(4, first_back, 4)

    def token_back(i):
        rows = strip(i)
        n, scale = normal(tokens[rows, :])
        d = d_a[rows, :]
        e = d * line(0)
        inner = e - jnp.mean(e, -1, keepdims=True) - n * jnp.mean(e * n, -1, keepdims=True)
        d_mid[rows, :] = d_mid[rows, :] + inner * scale
        add_sums(0, d * n)
        add_sums(1, d)

    for copy in sends:
        copy.wait_send()
    announce(ready)
    loop(8, token_back, 8)
    input_grad[...] = d_mid[0:TOKENS, :].astype(BF16)
    folded = jnp.sum(sums[...], 1)
    vec_out[0] = folded[:8]
    vec_out[1, 0 : NV - 8] = folded[8:]
    vec_out[1, NV - 8 :] = jnp.zeros((16 - NV, D), F32)

    def last(j):
        at = lanes(j, 256)
        d_a[:, at] = mid[:, at] + (dot(act[...], w_out[:, at]) + vec[7:8, at])

    return last


ROUNDS = (
    (2, 2), (2, 1), (1, 2), (3, 2), (2, 3), (1, 1), (3, 1), (0, 2), (2, 0), (1, 3), (3, 3), (0, 1), (1, 0), (3, 0), (0, 3), (0, 0),
)
AHEAD = 1
RING = 2 * AHEAD + 2
OUT_RING = 6
OUT_ROUNDS = tuple(round_ for round_ in ROUNDS if round_[0])


VMEM_LIMIT = 62 * MIB


def in_hbm(array):
    return pltpu.with_memory_space_constraint(array, pltpu.HBM)


class Rows:
    def __init__(self, buffer, first):
        self.buffer, self.first = buffer, first

    def row(self, n):
        return self.buffer.at[pl.ds(64 * (self.first + n), 64)]

    def half(self, n, second):
        return self.buffer.at[pl.ds(64 * (self.first + n) + 32 * second, 32)]

    def get(self, n, ai):
        return self.buffer[pl.ds(64 * (self.first + n) + 16 * ai, 16)].reshape(256, SIDE).astype(F32)

    def put(self, n, ai, value):
        self.buffer[pl.ds(64 * (self.first + n) + 16 * ai, 16)] = value.astype(BF16).reshape(16, 16, SIDE)


def scatter_kernel(
    tables, left, right, vec_in,
    total, window, norm_tile,
    g, kept, a_out, a_in,
    vec_y, vec_y_in, vec_x, vec_x_in, vec_z, vec_z_in, vec_t, tiles,
    tw_send, tw_recv, c_send, c_recv, b_send, b_recv, a_send, a_recv, v_send, v_recv, n_send, n_recv,
    between,
):
    pos, core = place()
    twin = device(pos, 1 - core)
    axes = [[device(moved(pos, a, s), core) for s in (1, 2, 3)] for a in range(3)]
    plane, column = partners()
    sizes, at = (3 * RING, 3 * RING, 3 * OUT_RING, 24, 12, 9, 6, 3), 0
    places = []
    for size in sizes:
        places.append(Rows(g, at))
        at += size
    tw_out, tw_in, c_out, c_in, c_half, b_out, b_in, b_half = places

    def out_row(p, round_):
        return 3 * (OUT_ROUNDS.index(round_) % OUT_RING) + p

    def pick(options, i):
        value = options[-1]
        for n in range(len(options) - 2, -1, -1):
            value = jnp.where(i == n, options[n], value)
        return value

    def axis_of(p, which):
        return lax.rem(p + which, 3)

    def neighbour(p, which, by):
        axis = axis_of(p, which)
        return tuple(pick([axes[a][by - 1][n] for a in range(3)], axis) for n in range(2))

    def along(p, which, by):
        return lax.rem(pick(pos, axis_of(p, which)) + by, 4)

    def pair(p, ci, bi, ai, of_core):
        spots = [along(p, 0, ai), along(p, 1, bi), along(p, 2, ci)]
        x, y, z = (pick([spots[(a - s) % 3] for s in range(3)], p) for a in range(3))
        wide, narrow = device((x, y, z), of_core)
        slot = (wide * 8 + narrow) * 6 + 2 * p
        made = []
        for i in range(2):
            row, lane = lax.div(slot + i, 128), lax.rem(slot + i, 128)
            made.append(dot(left[tables[8 + row, lane]], right[tables[16 + row, lane]]))
        return jnp.concatenate(made, 0)

    def remote(src, dst, send_sem, recv_sem, to):
        return pltpu.make_async_remote_copy(
            src_ref=src, dst_ref=dst, send_sem=send_sem, recv_sem=recv_sem, device_id=to, device_id_type=MESH
        )

    def twin_copy(k, p):
        n = 3 * (k % RING) + p
        return remote(tw_out.row(n), tw_in.row(n), tw_send.at[3 * k + p], tw_recv.at[3 * k + p], twin)

    def for_twin(k, p):
        if k >= len(ROUNDS):
            return
        if k >= RING:
            twin_copy(k - RING, p).wait_send()
        ci, bi = ROUNDS[k]
        for ai in range(4):
            tw_out.put(3 * (k % RING) + p, ai, pair(p, ci, bi, ai, 1 - core))
        twin_copy(k, p).start()

    def chip_sum(k, p, ai):
        ci, bi = ROUNDS[k]
        return pair(p, ci, bi, ai, core) + tw_in.get(3 * (k % RING) + p, ai)

    def c_half_copy(p, bi, second):
        n = p * 4 + bi
        return remote(
            c_out.half(out_row(p, (2, bi)), second), c_half.half(n, second), c_send.at[2 * n + second], c_recv.at[2 * n + second],
            neighbour(p, 2, 3 if second else 1),
        )

    def c_whole_copy(p, bi, leftward):
        n = 12 * leftward + p * 4 + bi
        return remote(
            c_out.row(out_row(p, (1 + 2 * leftward, bi))), c_in.row(n), c_send.at[24 + n], c_recv.at[24 + n], neighbour(p, 2, 3 if leftward else 1)
        )

    def free_out(p, round_):
        before = OUT_ROUNDS.index(round_) - OUT_RING
        if before >= 0:
            left_out(p, OUT_ROUNDS[before])

    def left_out(p, round_):
        ci, bi = round_
        if ci == 2:
            c_half_copy(p, bi, 0).wait_send()
            c_half_copy(p, bi, 1).wait_send()
        else:
            c_whole_copy(p, bi, ci // 2).wait_send()

    def b_half_copy(p, second):
        return remote(
            b_out.half(3 * p, second), b_half.half(p, second), b_send.at[4 * p + second], b_recv.at[4 * p + second],
            neighbour(p, 1, 3 if second else 1),
        )

    def b_whole_copy(p, leftward):
        return remote(
            b_out.row(3 * p + 1 + leftward), b_in.row(2 * p + leftward), b_send.at[4 * p + 2 + leftward],
            b_recv.at[4 * p + 2 + leftward], neighbour(p, 1, 3 if leftward else 1),
        )

    def a_copy(p, by):
        n = 3 * p + by - 1
        return remote(a_out.at[n], a_in.at[n], a_send.at[n], a_recv.at[n], neighbour(p, 0, by))

    def opposite_row(k, p):
        _, bi = ROUNDS[k]
        free_out(p, ROUNDS[k])
        for ai in range(4):
            c_out.put(out_row(p, ROUNDS[k]), ai, chip_sum(k, p, ai))
            if ai % 2:
                c_half_copy(p, bi, ai // 2).start()

    def side_row(k, p):
        ci, bi = ROUNDS[k]
        leftward = ci // 2
        n = p * 4 + bi
        c_half_copy(p, bi, leftward).wait_recv()
        free_out(p, ROUNDS[k])
        for ai in range(4):
            value = chip_sum(k, p, ai)
            if ai // 2 == leftward:
                value = value + c_half.get(n, ai)
            c_out.put(out_row(p, ROUNDS[k]), ai, value)
        c_whole_copy(p, bi, leftward).start()

    def own_row(k, p):
        _, bi = ROUNDS[k]
        n = p * 4 + bi
        leftward = bi // 2
        c_whole_copy(p, bi, 0).wait_recv()
        c_whole_copy(p, bi, 1).wait_recv()
        if bi % 2:
            b_half_copy(p, leftward).wait_recv()
        for ai in range(4):
            value = chip_sum(k, p, ai) + c_in.get(n, ai) + c_in.get(12 + n, ai)
            if bi == 0:
                kept[p, :, ai * 128 : (ai + 1) * 128] = value
                continue
            if bi % 2 and ai // 2 == leftward:
                value = value + b_half.get(p, ai)
            b_out.put(3 * p + (0 if bi == 2 else 1 + leftward), ai, value)
            if bi == 2 and ai % 2:
                b_half_copy(p, ai // 2).start()
        if bi % 2:
            b_whole_copy(p, leftward).start()

    def vec_twin():
        return remote(vec_in.at[1 - core], vec_t.at[0], v_send.at[0], v_recv.at[0], twin)

    def vec_copy(axis, by):
        src, dst = ((vec_x, vec_x_in), (vec_y, vec_y_in), (vec_z, vec_z_in))[axis]
        n = 1 + 3 * axis + by - 1
        there = lax.rem(pos[axis] + by, 4)
        piece = src.at[there] if axis == 1 else src.at[there // 2] if axis == 0 else src
        return remote(piece, dst.at[by - 1], v_send.at[n], v_recv.at[n], axes[axis][by - 1])

    def vec_start(axis):
        for by in (1, 2, 3):
            vec_copy(axis, by).start()

    def vec_sum(axis, whole):
        dst = (vec_x_in, vec_y_in, vec_z_in)[axis]
        for by in (1, 2, 3):
            vec_copy(axis, by).wait_recv()
            whole = whole + dst[by - 1]
        return whole

    def vec_last():
        return remote(window.at[core], window.at[core], v_send.at[10], v_recv.at[10], twin)

    def vec_stage(stage):
        if stage == 0:
            vec_twin().wait_recv()
            whole = vec_in[core] + vec_t[0]
            for i in range(4):
                vec_y[i] = whole[:, 256 * i : 256 * i + 256]
            vec_start(1)
        elif stage == 1:
            whole = vec_sum(1, vec_y[pos[1]])
            for i in range(2):
                vec_x[i] = whole[:, 128 * i : 128 * i + 128]
            vec_start(0)
        elif stage == 2:
            vec_z[...] = vec_sum(0, vec_x[pos[0] // 2])
            vec_start(2)
        elif stage == 3:
            window[core] = vec_sum(2, vec_z[...])
            vec_last().start()

    vec_twin().start()
    for k in range(AHEAD):
        loop(3, lambda p: for_twin(k, p))
    for k, (ci, _) in enumerate(ROUNDS):

        def one_round(p):
            for_twin(k + AHEAD, p)
            twin_copy(k, p).wait_recv()
            (own_row if ci == 0 else opposite_row if ci == 2 else side_row)(k, p)

        loop(3, one_round)
        if k % 3 == 2:
            vec_stage(k // 3)
        between(k)

    def row_sum(p, ai):
        return kept[p, :, ai * 128 : (ai + 1) * 128] + b_in.get(2 * p, ai) + b_in.get(2 * p + 1, ai)

    def last_axis(p):
        b_whole_copy(p, 0).wait_recv()
        b_whole_copy(p, 1).wait_recv()
        for by in (2, 1, 3):
            a_out[3 * p + by - 1] = row_sum(p, by).astype(BF16)
            a_copy(p, by).start()

    loop(3, last_axis)

    wide, narrow = lax.axis_index("wide"), lax.axis_index("narrow")
    remote(window.at[1 - core], window.at[1 - core], v_send.at[10], v_recv.at[10], twin).wait_recv()
    lane = lax.broadcasted_iota(jnp.int32, (8, 128), 1) // 8
    own_lanes = lane == lax.rem(wide, 2) * 8 + narrow
    squares = jnp.zeros((8, 128), F32)
    for i in range(2):
        own = jnp.where(own_lanes, window[i], 0.0)
        squares = squares + own * own

    for p in range(3):
        value = row_sum(p, 0)
        for by in (1, 3, 2):
            a_copy(p, by).wait_recv()
            value = value + a_in[3 * p + by - 1].astype(F32)
        total[2 * p] = value[:128]
        total[2 * p + 1] = value[128:]
        squares = squares + by_eights(value * value)

    def norm_copy(stage, i):
        n = 15 * stage + i
        to = (column if stage else plane)[i]
        return remote(tiles.at[stage], tiles.at[2 + n], n_send.at[n], n_recv.at[n], to)

    whole = squares
    for stage, count in ((0, 15), (1, 7)):
        tiles[stage] = whole
        for i in range(count):
            norm_copy(stage, i).start()
        for i in range(count):
            norm_copy(stage, i).wait_recv()
            whole = whole + tiles[2 + 15 * stage + i]
    norm_tile[...] = whole

    def sent(p):
        for k in range(len(ROUNDS) - RING, len(ROUNDS)):
            twin_copy(k, p).wait_send()
        for round_ in OUT_ROUNDS[-OUT_RING:]:
            left_out(p, round_)
        for side in (0, 1):
            b_half_copy(p, side).wait_send()
            b_whole_copy(p, side).wait_send()
        for by in (1, 2, 3):
            a_copy(p, by).wait_send()

    loop(3, sent)
    vec_twin().wait_send()
    vec_last().wait_send()
    for axis in range(3):
        for by in (1, 2, 3):
            vec_copy(axis, by).wait_send()
    for stage, count in ((0, 15), (1, 7)):
        for i in range(count):
            norm_copy(stage, i).wait_send()


def whole_kernel(
    owner, places, master_in, vectors_in, patches, keep_in, cotangent,
    output, input_grad, total, window, norm_tile, *scratch,
):
    gathered, scattered = scratch[:PASS_SCRATCH], scratch[PASS_SCRATCH:]
    g, left, right, flats = gathered[:4]
    vec_in, *scattered = scattered
    ready = gathered[-1]
    last = pass_kernel(
        owner, places, master_in, vectors_in, patches, keep_in, cotangent, output, input_grad, total, vec_in, *gathered
    )
    all_announced(ready)

    def between(k):
        if 1 <= k <= 4:
            last(k - 1)

    scatter_kernel(gathered[TABLES], left, right, vec_in, total, window, norm_tile, g, flats, *scattered, between)
    output[...] = flats[3, 0:TOKENS, :].astype(BF16)


PASS_SCRATCH, TABLES = 25, 20


def forward_backward(*operands):
    vmem = pl.BlockSpec(memory_space=pltpu.VMEM)
    flat = (ROWS, D)
    dma = pltpu.SemaphoreType.DMA
    pass_scratch = [
        pltpu.VMEM((ALL_ROWS, 16, 128), BF16),
        pltpu.VMEM((56, 128, ROWS), BF16),
        pltpu.VMEM((72, ROWS, 128), BF16),
        pltpu.VMEM((4, *flat), F32),
        *[pltpu.VMEM(flat, BF16)] * 5,
        pltpu.VMEM((HEADS, ROWS, ROWS), BF16),
        pltpu.VMEM((ROWS, FF), BF16),
        pltpu.VMEM((FF, D), BF16),
        pltpu.VMEM((ROWS, ROWS), F32),
        pltpu.VMEM((NV, 8, D), F32),
        pltpu.VMEM((16, D), F32),
        pltpu.VMEM((8, NV), F32),
        pltpu.VMEM((IMAGES, PATCHES), jnp.int32),
        pltpu.VMEM((6, 128), jnp.int32),
        pltpu.VMEM((6, 128), jnp.int32),
        pltpu.VMEM((24, 128), jnp.int32),
        pltpu.SMEM((24, 128), jnp.int32),
        dma((3, 40)),
        dma((3, 40)),
        dma((8,)),
        pltpu.SemaphoreType.REGULAR,
    ]
    assert len(pass_scratch) == PASS_SCRATCH
    return pl.pallas_call(
        whole_kernel,
        out_shape=[
            jax.ShapeDtypeStruct((TOKENS, D), BF16),
            jax.ShapeDtypeStruct((TOKENS, D), BF16),
            jax.ShapeDtypeStruct((6, SIDE, SIDE), F32),
            jax.ShapeDtypeStruct((2, 8, 128), F32),
            jax.ShapeDtypeStruct((8, 128), F32),
        ],
        in_specs=[pl.BlockSpec(memory_space=pltpu.HBM)] * 7,
        out_specs=[vmem] * 5,
        scratch_shapes=pass_scratch
        + [
            pltpu.VMEM((2, 8, D), F32),
            pltpu.VMEM((9, 256, 128), BF16),
            pltpu.VMEM((9, 256, 128), BF16),
            pltpu.VMEM((4, 8, 256), F32),
            pltpu.VMEM((3, 8, 256), F32),
            pltpu.VMEM((2, 8, 128), F32),
            pltpu.VMEM((3, 8, 128), F32),
            pltpu.VMEM((8, 128), F32),
            pltpu.VMEM((3, 8, 128), F32),
            pltpu.VMEM((1, 8, D), F32),
            pltpu.VMEM((24, 8, 128), F32),
            dma((48,)), dma((48,)), dma((48,)), dma((48,)), dma((12,)), dma((12,)), dma((9,)), dma((9,)),
            dma((11,)), dma((11,)), dma((22,)), dma((22,)),
        ],
        compiler_params=pltpu.CompilerParams(
            collective_id=0, has_side_effects=True, vmem_limit_bytes=VMEM_LIMIT
        ),
        cost_estimate=pl.CostEstimate(
            flops=19_000_000_000, bytes_accessed=10_000_000, transcendentals=3_000_000
        ),
        name="forward_backward",
    )(*(in_hbm(operand) for operand in operands))


def rounded_dot(left, right, over):
    return lax.dot_general(
        left.astype(BF16), right.astype(BF16), (over, ((), ())), preferred_element_type=F32
    )


def step_kernel(
    raw, window, norm_tile, shift, master, left_stats, right_stats, left_root, right_root, vectors, vec_accum,
    output_in, input_grad_in,
    block_grads, new_left, new_right, new_master, new_copy, vec_grads, vec_accum_new, vec_new, grad_norm,
    output, input_grad, passing, sem,
):
    def copies(way):
        ends = ((output_in, output), (input_grad_in, input_grad))
        return [
            pltpu.make_async_copy(
                passing.at[i] if way else pair[0], pair[1] if way else passing.at[i], sem.at[2 * way + i]
            )
            for i, pair in enumerate(ends)
        ]

    norm = jnp.sqrt(jnp.sum(norm_tile[...], keepdims=True))
    clip = 1.0 / jnp.maximum(norm, 1.0)

    @pl.when(pl.program_id(0) == 0)
    def _():
        for copy in copies(0):
            copy.start()
        grad_norm[...] = norm
        lanes = pltpu.roll(window[...].reshape(16, 128), shift[0], 1)
        grads = clip * lanes.T[:8, :NV]
        vec_grads[...] = grads
        accum = 0.5 * vec_accum[...] + 0.5 * grads * grads
        vec_accum_new[...] = accum
        vec_new[...] = vectors[...] - 0.5 * grads / (jnp.sqrt(accum) + 1e-08)

    for i in range(raw.shape[0]):
        grads = raw[i] * clip
        block_grads[i] = grads
        new_left[i] = 0.5 * left_stats[i] + 0.5 * rounded_dot(grads, grads, ((1,), (1,)))
        new_right[i] = 0.5 * right_stats[i] + 0.5 * rounded_dot(grads, grads, ((0,), (0,)))
        way = rounded_dot(rounded_dot(left_root[i], grads, ((1,), (0,))), right_root[i], ((1,), (0,)))
        master_now = master[i] - 0.5 * way
        new_master[i] = master_now
        new_copy[i] = master_now.astype(BF16)

    @pl.when(pl.program_id(0) == 0)
    def _():
        for came, copy in zip(copies(0), copies(1)):
            came.wait()
            copy.start()

    @pl.when(pl.program_id(0) == pl.num_programs(0) - 1)
    def _():
        for copy in copies(1):
            copy.wait()


def update(raw, window, norm_tile, shift, blocks_in, vectors, vec_accum, output, input_grad):
    per = 2
    blocks = pl.BlockSpec((per, SIDE, SIDE), lambda i: (i, 0, 0))
    anywhere = pl.BlockSpec(memory_space=pltpu.HBM)

    def whole(*shape):
        return pl.BlockSpec(shape, lambda i: (0,) * len(shape))

    f32_blocks = jax.ShapeDtypeStruct((6, SIDE, SIDE), F32)
    f32_vecs = jax.ShapeDtypeStruct((8, NV), F32)
    tokens = jax.ShapeDtypeStruct((TOKENS, D), BF16)
    return pl.pallas_call(
        step_kernel,
        grid=(6 // per,),
        out_shape=[f32_blocks] * 4
        + [jax.ShapeDtypeStruct((6, SIDE, SIDE), BF16)]
        + [f32_vecs] * 3
        + [jax.ShapeDtypeStruct((1, 1), F32)]
        + [tokens] * 2,
        in_specs=[blocks, whole(2, 8, 128), whole(8, 128), pl.BlockSpec(memory_space=pltpu.SMEM)]
        + [blocks] * 5
        + [whole(8, NV)] * 2
        + [anywhere] * 2,
        out_specs=[blocks] * 5 + [whole(8, NV)] * 3 + [whole(1, 1)] + [anywhere] * 2,
        scratch_shapes=[pltpu.VMEM((2, TOKENS, D), BF16), pltpu.SemaphoreType.DMA((4,))],
        compiler_params=pltpu.CompilerParams(vmem_limit_bytes=32 * MIB),
        name="update",
    )(*(in_hbm(a) for a in (raw, window, norm_tile)), shift, *blocks_in, vectors, vec_accum, in_hbm(output), in_hbm(input_grad))


def body(
    patches, keep, cotangent, owner_table, master, left_stats, right_stats, left_root, right_root, vectors, vec_accum,
):
    wide, narrow = lax.axis_index("wide"), lax.axis_index("narrow")
    output, input_grad, raw, window, norm_tile = forward_backward(
        owner_table.reshape(6, 128), jnp.asarray(BLOCK_AT.reshape(6, 128)), master, vectors.T, patches, keep, cotangent
    )
    lane = ((wide % 2) * 8 + narrow) * 8
    shift = jnp.reshape((128 - lane) % 128, (1,)).astype(jnp.int32)
    blocks_in = (master, left_stats, right_stats, left_root, right_root)
    *of_blocks, vec_grads, vec_accum_new, vec_new, grad_norm, output, input_grad = update(
        raw, window, norm_tile, shift, blocks_in, vectors.T, vec_accum.T, output, input_grad
    )
    return (output, input_grad, *of_blocks, vec_grads.T, vec_accum_new.T, vec_new.T, grad_norm.reshape(()))


def solution(mesh):
    rows, blocks, vecs = P(BOTH, None), P(BOTH, None, None), P(None, BOTH)
    return jax.shard_map(
        body,
        mesh=mesh,
        in_specs=(rows, rows, rows, P(), blocks, blocks, blocks, blocks, blocks, vecs, vecs),
        out_specs=(rows, rows, blocks, blocks, blocks, blocks, blocks, vecs, vecs, vecs, P()),
        check_vma=False,
    )
```

```python
import functools
import math

import jax
import jax.numpy as jnp
import numpy as np
from jax import lax
from jax.experimental import pallas as pl
from jax.experimental.pallas import tpu as pltpu
from jax.sharding import PartitionSpec as P

MESH = pl.DeviceIdType.MESH
BOTH = ("wide", "narrow")
F32, BF16 = jnp.float32, jnp.bfloat16
MIB = 2**20

D = 1024
FF = 4096
HEADS = 16
HEAD_DIM = 64
PATCHES = 49
IMAGES = 5
TOKENS = IMAGES * PATCHES
ROWS = 256
SIDE = 128
NBLK = 768
NV = 12
LAYER_EPS = 1e-05
MASKED = -1000000000.0
OUTSIDE = -3.0e38
SCALE = HEAD_DIM**-0.5

ORDERS = ((0, 1, 2), (1, 2, 0), (2, 0, 1))
SHARE = (16, 16, 17)
PART_FROM = (0, 128 * 16, 128 * 32)
ALL_ROWS = 128 * 49
NEXT = (0, 3, 1, 2)

FIRST = (0, 64, 128, 192, 256, 512)
WIDTH = (8, 8, 8, 8, 32, 8)
LEFT_AT = (0, 0, 0, 8, 16, 24)
RIGHT_AT = (0, 8, 16, 24, 32, 64)


def slot_places():
    block_at, vector_at = np.zeros(NBLK, np.int32), np.zeros(128, np.int32)
    for dev in range(128):
        wide, narrow = dev // 8, dev % 8
        core = wide % 2
        pos = (wide // 2 % 2 * 2 + narrow // 4, wide // 4, narrow % 4)
        for p, (a, b, c) in enumerate(ORDERS):
            at = PART_FROM[p] + (((core * 4 + pos[c]) * 4 + pos[b]) * 4 + pos[a]) * SHARE[p]
            block_at[dev * 6 + 2 * p] = at
            block_at[dev * 6 + 2 * p + 1] = at + 8
            if p == 2:
                vector_at[dev] = at + 16
    return block_at, vector_at


BLOCK_AT, VECTOR_AT = slot_places()


def place():
    wide, narrow = lax.axis_index("wide"), lax.axis_index("narrow")
    x = (wide // 2) % 2 * 2 + narrow // 4
    return (x, wide // 4, narrow % 4), wide % 2


def device(pos, core):
    x, y, z = pos
    return ((y * 2 + x // 2) * 2 + core, x % 2 * 4 + z)


def moved(pos, axis, by):
    return tuple((c + by) % 4 if a == axis else c for a, c in enumerate(pos))


def partners():
    pos, core = place()
    plane = [device(moved(moved(pos, 0, i), 1, j), core) for i in range(4) for j in range(4) if i or j]
    column = [
        device(moved(pos, 2, i), core if j == 0 else 1 - core) for j in range(2) for i in range(4) if i or j
    ]
    return plane, column


def neighbours():
    pos, core = place()
    return [device(pos, 1 - core)] + [device(moved(pos, a, s), core) for a in range(3) for s in (1, -1)]


def announce(semaphore, others):
    for other in others:
        pl.semaphore_signal(semaphore, inc=1, device_id=other, device_id_type=MESH)


def all_announced(semaphore, others):
    pl.semaphore_wait(semaphore, len(others))


def loop(count, body, together=1):
    lax.fori_loop(0, count, lambda i, _: (body(i), None)[1], None, unroll=together)


def dot(left, right):
    return jnp.dot(left, right, preferred_element_type=F32)


def dot_nt(left, right):
    return lax.dot_general(left, right, (((1,), (1,)), ((), ())), preferred_element_type=F32)


def dot_tn(left, right):
    return lax.dot_general(left, right, (((0,), (0,)), ((), ())), preferred_element_type=F32)


def gather_weights(master, vectors, loads, g, send_sem, recv_sem, meanwhile):
    pos, core = place()
    twin = device(pos, 1 - core)
    near = {(a, s): device(moved(pos, a, s), core) for a in range(3) for s in (1, -1)}

    for load in loads:
        load.wait()

    for p in range(3):
        a, b, c = (pos[axis] for axis in ORDERS[p])
        start = PART_FROM[p] + (((core * 4 + c) * 4 + b) * 4 + a) * SHARE[p]
        g[pl.ds(start, 16)] = master[2 * p : 2 * p + 2].astype(BF16).reshape(16, 16, SIDE)
        if p == 2:
            wide, narrow = lax.axis_index("wide"), lax.axis_index("narrow")
            first_lane = (lax.rem(wide, 2) * 8 + narrow) * 8
            spread = lax.broadcasted_iota(jnp.int32, (8, 128), 1) == (
                lax.broadcasted_iota(jnp.int32, (8, 128), 0) + first_lane
            )
            tile = dot_tn(vectors[...].astype(BF16), spread.astype(BF16)).astype(BF16)
            g[start + 16] = jnp.concatenate([tile, jnp.zeros((16 - NV, 128), BF16)], 0)

    sends = []

    def copy_of(src, dst, p, slot, to):
        return pltpu.make_async_remote_copy(
            src_ref=src, dst_ref=dst, send_sem=send_sem.at[p, slot],
            recv_sem=recv_sem.at[p, slot], device_id=to, device_id_type=MESH,
        )

    def send(src, dst, p, slot, to):
        copy = copy_of(src, dst, p, slot, to)
        copy.start()
        sends.append(copy)

    def arrived(dst, p, slot):
        copy_of(dst, dst, p, slot, twin).wait_recv()

    def at(p, of_core, c, b, a=0, count=4, skip=0, rows=None):
        start = PART_FROM[p] + (((of_core * 4 + c % 4) * 4 + b % 4) * 4 + a % 4) * SHARE[p] + skip
        return g.at[pl.ds(start, count * SHARE[p] if rows is None else rows)]

    def spot(p):
        a, b, c = ORDERS[p]
        return pos[a], pos[b], pos[c]

    def row(p, ci, bi):
        _, b, c = spot(p)
        return at(p, core, c + ci, b + bi)

    def half_row(p, ci, bi, second):
        _, b, c = spot(p)
        return at(p, core, c + ci, b + bi, 2 if second else 0, 2)

    def chunk(p, ai):
        a, b, c = spot(p)
        return at(p, core, c, b, a + ai, 1)

    def half_chunk(p, ai, second):
        a, b, c = spot(p)
        return at(p, core, c, b, a + ai, 1, 8 if second else 0, SHARE[p] - 8 if second else 8)

    def to_twin(p, ci, bi):
        r = row(p, ci, bi)
        send(r, r, p, 24 + 4 * (ci % 4) + bi % 4, twin)

    def onward(p, base, axis, half):
        first, second = half(False), half(True)
        return (
            lambda: send(first, first, p, base + 2, near[axis, 1]),
            lambda: send(second, second, p, base + 3, near[axis, -1]),
        )

    def both(p, base, axis, src, dst):
        send(src, dst, p, base, near[axis, 1])
        send(src, dst, p, base + 1, near[axis, -1])

    parts = range(3)
    for p in parts:
        both(p, 0, ORDERS[p][0], chunk(p, 0), chunk(p, 0))
    for p in parts:
        axis = ORDERS[p][0]
        arrived(chunk(p, -1), p, 0)
        onward(p, 0, axis, lambda second: half_chunk(p, -1, second))[0]()
        arrived(chunk(p, 1), p, 1)
        onward(p, 0, axis, lambda second: half_chunk(p, 1, second))[1]()
    for p in parts:
        arrived(half_chunk(p, 2, False), p, 2)
        arrived(half_chunk(p, 2, True), p, 3)
        r = row(p, 0, 0)
        both(p, 4, ORDERS[p][1], r, r)
        both(p, 8, ORDERS[p][2], r, r)
        to_twin(p, 0, 0)
    for p in parts:
        for bi, i in ((-1, 1), (1, 2)):
            r = row(p, 0, bi)
            arrived(r, p, 4 + (i - 1))
            onward(p, 4, ORDERS[p][1], lambda second: half_row(p, 0, bi, second))[i - 1]()
            both(p, 8 + 4 * i, ORDERS[p][2], r, r)
            to_twin(p, 0, bi)

    meanwhile()

    def sides(p, i):
        bi = NEXT[i]
        for ci, j in ((-1, 0), (1, 1)):
            arrived(row(p, ci, bi), p, 8 + 4 * i + j)
            onward(p, 8 + 4 * i, ORDERS[p][2], lambda second: half_row(p, ci, bi, second))[j]()
            to_twin(p, ci, bi)

    def opposite(p, i):
        bi = NEXT[i]
        arrived(half_row(p, 2, bi, False), p, 8 + 4 * i + 2)
        arrived(half_row(p, 2, bi, True), p, 8 + 4 * i + 3)
        to_twin(p, 2, bi)

    for p in parts:
        sides(p, 0)
    for p in parts:
        arrived(half_row(p, 0, 2, False), p, 6)
        arrived(half_row(p, 0, 2, True), p, 7)
        r = row(p, 0, 2)
        both(p, 8 + 12, ORDERS[p][2], r, r)
        to_twin(p, 0, 2)
    for p in parts:
        sides(p, 1)
        sides(p, 2)
    for p in parts:
        opposite(p, 0)
    early = len(sends)
    for p in parts:
        sides(p, 3)

    def from_twin(p, which):
        _, b, c = spot(p)
        for ci in range(4):
            for bi in range(4):
                if (ci == 2 or bi == 2) == which:
                    arrived(at(p, 1 - core, c + ci, b + bi), p, 24 + 4 * ci + bi)

    for p in parts:
        opposite(p, 1)
        opposite(p, 2)
        from_twin(p, False)
    for copy in sends[:early]:
        copy.wait_send()
    for p in parts:
        opposite(p, 3)
    for p in parts:
        from_twin(p, True)
    return sends[early:]


def normal(values):
    centre = jnp.mean(values, -1, keepdims=True)
    centred = values - centre
    spread = jnp.mean(centred * centred, -1, keepdims=True)
    scale = lax.rsqrt(spread + LAYER_EPS)
    return centred * scale, scale


def by_eights(values):
    return jnp.sum(values.reshape(values.shape[0] // 8, 8, values.shape[1]), 0)


def pass_kernel(
    owner_in, places_in, master_in, vectors_in, patches, keep_in, cotangent, output, input_grad, master, vec_out,
    g, left, right, flats, q, k, v, att, a_low, probs, w_qkv, w_out, wall, sums, vec,
    vectors, keep, owner, places, made, tables, send_sem, recv_sem, held_sem, ready,
):
    tokens, d_mid, d_a, mid = (flats.at[i] for i in range(4))
    loads = [
        pltpu.make_async_copy(src, to, held_sem.at[i])
        for i, (src, to) in enumerate(
            (
                (master_in, master), (vectors_in, vectors), (patches, output), (cotangent, input_grad), (keep_in, keep),
                (owner_in, owner), (places_in, places),
            )
        )
    ]
    for load in loads:
        load.start()

    def block(n):
        return g[pl.ds(tables[lax.div(n, 128), lax.rem(n, 128)], 8)].reshape(SIDE, SIDE)

    def columns(m, j, count):
        rows = (256 if m == 4 else 64 if m < 4 else 256) // WIDTH[m]
        return jnp.concatenate(
            [
                jnp.concatenate([block(FIRST[m] + r * WIDTH[m] + j + i) for i in range(count)], 1)
                for r in range(rows)
            ],
            0,
        )

    def rows_of(m, i, count):
        return jnp.concatenate(
            [
                jnp.concatenate([block(FIRST[m] + (i + r) * WIDTH[m] + c) for c in range(WIDTH[m])], 1)
                for r in range(count)
            ],
            0,
        )

    def lanes(i, width):
        return pl.ds(pl.multiple_of(i * width, width), width)

    def strip(i):
        return pl.ds(pl.multiple_of(i * 32, 32), 32)

    def stack(first, count):
        return jnp.concatenate([right[first + i] for i in range(count)], 1)

    def line(i):
        return vec[i : i + 1, :]

    def add_sums(i, value, where=slice(None)):
        sums[i, :, where] += by_eights(value)

    def first_normal(i):
        n, _ = normal(tokens[strip(i), :])
        d_a[strip(i), :] = n
        cot = d_mid[strip(i), :]
        for c in range(8):
            right[64 + c, strip(i), :] = cot[:, c * 128 : (c + 1) * 128].astype(BF16)
        add_sums(7, cot)

    def make_tables():
        number = owner[...]
        matrix = sum((number >= first).astype(jnp.int32) for first in FIRST[1:])

        def by_matrix(values):
            return sum(jnp.where(matrix == m, value, 0) for m, value in enumerate(values))

        inner = number - by_matrix(FIRST)
        wide_one = matrix == 4
        made[8:14, :] = by_matrix(LEFT_AT) + jnp.where(wide_one, inner >> 5, inner >> 3)
        made[16:22, :] = by_matrix(RIGHT_AT) + jnp.where(wide_one, inner & 31, inner & 7)
        lane = lax.broadcasted_iota(jnp.int32, (128, 128), 1)
        found = [jnp.zeros((8, 128), F32)] * 6
        for i in range(6):
            held_by = jnp.broadcast_to(number[i : i + 1].astype(F32), (128, 128)).T
            lies_at = jnp.broadcast_to(places[i : i + 1, :].astype(F32), (128, 128)).T
            for j in range(6):
                hit = held_by == (lane + 128 * j).astype(F32)
                found[j] = found[j] + by_eights(jnp.where(hit, lies_at, 0.0))
        for j in range(6):
            at = jnp.sum(found[j], 0, keepdims=True).astype(jnp.int32)
            made[j : j + 1, :] = jnp.clip(at, 0, ALL_ROWS - 8)

    def meanwhile():
        for load in loads[5:]:
            load.wait()
        make_tables()
        to_scalars = pltpu.make_async_copy(made, tables, held_sem.at[7])
        to_scalars.start()
        sums[...] = jnp.zeros_like(sums)
        for load in loads[2:5]:
            load.wait()
        for came, to in ((output, tokens), (input_grad, d_mid)):
            to[0:TOKENS, :] = came[...].astype(F32)
            to[TOKENS:ROWS, :] = jnp.zeros((ROWS - TOKENS, D), F32)
        row_at = lax.broadcasted_iota(jnp.int32, (ROWS, ROWS), 0)
        col_at = lax.broadcasted_iota(jnp.int32, (ROWS, ROWS), 1)

        def image(at):
            return sum((at >= PATCHES * (i + 1)).astype(jnp.int32) for i in range(IMAGES))

        spread = (
            lax.broadcasted_iota(jnp.int32, (PATCHES, ROWS), 1)
            - PATCHES * image(lax.broadcasted_iota(jnp.int32, (PATCHES, ROWS), 1))
            == lax.broadcasted_iota(jnp.int32, (PATCHES, ROWS), 0)
        )
        kept = dot(keep[...].astype(F32).astype(BF16), spread.astype(F32).astype(BF16))
        own = lax.broadcasted_iota(jnp.int32, (IMAGES, ROWS), 0) == image(
            lax.broadcasted_iota(jnp.int32, (IMAGES, ROWS), 1)
        )
        dropped = jnp.sum(jnp.where(own & (kept < 0.5), 1.0, 0.0), 0, keepdims=True)
        wall[...] = jnp.where(
            image(row_at) == image(col_at), jnp.broadcast_to(dropped, (ROWS, ROWS)) * MASKED, OUTSIDE
        )
        loop(8, first_normal, 2)
        to_scalars.wait()

    barrier = pltpu.get_barrier_semaphore()
    announce(barrier, neighbours())
    all_announced(barrier, neighbours())
    sends = gather_weights(master, vectors, loads[:2], g, send_sem, recv_sem, meanwhile)

    for w in range(8):
        window = sum(g[int(VECTOR_AT[16 * w + i])].astype(F32) for i in range(16))
        vec[:, w * 128 : (w + 1) * 128] = window

    def first_norm(i):
        a_low[strip(i), :] = (d_a[strip(i), :] * line(0) + line(1)).astype(BF16)

    loop(8, first_norm, 4)

    def project(j):
        left[pl.ds(2 * j, 2)] = a_low[:, lanes(j, 256)].T.reshape(2, 128, ROWS)
        at = lanes(j, 256)
        made = []
        for m in range(3):
            weights = columns(m, 2 * j, 2)
            w_qkv[m, :, at] = weights
            made.append(dot(a_low[...], weights))
        q[:, at] = (made[0] + vec[2:3, at]).astype(BF16)
        k[:, at] = made[1].astype(BF16)
        v[:, at] = (made[2] + vec[3:4, at]).astype(BF16)

    loop(4, project, 4)

    low_half = lax.broadcasted_iota(jnp.int32, (ROWS, 128), 1) < HEAD_DIM

    def split(pair):
        nothing = jnp.zeros_like(pair)
        return jnp.where(low_half, pair, nothing), jnp.where(low_half, nothing, pair)

    def attend(j):
        at = lanes(j, 128)
        kp = k[:, at]
        weights = []
        for h, qh in enumerate(split(q[:, at])):
            raw = dot_nt(qh, kp)
            masked = jnp.where(wall[...] == 0.0, raw * SCALE, wall[...])
            e = jnp.exp(masked - jnp.max(masked, -1, keepdims=True))
            p = e / jnp.sum(e, -1, keepdims=True)
            low = p.astype(BF16)
            probs[2 * j + h] = low
            weights.append(low)
        pair = dot(jnp.concatenate(weights, 1), jnp.concatenate(split(v[:, at]), 0)).astype(BF16)
        att[:, at] = pair
        left[8 + j] = pair.T

    loop(8, attend, 4)

    def to_mid(j):
        at = lanes(j, 256)
        mid[:, at] = tokens[:, at] + (dot(att[...], columns(3, 2 * j, 2)) + vec[4:5, at])

    loop(4, to_mid, 4)

    def second_norm(i):
        n, _ = normal(mid[strip(i), :])
        a_low[strip(i), :] = (n * line(5) + line(6)).astype(BF16)

    loop(8, second_norm, 8)

    def hidden(j):
        pre = dot(a_low[...], columns(4, 2 * j, 2)) + vec[pl.ds(8 + j // 4, 1), lanes(j % 4, 256)]
        half = 0.5 * (1.0 + lax.erf(pre * math.sqrt(0.5)))
        slope = half + pre * (jnp.exp(-0.5 * pre * pre) * (1.0 / math.sqrt(2.0 * math.pi)))
        low = (pre * half).astype(BF16)
        left[pl.ds(24 + 2 * j, 2)] = low.T.reshape(2, 128, ROWS)
        weights = rows_of(5, 2 * j, 2)
        w_out[lanes(j, 256), :] = weights
        d_pre = (dot_nt(stack(64, 8), weights) * slope).astype(BF16)
        right[32 + 2 * j] = d_pre[:, :128]
        right[33 + 2 * j] = d_pre[:, 128:]
        add_sums(8 + j // 4, d_pre.astype(F32), lanes(j % 4, 256))

    loop(16, hidden, 4)

    def second_back(j):
        at = lanes(j, 256)
        left[pl.ds(16 + 2 * j, 2)] = a_low[:, at].T.reshape(2, 128, ROWS)
        d_a[:, at] = dot_nt(stack(32, 32), rows_of(4, 2 * j, 2))

    loop(4, second_back, 4)

    def mid_back(i):
        rows = strip(i)
        n, scale = normal(mid[rows, :])
        d = d_a[rows, :]
        e = d * line(5)
        inner = e - jnp.mean(e, -1, keepdims=True) - n * jnp.mean(e * n, -1, keepdims=True)
        whole = d_mid[rows, :] + inner * scale
        d_mid[rows, :] = whole
        low = whole.astype(BF16)
        for c in range(8):
            right[24 + c, rows, :] = low[:, c * 128 : (c + 1) * 128]
        add_sums(5, d * n)
        add_sums(6, d)
        add_sums(4, low.astype(F32))

    loop(8, mid_back, 8)

    def att_back(j):
        att[:, lanes(j, 256)] = dot_nt(stack(24, 8), rows_of(3, 2 * j, 2)).astype(BF16)

    loop(4, att_back, 4)

    def heads_back(j):
        at = lanes(j, 128)
        vp = v[:, at]
        q_parts, k_parts, da_parts = split(q[:, at]), split(k[:, at]), split(att[:, at])
        d_raws, weights = [], []
        for h in range(2):
            low = probs[2 * j + h]
            p = low.astype(F32)
            d_p = dot_nt(da_parts[h], vp)
            d_m = p * (d_p - jnp.sum(p * d_p, -1, keepdims=True))
            d_raws.append(jnp.where(wall[...] == 0.0, d_m * SCALE, 0.0).astype(BF16))
            weights.append(low)
        d_q = dot(jnp.concatenate(d_raws, 1), jnp.concatenate(k_parts, 0)).astype(BF16)
        d_k = dot_tn(jnp.concatenate(d_raws, 0), jnp.concatenate(q_parts, 0)).astype(BF16)
        d_v = dot_tn(jnp.concatenate(weights, 0), jnp.concatenate(da_parts, 0)).astype(BF16)
        right[j] = d_q
        right[8 + j] = d_k
        right[16 + j] = d_v
        add_sums(2, d_q.astype(F32), at)
        add_sums(3, d_v.astype(F32), at)

    for copy in sends:
        copy.wait_send()
    announce(ready, sum(partners(), []))

    def first_back(j):
        at = lanes(j, 256)
        weights = jnp.concatenate([w_qkv[m, at, :] for m in range(3)], 1)
        d_a[:, at] = dot_nt(stack(0, 24), weights)

    def token_back(i):
        rows = strip(i)
        n, scale = normal(tokens[rows, :])
        d = d_a[rows, :]
        e = d * line(0)
        inner = e - jnp.mean(e, -1, keepdims=True) - n * jnp.mean(e * n, -1, keepdims=True)
        d_mid[rows, :] = d_mid[rows, :] + inner * scale
        add_sums(0, d * n)
        add_sums(1, d)

    def input_side(stage):
        if stage < 2:
            loop(2, lambda i: first_back(2 * stage + i), 2)
        else:
            loop(8, token_back, 8)
            input_grad[...] = d_mid[0:TOKENS, :].astype(BF16)
            folded = jnp.sum(sums[...], 1)
            vec_out[0] = folded[:8]
            vec_out[1, 0 : NV - 8] = folded[8:]
            vec_out[1, NV - 8 :] = jnp.zeros((16 - NV, D), F32)

    def output_side(stage):
        fan = left[24 + 8 * stage : 32 + 8 * stage].reshape(D, ROWS)
        mid[...] += dot_tn(fan, w_out[stage * D : (stage + 1) * D, :])
        if stage == 3:
            output[...] = (mid[...] + vec[7:8, :])[:TOKENS].astype(BF16)

    return heads_back, input_side, output_side


ROUNDS = (
    (2, 2), (2, 1), (1, 2), (3, 2), (2, 3), (1, 1), (3, 1), (0, 2), (2, 0), (1, 3), (3, 3), (0, 1), (1, 0), (3, 0), (0, 3), (0, 0),
)
AHEAD = 1
RING = 2 * AHEAD + 2
OUT_RING = 6
OUT_ROUNDS = tuple(round_ for round_ in ROUNDS if round_[0])


VMEM_LIMIT = 62 * MIB


def in_hbm(array):
    return pltpu.with_memory_space_constraint(array, pltpu.HBM)


class Rows:
    def __init__(self, buffer, first):
        self.buffer, self.first = buffer, first

    def row(self, n):
        return self.buffer.at[pl.ds(64 * (self.first + n), 64)]

    def half(self, n, second):
        return self.buffer.at[pl.ds(64 * (self.first + n) + 32 * second, 32)]

    def get(self, n, ai):
        return self.buffer[pl.ds(64 * (self.first + n) + 16 * ai, 16)].reshape(256, SIDE).astype(F32)

    def put(self, n, ai, value):
        self.buffer[pl.ds(64 * (self.first + n) + 16 * ai, 16)] = value.astype(BF16).reshape(16, 16, SIDE)


def scatter_kernel(
    tables, left, right, vec_in,
    total, window, norm_tile,
    g, kept, a_out, a_in,
    vec_y, vec_y_in, vec_x, vec_x_in, vec_z, vec_z_in, vec_t, tiles,
    tw_send, tw_recv, c_send, c_recv, b_send, b_recv, a_send, a_recv, v_send, v_recv, n_send, n_recv,
    heads_back, between,
):
    pos, core = place()
    twin = device(pos, 1 - core)
    axes = [[device(moved(pos, a, s), core) for s in (1, 2, 3)] for a in range(3)]
    plane, column = partners()
    sizes, at = (3 * RING, 3 * RING, 3 * OUT_RING, 24, 12, 9, 6, 3), 0
    places = []
    for size in sizes:
        places.append(Rows(g, at))
        at += size
    tw_out, tw_in, c_out, c_in, c_half, b_out, b_in, b_half = places

    def out_row(p, round_):
        return 3 * (OUT_ROUNDS.index(round_) % OUT_RING) + p

    def pick(options, i):
        value = options[-1]
        for n in range(len(options) - 2, -1, -1):
            value = jnp.where(i == n, options[n], value)
        return value

    def axis_of(p, which):
        return lax.rem(p + which, 3)

    def neighbour(p, which, by):
        axis = axis_of(p, which)
        return tuple(pick([axes[a][by - 1][n] for a in range(3)], axis) for n in range(2))

    adds = (lambda x: 16 * lax.div(x, 2) + 4 * lax.rem(x, 2), lambda y: 32 * y, lambda z: z)
    share = [
        [[adds[axis](lax.rem(pos[axis] + by, 4)) for by in range(4)] for axis in ORDERS[p]] for p in range(3)
    ]

    def row_pairs(k, p, of_core):
        ci, bi = ROUNDS[k]
        base = pick([share[i][2][ci] + share[i][1][bi] for i in range(3)], p) + 8 * of_core
        pairs = []
        for ai in range(4):
            slot = (base + pick([share[i][0][ai] for i in range(3)], p)) * 6 + 2 * p
            made = []
            for i in range(2):
                row, lane = lax.div(slot + i, 128), lax.rem(slot + i, 128)
                made.append(dot(left[tables[8 + row, lane]], right[tables[16 + row, lane]]))
            pairs.append(jnp.concatenate(made, 0))
        return pairs

    def remote(src, dst, send_sem, recv_sem, to):
        return pltpu.make_async_remote_copy(
            src_ref=src, dst_ref=dst, send_sem=send_sem, recv_sem=recv_sem, device_id=to, device_id_type=MESH
        )

    def twin_copy(k, p):
        n = 3 * (k % RING) + p
        return remote(tw_out.row(n), tw_in.row(n), tw_send.at[3 * k + p], tw_recv.at[3 * k + p], twin)

    def for_twin(k, p, pairs=None):
        if k >= len(ROUNDS):
            return
        if k >= RING:
            twin_copy(k - RING, p).wait_send()
        for ai, value in enumerate(pairs or row_pairs(k, p, 1 - core)):
            tw_out.put(3 * (k % RING) + p, ai, value)
        twin_copy(k, p).start()

    def chip_sum(k, p, ai, pairs):
        return pairs[ai] + tw_in.get(3 * (k % RING) + p, ai)

    def c_half_copy(p, bi, second):
        n = p * 4 + bi
        return remote(
            c_out.half(out_row(p, (2, bi)), second), c_half.half(n, second), c_send.at[2 * n + second], c_recv.at[2 * n + second],
            neighbour(p, 2, 3 if second else 1),
        )

    def c_whole_copy(p, bi, leftward):
        n = 12 * leftward + p * 4 + bi
        return remote(
            c_out.row(out_row(p, (1 + 2 * leftward, bi))), c_in.row(n), c_send.at[24 + n], c_recv.at[24 + n], neighbour(p, 2, 3 if leftward else 1)
        )

    def free_out(p, round_):
        before = OUT_ROUNDS.index(round_) - OUT_RING
        if before >= 0:
            left_out(p, OUT_ROUNDS[before])

    def left_out(p, round_):
        ci, bi = round_
        if ci == 2:
            c_half_copy(p, bi, 0).wait_send()
            c_half_copy(p, bi, 1).wait_send()
        else:
            c_whole_copy(p, bi, ci // 2).wait_send()

    def b_half_copy(p, second):
        return remote(
            b_out.half(3 * p, second), b_half.half(p, second), b_send.at[4 * p + second], b_recv.at[4 * p + second],
            neighbour(p, 1, 3 if second else 1),
        )

    def b_whole_copy(p, leftward):
        return remote(
            b_out.row(3 * p + 1 + leftward), b_in.row(2 * p + leftward), b_send.at[4 * p + 2 + leftward],
            b_recv.at[4 * p + 2 + leftward], neighbour(p, 1, 3 if leftward else 1),
        )

    def a_copy(p, by):
        n = 3 * p + by - 1
        return remote(a_out.at[n], a_in.at[n], a_send.at[n], a_recv.at[n], neighbour(p, 0, by))

    def opposite_row(k, p, pairs):
        _, bi = ROUNDS[k]
        free_out(p, ROUNDS[k])
        for ai in range(4):
            c_out.put(out_row(p, ROUNDS[k]), ai, chip_sum(k, p, ai, pairs))
            if ai % 2:
                c_half_copy(p, bi, ai // 2).start()

    def side_row(k, p, pairs):
        ci, bi = ROUNDS[k]
        leftward = ci // 2
        n = p * 4 + bi
        c_half_copy(p, bi, leftward).wait_recv()
        free_out(p, ROUNDS[k])
        for ai in range(4):
            value = chip_sum(k, p, ai, pairs)
            if ai // 2 == leftward:
                value = value + c_half.get(n, ai)
            c_out.put(out_row(p, ROUNDS[k]), ai, value)
        c_whole_copy(p, bi, leftward).start()

    def own_row(k, p, pairs):
        _, bi = ROUNDS[k]
        n = p * 4 + bi
        leftward = bi // 2
        c_whole_copy(p, bi, 0).wait_recv()
        c_whole_copy(p, bi, 1).wait_recv()
        if bi % 2:
            b_half_copy(p, leftward).wait_recv()
        for ai in range(4):
            value = chip_sum(k, p, ai, pairs) + c_in.get(n, ai) + c_in.get(12 + n, ai)
            if bi == 0:
                kept[p, :, ai * 128 : (ai + 1) * 128] = value
                continue
            if bi % 2 and ai // 2 == leftward:
                value = value + b_half.get(p, ai)
            b_out.put(3 * p + (0 if bi == 2 else 1 + leftward), ai, value)
            if bi == 2 and ai % 2:
                b_half_copy(p, ai // 2).start()
        if bi % 2:
            b_whole_copy(p, leftward).start()

    def vec_twin():
        return remote(vec_in.at[1 - core], vec_t.at[0], v_send.at[0], v_recv.at[0], twin)

    def vec_copy(axis, by):
        src, dst = ((vec_x, vec_x_in), (vec_y, vec_y_in), (vec_z, vec_z_in))[axis]
        n = 1 + 3 * axis + by - 1
        there = lax.rem(pos[axis] + by, 4)
        piece = src.at[there] if axis == 1 else src.at[there // 2] if axis == 0 else src
        return remote(piece, dst.at[by - 1], v_send.at[n], v_recv.at[n], axes[axis][by - 1])

    def vec_start(axis):
        for by in (1, 2, 3):
            vec_copy(axis, by).start()

    def vec_sum(axis, whole):
        dst = (vec_x_in, vec_y_in, vec_z_in)[axis]
        for by in (1, 2, 3):
            vec_copy(axis, by).wait_recv()
            whole = whole + dst[by - 1]
        return whole

    def vec_last():
        return remote(window.at[core], window.at[core], v_send.at[10], v_recv.at[10], twin)

    def vec_stage(stage):
        if stage < 0:
            vec_twin().start()
        elif stage == 0:
            vec_twin().wait_recv()
            whole = vec_in[core] + vec_t[0]
            for i in range(4):
                vec_y[i] = whole[:, 256 * i : 256 * i + 256]
            vec_start(1)
        elif stage == 1:
            whole = vec_sum(1, vec_y[pos[1]])
            for i in range(2):
                vec_x[i] = whole[:, 128 * i : 128 * i + 128]
            vec_start(0)
        elif stage == 2:
            vec_z[...] = vec_sum(0, vec_x[pos[0] // 2])
            vec_start(2)
        elif stage == 3:
            window[core] = vec_sum(2, vec_z[...])
            vec_last().start()

    def one_row(k, p, pairs=None):
        pairs = pairs or row_pairs(k, p, core)
        twin_copy(k, p).wait_recv()
        ci = ROUNDS[k][0]
        (own_row if ci == 0 else opposite_row if ci == 2 else side_row)(k, p, pairs)

    x_low = lax.rem(pos[0], 2)

    def class_at(i):
        mine = jnp.where((i == 0) | ((i >= 2) & (i < 5)), x_low, 1 - x_low)
        step = pick([2, 2, 0, 1, 3, 1, 0, 3], i)
        return mine * 4 + lax.rem(pos[2] + step, 4)

    def classes_back(first, count):
        loop(count, lambda i: heads_back(class_at(first + i)), count)

    classes_back(0, 2)
    between(-1, vec_stage)
    loop(2, lambda p: for_twin(0, p))
    classes_back(2, 3)
    for_twin(0, jnp.int32(2))
    loop(2, lambda p: one_row(0, p))
    classes_back(5, 3)
    loop(2, lambda p: for_twin(1, p))
    one_row(0, jnp.int32(2))
    for_twin(1, jnp.int32(2))
    for k in range(1, len(ROUNDS)):

        def one_round(p):
            ahead = row_pairs(k + AHEAD, p, 1 - core) if k + AHEAD < len(ROUNDS) else None
            pairs = row_pairs(k, p, core)
            for_twin(k + AHEAD, p, ahead)
            one_row(k, p, pairs)

        between(k, vec_stage)
        loop(3, one_round)

    def row_sum(p, ai):
        return kept[p, :, ai * 128 : (ai + 1) * 128] + b_in.get(2 * p, ai) + b_in.get(2 * p + 1, ai)

    def last_axis(p):
        b_whole_copy(p, 0).wait_recv()
        b_whole_copy(p, 1).wait_recv()
        for by in (2, 1, 3):
            a_out[3 * p + by - 1] = row_sum(p, by).astype(BF16)
            a_copy(p, by).start()

    loop(3, last_axis)

    wide, narrow = lax.axis_index("wide"), lax.axis_index("narrow")
    remote(window.at[1 - core], window.at[1 - core], v_send.at[10], v_recv.at[10], twin).wait_recv()
    lane = lax.broadcasted_iota(jnp.int32, (8, 128), 1) // 8
    own_lanes = lane == lax.rem(wide, 2) * 8 + narrow
    squares = jnp.zeros((8, 128), F32)
    for i in range(2):
        own = jnp.where(own_lanes, window[i], 0.0)
        squares = squares + own * own

    for p in range(3):
        value = row_sum(p, 0)
        for by in (1, 3, 2):
            a_copy(p, by).wait_recv()
            value = value + a_in[3 * p + by - 1].astype(F32)
        total[2 * p] = value[:128]
        total[2 * p + 1] = value[128:]
        squares = squares + by_eights(value * value)

    def norm_copy(stage, i):
        n = 15 * stage + i
        to = (column if stage else plane)[i]
        return remote(tiles.at[stage], tiles.at[2 + n], n_send.at[n], n_recv.at[n], to)

    def sent(p):
        for k in range(len(ROUNDS) - RING, len(ROUNDS)):
            twin_copy(k, p).wait_send()
        for round_ in OUT_ROUNDS[-OUT_RING:]:
            left_out(p, round_)
        for side in (0, 1):
            b_half_copy(p, side).wait_send()
            b_whole_copy(p, side).wait_send()
        for by in (1, 2, 3):
            a_copy(p, by).wait_send()

    def all_sent():
        loop(3, sent)
        vec_twin().wait_send()
        vec_last().wait_send()
        for axis in range(3):
            for by in (1, 2, 3):
                vec_copy(axis, by).wait_send()

    whole = squares
    for stage, count in ((0, 15), (1, 7)):
        tiles[stage] = whole
        for i in range(count):
            norm_copy(stage, i).start()
        if stage == 0:
            all_sent()
        for i in range(count):
            norm_copy(stage, i).wait_recv()
            whole = whole + tiles[2 + 15 * stage + i]
    norm_tile[...] = whole
    for stage, count in ((0, 15), (1, 7)):
        for i in range(count):
            norm_copy(stage, i).wait_send()


def whole_kernel(
    owner, places, master_in, vectors_in, patches, keep_in, cotangent,
    output, input_grad, total, window, norm_tile, *scratch,
):
    gathered, scattered = scratch[:PASS_SCRATCH], scratch[PASS_SCRATCH:]
    g, left, right, flats = gathered[:4]
    vec_in, *scattered = scattered
    ready = gathered[-1]
    heads_back, input_side, output_side = pass_kernel(
        owner, places, master_in, vectors_in, patches, keep_in, cotangent, output, input_grad, total, vec_in, *gathered
    )

    def between(k, vec_stage):
        if k < 0:
            all_announced(ready, sum(partners(), []))
        elif 1 <= k <= 3:
            input_side(k - 1)
            if k == 3:
                vec_stage(-1)
        elif 4 <= k <= 7:
            output_side(k - 4)
        if k in (5, 7, 9, 11):
            vec_stage((k - 5) // 2)

    scatter_kernel(
        gathered[TABLES], left, right, vec_in, total, window, norm_tile, g, flats, *scattered, heads_back, between
    )


PASS_SCRATCH, TABLES = 25, 20


def forward_backward(*operands):
    vmem = pl.BlockSpec(memory_space=pltpu.VMEM)
    flat = (ROWS, D)
    dma = pltpu.SemaphoreType.DMA
    pass_scratch = [
        pltpu.VMEM((ALL_ROWS, 16, 128), BF16),
        pltpu.VMEM((56, 128, ROWS), BF16),
        pltpu.VMEM((72, ROWS, 128), BF16),
        pltpu.VMEM((4, *flat), F32),
        *[pltpu.VMEM(flat, BF16)] * 5,
        pltpu.VMEM((HEADS, ROWS, ROWS), BF16),
        pltpu.VMEM((3, D, D), BF16),
        pltpu.VMEM((FF, D), BF16),
        pltpu.VMEM((ROWS, ROWS), F32),
        pltpu.VMEM((NV, 8, D), F32),
        pltpu.VMEM((16, D), F32),
        pltpu.VMEM((8, NV), F32),
        pltpu.VMEM((IMAGES, PATCHES), jnp.int32),
        pltpu.VMEM((6, 128), jnp.int32),
        pltpu.VMEM((6, 128), jnp.int32),
        pltpu.VMEM((24, 128), jnp.int32),
        pltpu.SMEM((24, 128), jnp.int32),
        dma((3, 40)),
        dma((3, 40)),
        dma((8,)),
        pltpu.SemaphoreType.REGULAR,
    ]
    assert len(pass_scratch) == PASS_SCRATCH
    return pl.pallas_call(
        whole_kernel,
        out_shape=[
            jax.ShapeDtypeStruct((TOKENS, D), BF16),
            jax.ShapeDtypeStruct((TOKENS, D), BF16),
            jax.ShapeDtypeStruct((6, SIDE, SIDE), F32),
            jax.ShapeDtypeStruct((2, 8, 128), F32),
            jax.ShapeDtypeStruct((8, 128), F32),
        ],
        in_specs=[pl.BlockSpec(memory_space=pltpu.HBM)] * 7,
        out_specs=[vmem] * 5,
        scratch_shapes=pass_scratch
        + [
            pltpu.VMEM((2, 8, D), F32),
            pltpu.VMEM((9, 256, 128), BF16),
            pltpu.VMEM((9, 256, 128), BF16),
            pltpu.VMEM((4, 8, 256), F32),
            pltpu.VMEM((3, 8, 256), F32),
            pltpu.VMEM((2, 8, 128), F32),
            pltpu.VMEM((3, 8, 128), F32),
            pltpu.VMEM((8, 128), F32),
            pltpu.VMEM((3, 8, 128), F32),
            pltpu.VMEM((1, 8, D), F32),
            pltpu.VMEM((24, 8, 128), F32),
            dma((48,)), dma((48,)), dma((48,)), dma((48,)), dma((12,)), dma((12,)), dma((9,)), dma((9,)),
            dma((11,)), dma((11,)), dma((22,)), dma((22,)),
        ],
        compiler_params=pltpu.CompilerParams(
            collective_id=0, has_side_effects=True, vmem_limit_bytes=VMEM_LIMIT
        ),
        cost_estimate=pl.CostEstimate(
            flops=19_000_000_000, bytes_accessed=10_000_000, transcendentals=3_000_000
        ),
        name="forward_backward",
    )(*(in_hbm(operand) for operand in operands))


def rounded_dot(left, right, over):
    return lax.dot_general(
        left.astype(BF16), right.astype(BF16), (over, ((), ())), preferred_element_type=F32
    )


def step_kernel(
    raw, window, norm_tile, shift, master, left_stats, right_stats, left_root, right_root, vectors, vec_accum,
    output_in, input_grad_in,
    block_grads, new_left, new_right, new_master, new_copy, vec_grads, vec_accum_new, vec_new, grad_norm,
    output, input_grad, passing, sem,
):
    def copies(way):
        ends = ((output_in, output), (input_grad_in, input_grad))
        return [
            pltpu.make_async_copy(
                passing.at[i] if way else pair[0], pair[1] if way else passing.at[i], sem.at[2 * way + i]
            )
            for i, pair in enumerate(ends)
        ]

    norm = jnp.sqrt(jnp.sum(norm_tile[...], keepdims=True))
    clip = 1.0 / jnp.maximum(norm, 1.0)

    @pl.when(pl.program_id(0) == 0)
    def _():
        for copy in copies(0):
            copy.start()
        grad_norm[...] = norm
        lanes = pltpu.roll(window[...].reshape(16, 128), shift[0], 1)
        grads = clip * lanes.T[:8, :NV]
        vec_grads[...] = grads
        accum = 0.5 * vec_accum[...] + 0.5 * grads * grads
        vec_accum_new[...] = accum
        vec_new[...] = vectors[...] - 0.5 * grads / (jnp.sqrt(accum) + 1e-08)

    for i in range(raw.shape[0]):
        grads = raw[i] * clip
        block_grads[i] = grads
        new_left[i] = 0.5 * left_stats[i] + 0.5 * rounded_dot(grads, grads, ((1,), (1,)))
        new_right[i] = 0.5 * right_stats[i] + 0.5 * rounded_dot(grads, grads, ((0,), (0,)))
        way = rounded_dot(rounded_dot(left_root[i], grads, ((1,), (0,))), right_root[i], ((1,), (0,)))
        master_now = master[i] - 0.5 * way
        new_master[i] = master_now
        new_copy[i] = master_now.astype(BF16)

    @pl.when(pl.program_id(0) == 0)
    def _():
        for came, copy in zip(copies(0), copies(1)):
            came.wait()
            copy.start()

    @pl.when(pl.program_id(0) == pl.num_programs(0) - 1)
    def _():
        for copy in copies(1):
            copy.wait()


def update(raw, window, norm_tile, shift, blocks_in, vectors, vec_accum, output, input_grad):
    per = 3
    blocks = pl.BlockSpec((per, SIDE, SIDE), lambda i: (i, 0, 0))
    anywhere = pl.BlockSpec(memory_space=pltpu.HBM)

    def whole(*shape):
        return pl.BlockSpec(shape, lambda i: (0,) * len(shape))

    f32_blocks = jax.ShapeDtypeStruct((6, SIDE, SIDE), F32)
    f32_vecs = jax.ShapeDtypeStruct((8, NV), F32)
    tokens = jax.ShapeDtypeStruct((TOKENS, D), BF16)
    return pl.pallas_call(
        step_kernel,
        grid=(6 // per,),
        out_shape=[f32_blocks] * 4
        + [jax.ShapeDtypeStruct((6, SIDE, SIDE), BF16)]
        + [f32_vecs] * 3
        + [jax.ShapeDtypeStruct((1, 1), F32)]
        + [tokens] * 2,
        in_specs=[blocks, whole(2, 8, 128), whole(8, 128), pl.BlockSpec(memory_space=pltpu.SMEM)]
        + [blocks] * 5
        + [whole(8, NV)] * 2
        + [anywhere] * 2,
        out_specs=[blocks] * 5 + [whole(8, NV)] * 3 + [whole(1, 1)] + [anywhere] * 2,
        scratch_shapes=[pltpu.VMEM((2, TOKENS, D), BF16), pltpu.SemaphoreType.DMA((4,))],
        compiler_params=pltpu.CompilerParams(vmem_limit_bytes=32 * MIB),
        name="update",
    )(*(in_hbm(a) for a in (raw, window, norm_tile)), shift, *blocks_in, in_hbm(vectors), in_hbm(vec_accum), in_hbm(output), in_hbm(input_grad))


def body(
    patches, keep, cotangent, owner_table, master, left_stats, right_stats, left_root, right_root, vectors, vec_accum,
):
    wide, narrow = lax.axis_index("wide"), lax.axis_index("narrow")
    output, input_grad, raw, window, norm_tile = forward_backward(
        owner_table.reshape(6, 128), jnp.asarray(BLOCK_AT.reshape(6, 128)), master, vectors.T, patches, keep, cotangent
    )
    lane = ((wide % 2) * 8 + narrow) * 8
    shift = jnp.reshape((128 - lane) % 128, (1,)).astype(jnp.int32)
    blocks_in = (master, left_stats, right_stats, left_root, right_root)
    *of_blocks, vec_grads, vec_accum_new, vec_new, grad_norm, output, input_grad = update(
        raw, window, norm_tile, shift, blocks_in, vectors.T, vec_accum.T, output, input_grad
    )
    return (output, input_grad, *of_blocks, vec_grads.T, vec_accum_new.T, vec_new.T, grad_norm.reshape(()))


def solution(mesh):
    rows, blocks, vecs = P(BOTH, None), P(BOTH, None, None), P(None, BOTH)
    return jax.shard_map(
        body,
        mesh=mesh,
        in_specs=(rows, rows, rows, P(), blocks, blocks, blocks, blocks, blocks, vecs, vecs),
        out_specs=(rows, rows, blocks, blocks, blocks, blocks, blocks, vecs, vecs, vecs, P()),
        check_vma=False,
    )
```

```python
import functools
import math

import jax
import jax.numpy as jnp
import numpy as np
from jax import lax
from jax.experimental import pallas as pl
from jax.experimental.pallas import tpu as pltpu
from jax.sharding import PartitionSpec as P

MESH = pl.DeviceIdType.MESH
BOTH = ("wide", "narrow")
F32, BF16 = jnp.float32, jnp.bfloat16
MIB = 2**20

D = 1024
FF = 4096
HEADS = 16
HEAD_DIM = 64
PATCHES = 49
IMAGES = 5
TOKENS = IMAGES * PATCHES
ROWS = 256
SIDE = 128
NBLK = 768
NV = 12
LAYER_EPS = 1e-05
MASKED = -1000000000.0
OUTSIDE = -3.0e38
SCALE = HEAD_DIM**-0.5

ORDERS = ((0, 1, 2), (1, 2, 0), (2, 0, 1))
SHARE = (16, 16, 17)
PART_FROM = (0, 128 * 16, 128 * 32)
ALL_ROWS = 128 * 49
NEXT = (0, 3, 1, 2)

FIRST = (0, 64, 128, 192, 256, 512)
WIDTH = (8, 8, 8, 8, 32, 8)
LEFT_AT = (0, 0, 0, 8, 16, 24)
RIGHT_AT = (0, 8, 16, 24, 32, 64)


def slot_places():
    block_at, vector_at = np.zeros(NBLK, np.int32), np.zeros(128, np.int32)
    for dev in range(128):
        wide, narrow = dev // 8, dev % 8
        core = wide % 2
        pos = (wide // 2 % 2 * 2 + narrow // 4, wide // 4, narrow % 4)
        for p, (a, b, c) in enumerate(ORDERS):
            at = PART_FROM[p] + (((core * 4 + pos[c]) * 4 + pos[b]) * 4 + pos[a]) * SHARE[p]
            block_at[dev * 6 + 2 * p] = at
            block_at[dev * 6 + 2 * p + 1] = at + 8
            if p == 2:
                vector_at[dev] = at + 16
    return block_at, vector_at


BLOCK_AT, VECTOR_AT = slot_places()


def place():
    wide, narrow = lax.axis_index("wide"), lax.axis_index("narrow")
    x = (wide // 2) % 2 * 2 + narrow // 4
    return (x, wide // 4, narrow % 4), wide % 2


def device(pos, core):
    x, y, z = pos
    return ((y * 2 + x // 2) * 2 + core, x % 2 * 4 + z)


def moved(pos, axis, by):
    return tuple((c + by) % 4 if a == axis else c for a, c in enumerate(pos))


def partners():
    pos, core = place()
    plane = [device(moved(moved(pos, 0, i), 1, j), core) for i in range(4) for j in range(4) if i or j]
    column = [
        device(moved(pos, 2, i), core if j == 0 else 1 - core) for j in range(2) for i in range(4) if i or j
    ]
    return plane, column


def neighbours():
    pos, core = place()
    return [device(pos, 1 - core)] + [device(moved(pos, a, s), core) for a in range(3) for s in (1, -1)]


def others():
    pos, core = place()
    plane = [(i, j, 0, 0) for i in range(4) for j in range(4) if i or j]
    column = [(0, 0, i, j) for j in range(2) for i in range(4) if i or j]
    near = [(1, 0, 0, 0), (3, 0, 0, 0), (0, 1, 0, 0), (0, 3, 0, 0), (0, 0, 1, 0), (0, 0, 3, 0), (0, 0, 0, 1)]
    return [
        device(tuple((c + by) % 4 for c, by in zip(pos, steps)), core if turn == 0 else 1 - core)
        for *steps, turn in plane + column
        if (*steps, turn) not in near
    ]


def announce(semaphore, partners):
    for partner in partners:
        pl.semaphore_signal(semaphore, inc=1, device_id=partner, device_id_type=MESH)


def all_announced(semaphore, partners):
    pl.semaphore_wait(semaphore, len(partners))


def loop(count, body, together=1):
    lax.fori_loop(0, count, lambda i, _: (body(i), None)[1], None, unroll=together)


def dot(left, right):
    return jnp.dot(left, right, preferred_element_type=F32)


def dot_nt(left, right):
    return lax.dot_general(left, right, (((1,), (1,)), ((), ())), preferred_element_type=F32)


def dot_tn(left, right):
    return lax.dot_general(left, right, (((0,), (0,)), ((), ())), preferred_element_type=F32)


def gather_weights(master, vectors, loads, g, send_sem, recv_sem, meanwhile):
    pos, core = place()
    twin = device(pos, 1 - core)
    near = {(a, s): device(moved(pos, a, s), core) for a in range(3) for s in (1, -1)}

    for load in loads:
        load.wait()

    for p in range(3):
        a, b, c = (pos[axis] for axis in ORDERS[p])
        start = PART_FROM[p] + (((core * 4 + c) * 4 + b) * 4 + a) * SHARE[p]
        g[pl.ds(start, 16)] = master[2 * p : 2 * p + 2].astype(BF16).reshape(16, 16, SIDE)
        if p == 2:
            wide, narrow = lax.axis_index("wide"), lax.axis_index("narrow")
            first_lane = (lax.rem(wide, 2) * 8 + narrow) * 8
            spread = lax.broadcasted_iota(jnp.int32, (8, 128), 1) == (
                lax.broadcasted_iota(jnp.int32, (8, 128), 0) + first_lane
            )
            tile = dot_tn(vectors[...].astype(BF16), spread.astype(BF16)).astype(BF16)
            g[start + 16] = jnp.concatenate([tile, jnp.zeros((16 - NV, 128), BF16)], 0)

    sends = []

    def copy_of(src, dst, p, slot, to):
        return pltpu.make_async_remote_copy(
            src_ref=src, dst_ref=dst, send_sem=send_sem.at[p, slot],
            recv_sem=recv_sem.at[p, slot], device_id=to, device_id_type=MESH,
        )

    def send(src, dst, p, slot, to):
        copy = copy_of(src, dst, p, slot, to)
        copy.start()
        sends.append(copy)

    def arrived(dst, p, slot):
        copy_of(dst, dst, p, slot, twin).wait_recv()

    def at(p, of_core, c, b, a=0, count=4, skip=0, rows=None):
        start = PART_FROM[p] + (((of_core * 4 + c % 4) * 4 + b % 4) * 4 + a % 4) * SHARE[p] + skip
        return g.at[pl.ds(start, count * SHARE[p] if rows is None else rows)]

    def spot(p):
        a, b, c = ORDERS[p]
        return pos[a], pos[b], pos[c]

    def row(p, ci, bi):
        _, b, c = spot(p)
        return at(p, core, c + ci, b + bi)

    def half_row(p, ci, bi, second):
        _, b, c = spot(p)
        return at(p, core, c + ci, b + bi, 2 if second else 0, 2)

    def chunk(p, ai):
        a, b, c = spot(p)
        return at(p, core, c, b, a + ai, 1)

    def half_chunk(p, ai, second):
        a, b, c = spot(p)
        return at(p, core, c, b, a + ai, 1, 8 if second else 0, SHARE[p] - 8 if second else 8)

    def to_twin(p, ci, bi):
        r = row(p, ci, bi)
        send(r, r, p, 24 + 4 * (ci % 4) + bi % 4, twin)

    def onward(p, base, axis, half):
        first, second = half(False), half(True)
        return (
            lambda: send(first, first, p, base + 2, near[axis, 1]),
            lambda: send(second, second, p, base + 3, near[axis, -1]),
        )

    def both(p, base, axis, src, dst):
        send(src, dst, p, base, near[axis, 1])
        send(src, dst, p, base + 1, near[axis, -1])

    parts = range(3)
    for p in parts:
        both(p, 0, ORDERS[p][0], chunk(p, 0), chunk(p, 0))
    for p in parts:
        axis = ORDERS[p][0]
        arrived(chunk(p, -1), p, 0)
        onward(p, 0, axis, lambda second: half_chunk(p, -1, second))[0]()
        arrived(chunk(p, 1), p, 1)
        onward(p, 0, axis, lambda second: half_chunk(p, 1, second))[1]()
    for p in parts:
        arrived(half_chunk(p, 2, False), p, 2)
        arrived(half_chunk(p, 2, True), p, 3)
        r = row(p, 0, 0)
        both(p, 4, ORDERS[p][1], r, r)
        both(p, 8, ORDERS[p][2], r, r)
        to_twin(p, 0, 0)
    for p in parts:
        for bi, i in ((-1, 1), (1, 2)):
            r = row(p, 0, bi)
            arrived(r, p, 4 + (i - 1))
            onward(p, 4, ORDERS[p][1], lambda second: half_row(p, 0, bi, second))[i - 1]()
            both(p, 8 + 4 * i, ORDERS[p][2], r, r)
            to_twin(p, 0, bi)

    meanwhile()

    def sides(p, i):
        bi = NEXT[i]
        for ci, j in ((-1, 0), (1, 1)):
            arrived(row(p, ci, bi), p, 8 + 4 * i + j)
            onward(p, 8 + 4 * i, ORDERS[p][2], lambda second: half_row(p, ci, bi, second))[j]()
            to_twin(p, ci, bi)

    def opposite(p, i):
        bi = NEXT[i]
        arrived(half_row(p, 2, bi, False), p, 8 + 4 * i + 2)
        arrived(half_row(p, 2, bi, True), p, 8 + 4 * i + 3)
        to_twin(p, 2, bi)

    for p in parts:
        sides(p, 0)
    for p in parts:
        arrived(half_row(p, 0, 2, False), p, 6)
        arrived(half_row(p, 0, 2, True), p, 7)
        r = row(p, 0, 2)
        both(p, 8 + 12, ORDERS[p][2], r, r)
        to_twin(p, 0, 2)
    for p in parts:
        sides(p, 1)
        sides(p, 2)
    for p in parts:
        opposite(p, 0)
    early = len(sends)
    for p in parts:
        sides(p, 3)

    def from_twin(p, which):
        _, b, c = spot(p)
        for ci in range(4):
            for bi in range(4):
                if (ci == 2 or bi == 2) == which:
                    arrived(at(p, 1 - core, c + ci, b + bi), p, 24 + 4 * ci + bi)

    for p in parts:
        opposite(p, 1)
        opposite(p, 2)
        from_twin(p, False)
    for copy in sends[:early]:
        copy.wait_send()
    for p in parts:
        opposite(p, 3)
    for p in parts:
        from_twin(p, True)
    return sends[early:]


def normal(values):
    centre = jnp.mean(values, -1, keepdims=True)
    centred = values - centre
    spread = jnp.mean(centred * centred, -1, keepdims=True)
    scale = lax.rsqrt(spread + LAYER_EPS)
    return centred * scale, scale


def by_eights(values):
    return jnp.sum(values.reshape(values.shape[0] // 8, 8, values.shape[1]), 0)


def pass_kernel(
    owner_in, places_in, master_in, vectors_in, patches, keep_in, cotangent, output, input_grad, master, vec_out,
    g, left, right, flats, q, k, v, att, a_low, probs, w_qkv, w_out, wall, sums, vec,
    vectors, keep, owner, places, made, tables, send_sem, recv_sem, held_sem, ready, ready_too,
):
    tokens, d_mid, d_a, mid = (flats.at[i] for i in range(4))
    loads = [
        pltpu.make_async_copy(src, to, held_sem.at[i])
        for i, (src, to) in enumerate(
            (
                (master_in, master), (vectors_in, vectors), (patches, output), (cotangent, input_grad), (keep_in, keep),
                (owner_in, owner), (places_in, places),
            )
        )
    ]
    for load in loads:
        load.start()

    def block(n):
        return g[pl.ds(tables[lax.div(n, 128), lax.rem(n, 128)], 8)].reshape(SIDE, SIDE)

    def columns(m, j, count):
        rows = (256 if m == 4 else 64 if m < 4 else 256) // WIDTH[m]
        return jnp.concatenate(
            [
                jnp.concatenate([block(FIRST[m] + r * WIDTH[m] + j + i) for i in range(count)], 1)
                for r in range(rows)
            ],
            0,
        )

    def rows_of(m, i, count):
        return jnp.concatenate(
            [
                jnp.concatenate([block(FIRST[m] + (i + r) * WIDTH[m] + c) for c in range(WIDTH[m])], 1)
                for r in range(count)
            ],
            0,
        )

    def lanes(i, width):
        return pl.ds(pl.multiple_of(i * width, width), width)

    def strip(i):
        return pl.ds(pl.multiple_of(i * 32, 32), 32)

    def stack(first, count):
        return jnp.concatenate([right[first + i] for i in range(count)], 1)

    def line(i):
        return vec[i : i + 1, :]

    def add_sums(i, value, where=slice(None)):
        sums[i, :, where] += by_eights(value)

    def first_normal(i):
        n, _ = normal(tokens[strip(i), :])
        d_a[strip(i), :] = n
        cot = d_mid[strip(i), :]
        for c in range(8):
            right[64 + c, strip(i), :] = cot[:, c * 128 : (c + 1) * 128].astype(BF16)
        add_sums(7, cot)

    def make_tables():
        number = owner[...]
        matrix = sum((number >= first).astype(jnp.int32) for first in FIRST[1:])

        def by_matrix(values):
            return sum(jnp.where(matrix == m, value, 0) for m, value in enumerate(values))

        inner = number - by_matrix(FIRST)
        wide_one = matrix == 4
        made[8:14, :] = by_matrix(LEFT_AT) + jnp.where(wide_one, inner >> 5, inner >> 3)
        made[16:22, :] = by_matrix(RIGHT_AT) + jnp.where(wide_one, inner & 31, inner & 7)
        lane = lax.broadcasted_iota(jnp.int32, (128, 128), 1)
        found = [jnp.zeros((8, 128), F32)] * 6
        for i in range(6):
            held_by = jnp.broadcast_to(number[i : i + 1].astype(F32), (128, 128)).T
            lies_at = jnp.broadcast_to(places[i : i + 1, :].astype(F32), (128, 128)).T
            for j in range(6):
                hit = held_by == (lane + 128 * j).astype(F32)
                found[j] = found[j] + by_eights(jnp.where(hit, lies_at, 0.0))
        for j in range(6):
            at = jnp.sum(found[j], 0, keepdims=True).astype(jnp.int32)
            made[j : j + 1, :] = jnp.clip(at, 0, ALL_ROWS - 8)

    def meanwhile():
        for load in loads[5:]:
            load.wait()
        make_tables()
        to_scalars = pltpu.make_async_copy(made, tables, held_sem.at[7])
        to_scalars.start()
        sums[...] = jnp.zeros_like(sums)
        for load in loads[2:5]:
            load.wait()
        for came, to in ((output, tokens), (input_grad, d_mid)):
            to[0:TOKENS, :] = came[...].astype(F32)
            to[TOKENS:ROWS, :] = jnp.zeros((ROWS - TOKENS, D), F32)
        row_at = lax.broadcasted_iota(jnp.int32, (ROWS, ROWS), 0)
        col_at = lax.broadcasted_iota(jnp.int32, (ROWS, ROWS), 1)

        def image(at):
            return sum((at >= PATCHES * (i + 1)).astype(jnp.int32) for i in range(IMAGES))

        spread = (
            lax.broadcasted_iota(jnp.int32, (PATCHES, ROWS), 1)
            - PATCHES * image(lax.broadcasted_iota(jnp.int32, (PATCHES, ROWS), 1))
            == lax.broadcasted_iota(jnp.int32, (PATCHES, ROWS), 0)
        )
        kept = dot(keep[...].astype(F32).astype(BF16), spread.astype(F32).astype(BF16))
        own = lax.broadcasted_iota(jnp.int32, (IMAGES, ROWS), 0) == image(
            lax.broadcasted_iota(jnp.int32, (IMAGES, ROWS), 1)
        )
        dropped = jnp.sum(jnp.where(own & (kept < 0.5), 1.0, 0.0), 0, keepdims=True)
        wall[...] = jnp.where(
            image(row_at) == image(col_at), jnp.broadcast_to(dropped, (ROWS, ROWS)) * MASKED, OUTSIDE
        )
        loop(8, first_normal, 2)
        to_scalars.wait()

    barrier = pltpu.get_barrier_semaphore()
    announce(barrier, neighbours())
    all_announced(barrier, neighbours())
    sends = gather_weights(master, vectors, loads[:2], g, send_sem, recv_sem, meanwhile)

    for w in range(8):
        window = sum(g[int(VECTOR_AT[16 * w + i])].astype(F32) for i in range(16))
        vec[:, w * 128 : (w + 1) * 128] = window

    def first_norm(i):
        a_low[strip(i), :] = (d_a[strip(i), :] * line(0) + line(1)).astype(BF16)

    loop(8, first_norm, 4)

    def project(j):
        left[pl.ds(2 * j, 2)] = a_low[:, lanes(j, 256)].T.reshape(2, 128, ROWS)
        at = lanes(j, 256)
        made = []
        for m in range(3):
            weights = columns(m, 2 * j, 2)
            w_qkv[m, :, at] = weights
            made.append(dot(a_low[...], weights))
        q[:, at] = (made[0] + vec[2:3, at]).astype(BF16)
        k[:, at] = made[1].astype(BF16)
        v[:, at] = (made[2] + vec[3:4, at]).astype(BF16)

    loop(4, project, 4)

    low_half = lax.broadcasted_iota(jnp.int32, (ROWS, 128), 1) < HEAD_DIM

    def split(pair):
        nothing = jnp.zeros_like(pair)
        return jnp.where(low_half, pair, nothing), jnp.where(low_half, nothing, pair)

    def attend(j):
        at = lanes(j, 128)
        kp = k[:, at]
        weights = []
        for h, qh in enumerate(split(q[:, at])):
            raw = dot_nt(qh, kp)
            masked = jnp.where(wall[...] == 0.0, raw * SCALE, wall[...])
            e = jnp.exp(masked - jnp.max(masked, -1, keepdims=True))
            p = e / jnp.sum(e, -1, keepdims=True)
            low = p.astype(BF16)
            probs[2 * j + h] = low
            weights.append(low)
        pair = dot(jnp.concatenate(weights, 1), jnp.concatenate(split(v[:, at]), 0)).astype(BF16)
        att[:, at] = pair
        left[8 + j] = pair.T

    loop(8, attend, 4)

    def to_mid(j):
        at = lanes(j, 256)
        mid[:, at] = tokens[:, at] + (dot(att[...], columns(3, 2 * j, 2)) + vec[4:5, at])

    loop(4, to_mid, 4)

    def second_norm(i):
        n, _ = normal(mid[strip(i), :])
        a_low[strip(i), :] = (n * line(5) + line(6)).astype(BF16)

    loop(8, second_norm, 8)

    def hidden(j):
        pre = dot(a_low[...], columns(4, 2 * j, 2)) + vec[pl.ds(8 + j // 4, 1), lanes(j % 4, 256)]
        half = 0.5 * (1.0 + lax.erf(pre * math.sqrt(0.5)))
        slope = half + pre * (jnp.exp(-0.5 * pre * pre) * (1.0 / math.sqrt(2.0 * math.pi)))
        low = (pre * half).astype(BF16)
        left[pl.ds(24 + 2 * j, 2)] = low.T.reshape(2, 128, ROWS)
        weights = rows_of(5, 2 * j, 2)
        w_out[lanes(j, 256), :] = weights
        d_pre = (dot_nt(stack(64, 8), weights) * slope).astype(BF16)
        right[32 + 2 * j] = d_pre[:, :128]
        right[33 + 2 * j] = d_pre[:, 128:]
        add_sums(8 + j // 4, d_pre.astype(F32), lanes(j % 4, 256))

    loop(16, hidden, 4)

    def second_back(j):
        at = lanes(j, 256)
        left[pl.ds(16 + 2 * j, 2)] = a_low[:, at].T.reshape(2, 128, ROWS)
        d_a[:, at] = dot_nt(stack(32, 32), rows_of(4, 2 * j, 2))

    loop(4, second_back, 4)

    def mid_back(i):
        rows = strip(i)
        n, scale = normal(mid[rows, :])
        d = d_a[rows, :]
        e = d * line(5)
        inner = e - jnp.mean(e, -1, keepdims=True) - n * jnp.mean(e * n, -1, keepdims=True)
        whole = d_mid[rows, :] + inner * scale
        d_mid[rows, :] = whole
        low = whole.astype(BF16)
        for c in range(8):
            right[24 + c, rows, :] = low[:, c * 128 : (c + 1) * 128]
        add_sums(5, d * n)
        add_sums(6, d)
        add_sums(4, low.astype(F32))

    loop(8, mid_back, 8)

    def att_back(j):
        att[:, lanes(j, 256)] = dot_nt(stack(24, 8), rows_of(3, 2 * j, 2)).astype(BF16)

    loop(4, att_back, 4)

    def heads_back(j):
        at = lanes(j, 128)
        vp = v[:, at]
        q_parts, k_parts, da_parts = split(q[:, at]), split(k[:, at]), split(att[:, at])
        d_raws, weights = [], []
        for h in range(2):
            low = probs[2 * j + h]
            p = low.astype(F32)
            d_p = dot_nt(da_parts[h], vp)
            d_m = p * (d_p - jnp.sum(p * d_p, -1, keepdims=True))
            d_raws.append(jnp.where(wall[...] == 0.0, d_m * SCALE, 0.0).astype(BF16))
            weights.append(low)
        d_q = dot(jnp.concatenate(d_raws, 1), jnp.concatenate(k_parts, 0)).astype(BF16)
        d_k = dot_tn(jnp.concatenate(d_raws, 0), jnp.concatenate(q_parts, 0)).astype(BF16)
        d_v = dot_tn(jnp.concatenate(weights, 0), jnp.concatenate(da_parts, 0)).astype(BF16)
        right[j] = d_q
        right[8 + j] = d_k
        right[16 + j] = d_v
        add_sums(2, d_q.astype(F32), at)
        add_sums(3, d_v.astype(F32), at)

    for copy in sends:
        copy.wait_send()
    announce(ready, neighbours())

    def first_back(j):
        at = lanes(j, 256)
        weights = jnp.concatenate([w_qkv[m, at, :] for m in range(3)], 1)
        d_a[:, at] = dot_nt(stack(0, 24), weights)

    def token_back(i):
        rows = strip(i)
        n, scale = normal(tokens[rows, :])
        d = d_a[rows, :]
        e = d * line(0)
        inner = e - jnp.mean(e, -1, keepdims=True) - n * jnp.mean(e * n, -1, keepdims=True)
        d_mid[rows, :] = d_mid[rows, :] + inner * scale
        add_sums(0, d * n)
        add_sums(1, d)

    def input_side(stage):
        if stage < 2:
            loop(2, lambda i: first_back(2 * stage + i), 2)
        else:
            loop(8, token_back, 8)
            input_grad[...] = d_mid[0:TOKENS, :].astype(BF16)
            folded = jnp.sum(sums[...], 1)
            vec_out[0] = folded[:8]
            vec_out[1, 0 : NV - 8] = folded[8:]
            vec_out[1, NV - 8 :] = jnp.zeros((16 - NV, D), F32)

    def output_side(stage):
        fan = left[24 + 8 * stage : 32 + 8 * stage].reshape(D, ROWS)
        mid[...] += dot_tn(fan, w_out[stage * D : (stage + 1) * D, :])
        if stage == 3:
            output[...] = (mid[...] + vec[7:8, :])[:TOKENS].astype(BF16)

    def further():
        announce(ready_too, others())

    return heads_back, input_side, output_side, further


ROUNDS = (
    (2, 2), (2, 1), (1, 2), (3, 2), (2, 3), (1, 1), (3, 1), (0, 2), (2, 0), (1, 3), (3, 3), (0, 1), (1, 0), (3, 0), (0, 3), (0, 0),
)
AHEAD = 1
RING = 2 * AHEAD + 2
OUT_RING = 6
OUT_ROUNDS = tuple(round_ for round_ in ROUNDS if round_[0])


VMEM_LIMIT = 62 * MIB


def in_hbm(array):
    return pltpu.with_memory_space_constraint(array, pltpu.HBM)


class Rows:
    def __init__(self, buffer, first):
        self.buffer, self.first = buffer, first

    def row(self, n):
        return self.buffer.at[pl.ds(64 * (self.first + n), 64)]

    def half(self, n, second):
        return self.buffer.at[pl.ds(64 * (self.first + n) + 32 * second, 32)]

    def get(self, n, ai):
        return self.buffer[pl.ds(64 * (self.first + n) + 16 * ai, 16)].reshape(256, SIDE).astype(F32)

    def put(self, n, ai, value):
        self.buffer[pl.ds(64 * (self.first + n) + 16 * ai, 16)] = value.astype(BF16).reshape(16, 16, SIDE)


def scatter_kernel(
    tables, left, right, vec_in,
    total, window, norm_tile,
    g, kept, a_out, a_in,
    vec_y, vec_y_in, vec_x, vec_x_in, vec_z, vec_z_in, vec_t, tiles,
    tw_send, tw_recv, c_send, c_recv, b_send, b_recv, a_send, a_recv, v_send, v_recv, n_send, n_recv,
    heads_back, between, total_copy,
):
    pos, core = place()
    twin = device(pos, 1 - core)
    axes = [[device(moved(pos, a, s), core) for s in (1, 2, 3)] for a in range(3)]
    plane, column = partners()
    sizes, at = (3 * RING, 3 * RING, 3 * OUT_RING, 24, 12, 9, 6, 3), 0
    places = []
    for size in sizes:
        places.append(Rows(g, at))
        at += size
    tw_out, tw_in, c_out, c_in, c_half, b_out, b_in, b_half = places

    def out_row(p, round_):
        return 3 * (OUT_ROUNDS.index(round_) % OUT_RING) + p

    def pick(options, i):
        value = options[-1]
        for n in range(len(options) - 2, -1, -1):
            value = jnp.where(i == n, options[n], value)
        return value

    def axis_of(p, which):
        return lax.rem(p + which, 3)

    def neighbour(p, which, by):
        axis = axis_of(p, which)
        return tuple(pick([axes[a][by - 1][n] for a in range(3)], axis) for n in range(2))

    adds = (lambda x: 16 * lax.div(x, 2) + 4 * lax.rem(x, 2), lambda y: 32 * y, lambda z: z)
    share = [
        [[adds[axis](lax.rem(pos[axis] + by, 4)) for by in range(4)] for axis in ORDERS[p]] for p in range(3)
    ]

    def row_pairs(k, p, of_core):
        ci, bi = ROUNDS[k]
        base = pick([share[i][2][ci] + share[i][1][bi] for i in range(3)], p) + 8 * of_core
        pairs = []
        for ai in range(4):
            slot = (base + pick([share[i][0][ai] for i in range(3)], p)) * 6 + 2 * p
            made = []
            for i in range(2):
                row, lane = lax.div(slot + i, 128), lax.rem(slot + i, 128)
                made.append(dot(left[tables[8 + row, lane]], right[tables[16 + row, lane]]))
            pairs.append(jnp.concatenate(made, 0))
        return pairs

    def remote(src, dst, send_sem, recv_sem, to):
        return pltpu.make_async_remote_copy(
            src_ref=src, dst_ref=dst, send_sem=send_sem, recv_sem=recv_sem, device_id=to, device_id_type=MESH
        )

    def twin_copy(k, p):
        n = 3 * (k % RING) + p
        return remote(tw_out.row(n), tw_in.row(n), tw_send.at[3 * k + p], tw_recv.at[3 * k + p], twin)

    def for_twin(k, p, pairs=None):
        if k >= len(ROUNDS):
            return
        if k >= RING:
            twin_copy(k - RING, p).wait_send()
        for ai, value in enumerate(pairs or row_pairs(k, p, 1 - core)):
            tw_out.put(3 * (k % RING) + p, ai, value)
        twin_copy(k, p).start()

    def chip_sum(k, p, ai, pairs):
        return pairs[ai] + tw_in.get(3 * (k % RING) + p, ai)

    def c_half_copy(p, bi, second):
        n = p * 4 + bi
        return remote(
            c_out.half(out_row(p, (2, bi)), second), c_half.half(n, second), c_send.at[2 * n + second], c_recv.at[2 * n + second],
            neighbour(p, 2, 3 if second else 1),
        )

    def c_whole_copy(p, bi, leftward):
        n = 12 * leftward + p * 4 + bi
        return remote(
            c_out.row(out_row(p, (1 + 2 * leftward, bi))), c_in.row(n), c_send.at[24 + n], c_recv.at[24 + n], neighbour(p, 2, 3 if leftward else 1)
        )

    def free_out(p, round_):
        before = OUT_ROUNDS.index(round_) - OUT_RING
        if before >= 0:
            left_out(p, OUT_ROUNDS[before])

    def left_out(p, round_):
        ci, bi = round_
        if ci == 2:
            c_half_copy(p, bi, 0).wait_send()
            c_half_copy(p, bi, 1).wait_send()
        else:
            c_whole_copy(p, bi, ci // 2).wait_send()

    def b_half_copy(p, second):
        return remote(
            b_out.half(3 * p, second), b_half.half(p, second), b_send.at[4 * p + second], b_recv.at[4 * p + second],
            neighbour(p, 1, 3 if second else 1),
        )

    def b_whole_copy(p, leftward):
        return remote(
            b_out.row(3 * p + 1 + leftward), b_in.row(2 * p + leftward), b_send.at[4 * p + 2 + leftward],
            b_recv.at[4 * p + 2 + leftward], neighbour(p, 1, 3 if leftward else 1),
        )

    def a_copy(p, by):
        n = 3 * p + by - 1
        return remote(a_out.at[n], a_in.at[n], a_send.at[n], a_recv.at[n], neighbour(p, 0, by))

    def opposite_row(k, p, pairs):
        _, bi = ROUNDS[k]
        free_out(p, ROUNDS[k])
        for ai in range(4):
            c_out.put(out_row(p, ROUNDS[k]), ai, chip_sum(k, p, ai, pairs))
            if ai % 2:
                c_half_copy(p, bi, ai // 2).start()

    def side_row(k, p, pairs):
        ci, bi = ROUNDS[k]
        leftward = ci // 2
        n = p * 4 + bi
        c_half_copy(p, bi, leftward).wait_recv()
        free_out(p, ROUNDS[k])
        for ai in range(4):
            value = chip_sum(k, p, ai, pairs)
            if ai // 2 == leftward:
                value = value + c_half.get(n, ai)
            c_out.put(out_row(p, ROUNDS[k]), ai, value)
        c_whole_copy(p, bi, leftward).start()

    def own_row(k, p, pairs):
        _, bi = ROUNDS[k]
        n = p * 4 + bi
        leftward = bi // 2
        c_whole_copy(p, bi, 0).wait_recv()
        c_whole_copy(p, bi, 1).wait_recv()
        if bi % 2:
            b_half_copy(p, leftward).wait_recv()
        for ai in range(4):
            value = chip_sum(k, p, ai, pairs) + c_in.get(n, ai) + c_in.get(12 + n, ai)
            if bi == 0:
                kept[p, :, ai * 128 : (ai + 1) * 128] = value
                continue
            if bi % 2 and ai // 2 == leftward:
                value = value + b_half.get(p, ai)
            b_out.put(3 * p + (0 if bi == 2 else 1 + leftward), ai, value)
            if bi == 2 and ai % 2:
                b_half_copy(p, ai // 2).start()
        if bi % 2:
            b_whole_copy(p, leftward).start()

    def vec_twin():
        return remote(vec_in.at[1 - core], vec_t.at[0], v_send.at[0], v_recv.at[0], twin)

    def vec_copy(axis, by):
        src, dst = ((vec_x, vec_x_in), (vec_y, vec_y_in), (vec_z, vec_z_in))[axis]
        n = 1 + 3 * axis + by - 1
        there = lax.rem(pos[axis] + by, 4)
        piece = src.at[there] if axis == 1 else src.at[there // 2] if axis == 0 else src
        return remote(piece, dst.at[by - 1], v_send.at[n], v_recv.at[n], axes[axis][by - 1])

    def vec_start(axis):
        for by in (1, 2, 3):
            vec_copy(axis, by).start()

    def vec_sum(axis, whole):
        dst = (vec_x_in, vec_y_in, vec_z_in)[axis]
        for by in (1, 2, 3):
            vec_copy(axis, by).wait_recv()
            whole = whole + dst[by - 1]
        return whole

    def vec_last():
        return remote(window.at[core], window.at[core], v_send.at[10], v_recv.at[10], twin)

    def vec_stage(stage):
        if stage < 0:
            vec_twin().start()
        elif stage == 0:
            vec_twin().wait_recv()
            whole = vec_in[core] + vec_t[0]
            for i in range(4):
                vec_y[i] = whole[:, 256 * i : 256 * i + 256]
            vec_start(1)
        elif stage == 1:
            whole = vec_sum(1, vec_y[pos[1]])
            for i in range(2):
                vec_x[i] = whole[:, 128 * i : 128 * i + 128]
            vec_start(0)
        elif stage == 2:
            vec_z[...] = vec_sum(0, vec_x[pos[0] // 2])
            vec_start(2)
        elif stage == 3:
            window[core] = vec_sum(2, vec_z[...])
            vec_last().start()

    def one_row(k, p, pairs=None):
        pairs = pairs or row_pairs(k, p, core)
        twin_copy(k, p).wait_recv()
        ci = ROUNDS[k][0]
        (own_row if ci == 0 else opposite_row if ci == 2 else side_row)(k, p, pairs)

    x_low = lax.rem(pos[0], 2)

    def class_at(i):
        mine = jnp.where((i == 0) | ((i >= 2) & (i < 5)), x_low, 1 - x_low)
        step = pick([2, 2, 0, 1, 3, 1, 0, 3], i)
        return mine * 4 + lax.rem(pos[2] + step, 4)

    def classes_back(first, count):
        loop(count, lambda i: heads_back(class_at(first + i)), count)

    classes_back(0, 2)
    between(-1, vec_stage)
    loop(2, lambda p: for_twin(0, p))
    classes_back(2, 3)
    for_twin(0, jnp.int32(2))
    loop(2, lambda p: one_row(0, p))
    classes_back(5, 3)
    loop(2, lambda p: for_twin(1, p))
    one_row(0, jnp.int32(2))
    for_twin(1, jnp.int32(2))
    for k in range(1, len(ROUNDS)):

        def one_round(p):
            ahead = row_pairs(k + AHEAD, p, 1 - core) if k + AHEAD < len(ROUNDS) else None
            pairs = row_pairs(k, p, core)
            for_twin(k + AHEAD, p, ahead)
            one_row(k, p, pairs)

        between(k, vec_stage)
        loop(3, one_round)

    def row_sum(p, ai):
        return kept[p, :, ai * 128 : (ai + 1) * 128] + b_in.get(2 * p, ai) + b_in.get(2 * p + 1, ai)

    def last_axis(p):
        b_whole_copy(p, 0).wait_recv()
        b_whole_copy(p, 1).wait_recv()
        for by in (2, 1, 3):
            a_out[3 * p + by - 1] = row_sum(p, by).astype(BF16)
            a_copy(p, by).start()

    loop(3, last_axis)

    wide, narrow = lax.axis_index("wide"), lax.axis_index("narrow")
    remote(window.at[1 - core], window.at[1 - core], v_send.at[10], v_recv.at[10], twin).wait_recv()
    lane = lax.broadcasted_iota(jnp.int32, (8, 128), 1) // 8
    own_lanes = lane == lax.rem(wide, 2) * 8 + narrow
    squares = jnp.zeros((8, 128), F32)
    for i in range(2):
        own = jnp.where(own_lanes, window[i], 0.0)
        squares = squares + own * own

    for p in range(3):
        value = row_sum(p, 0)
        for by in (1, 3, 2):
            a_copy(p, by).wait_recv()
            value = value + a_in[3 * p + by - 1].astype(F32)
        total[2 * p] = value[:128]
        total[2 * p + 1] = value[128:]
        squares = squares + by_eights(value * value)
    total_copy.start()

    def norm_copy(stage, i):
        n = 15 * stage + i
        to = (column if stage else plane)[i]
        return remote(tiles.at[stage], tiles.at[2 + n], n_send.at[n], n_recv.at[n], to)

    def sent(p):
        for k in range(len(ROUNDS) - RING, len(ROUNDS)):
            twin_copy(k, p).wait_send()
        for round_ in OUT_ROUNDS[-OUT_RING:]:
            left_out(p, round_)
        for side in (0, 1):
            b_half_copy(p, side).wait_send()
            b_whole_copy(p, side).wait_send()
        for by in (1, 2, 3):
            a_copy(p, by).wait_send()

    def all_sent():
        loop(3, sent)
        vec_twin().wait_send()
        vec_last().wait_send()
        for axis in range(3):
            for by in (1, 2, 3):
                vec_copy(axis, by).wait_send()

    whole = squares
    for stage, count in ((0, 15), (1, 7)):
        tiles[stage] = whole
        for i in range(count):
            norm_copy(stage, i).start()
        if stage == 0:
            all_sent()
        for i in range(count):
            norm_copy(stage, i).wait_recv()
            whole = whole + tiles[2 + 15 * stage + i]
    norm_tile[...] = whole
    for stage, count in ((0, 15), (1, 7)):
        for i in range(count):
            norm_copy(stage, i).wait_send()


def whole_kernel(
    owner, places, master_in, vectors_in, patches, keep_in, cotangent,
    output_out, input_grad_out, total_out, window, norm_tile, *scratch,
):
    gathered, scattered = scratch[:PASS_SCRATCH], scratch[PASS_SCRATCH:]
    g, left, right, flats = gathered[:4]
    vec_in, output, input_grad, total, out_sem, *scattered = scattered
    ready, ready_too = gathered[-2:]
    results = [
        pltpu.make_async_copy(src, dst, out_sem.at[i])
        for i, (src, dst) in enumerate(((output, output_out), (input_grad, input_grad_out), (total, total_out)))
    ]
    heads_back, input_side, output_side, further = pass_kernel(
        owner, places, master_in, vectors_in, patches, keep_in, cotangent, output, input_grad, total, vec_in, *gathered
    )

    def between(k, vec_stage):
        if k < 0:
            all_announced(ready, neighbours())
        elif 1 <= k <= 3:
            input_side(k - 1)
            if k == 1:
                further()
            if k == 3:
                results[1].start()
                vec_stage(-1)
        elif 4 <= k <= 7:
            output_side(k - 4)
            if k == 5:
                all_announced(ready_too, others())
            if k == 7:
                results[0].start()
        if k in (5, 7, 9, 11):
            vec_stage((k - 5) // 2)

    scatter_kernel(
        gathered[TABLES], left, right, vec_in, total, window, norm_tile, g, flats, *scattered, heads_back, between, results[2]
    )
    for result in results:
        result.wait()


PASS_SCRATCH, TABLES = 26, 20


def forward_backward(*operands):
    vmem = pl.BlockSpec(memory_space=pltpu.VMEM)
    flat = (ROWS, D)
    dma = pltpu.SemaphoreType.DMA
    pass_scratch = [
        pltpu.VMEM((ALL_ROWS, 16, 128), BF16),
        pltpu.VMEM((56, 128, ROWS), BF16),
        pltpu.VMEM((72, ROWS, 128), BF16),
        pltpu.VMEM((4, *flat), F32),
        *[pltpu.VMEM(flat, BF16)] * 5,
        pltpu.VMEM((HEADS, ROWS, ROWS), BF16),
        pltpu.VMEM((3, D, D), BF16),
        pltpu.VMEM((FF, D), BF16),
        pltpu.VMEM((ROWS, ROWS), F32),
        pltpu.VMEM((NV, 8, D), F32),
        pltpu.VMEM((16, D), F32),
        pltpu.VMEM((8, NV), F32),
        pltpu.VMEM((IMAGES, PATCHES), jnp.int32),
        pltpu.VMEM((6, 128), jnp.int32),
        pltpu.VMEM((6, 128), jnp.int32),
        pltpu.VMEM((24, 128), jnp.int32),
        pltpu.SMEM((24, 128), jnp.int32),
        dma((3, 40)),
        dma((3, 40)),
        dma((8,)),
        pltpu.SemaphoreType.REGULAR,
        pltpu.SemaphoreType.REGULAR,
    ]
    assert len(pass_scratch) == PASS_SCRATCH
    return pl.pallas_call(
        whole_kernel,
        out_shape=[
            jax.ShapeDtypeStruct((TOKENS, D), BF16),
            jax.ShapeDtypeStruct((TOKENS, D), BF16),
            jax.ShapeDtypeStruct((6, SIDE, SIDE), F32),
            jax.ShapeDtypeStruct((2, 8, 128), F32),
            jax.ShapeDtypeStruct((8, 128), F32),
        ],
        in_specs=[pl.BlockSpec(memory_space=pltpu.HBM)] * 7,
        out_specs=[pl.BlockSpec(memory_space=pltpu.HBM)] * 3 + [vmem] * 2,
        scratch_shapes=pass_scratch
        + [
            pltpu.VMEM((2, 8, D), F32),
            pltpu.VMEM((TOKENS, D), BF16),
            pltpu.VMEM((TOKENS, D), BF16),
            pltpu.VMEM((6, SIDE, SIDE), F32),
            dma((3,)),
            pltpu.VMEM((9, 256, 128), BF16),
            pltpu.VMEM((9, 256, 128), BF16),
            pltpu.VMEM((4, 8, 256), F32),
            pltpu.VMEM((3, 8, 256), F32),
            pltpu.VMEM((2, 8, 128), F32),
            pltpu.VMEM((3, 8, 128), F32),
            pltpu.VMEM((8, 128), F32),
            pltpu.VMEM((3, 8, 128), F32),
            pltpu.VMEM((1, 8, D), F32),
            pltpu.VMEM((24, 8, 128), F32),
            dma((48,)), dma((48,)), dma((48,)), dma((48,)), dma((12,)), dma((12,)), dma((9,)), dma((9,)),
            dma((11,)), dma((11,)), dma((22,)), dma((22,)),
        ],
        compiler_params=pltpu.CompilerParams(
            collective_id=0, has_side_effects=True, vmem_limit_bytes=VMEM_LIMIT
        ),
        cost_estimate=pl.CostEstimate(
            flops=19_000_000_000, bytes_accessed=10_000_000, transcendentals=3_000_000
        ),
        name="forward_backward",
    )(*(in_hbm(operand) for operand in operands))


def rounded_dot(left, right, over):
    return lax.dot_general(
        left.astype(BF16), right.astype(BF16), (over, ((), ())), preferred_element_type=F32
    )


def step_kernel(
    raw, window, norm_tile, shift, master, left_stats, right_stats, left_root, right_root, vectors, vec_accum,
    output_in, input_grad_in,
    block_grads, new_left, new_right, new_master, new_copy, vec_grads, vec_accum_new, vec_new, grad_norm,
    output, input_grad, passing, sem,
):
    def copies(way):
        ends = ((output_in, output), (input_grad_in, input_grad))
        return [
            pltpu.make_async_copy(
                passing.at[i] if way else pair[0], pair[1] if way else passing.at[i], sem.at[2 * way + i]
            )
            for i, pair in enumerate(ends)
        ]

    norm = jnp.sqrt(jnp.sum(norm_tile[...], keepdims=True))
    clip = 1.0 / jnp.maximum(norm, 1.0)

    @pl.when(pl.program_id(0) == 0)
    def _():
        for copy in copies(0):
            copy.start()
        grad_norm[...] = norm
        lanes = pltpu.roll(window[...].reshape(16, 128), shift[0], 1)
        grads = clip * lanes.T[:8, :NV]
        vec_grads[...] = grads
        accum = 0.5 * vec_accum[...] + 0.5 * grads * grads
        vec_accum_new[...] = accum
        vec_new[...] = vectors[...] - 0.5 * grads / (jnp.sqrt(accum) + 1e-08)

    for i in range(raw.shape[0]):
        grads = raw[i] * clip
        block_grads[i] = grads
        new_left[i] = 0.5 * left_stats[i] + 0.5 * rounded_dot(grads, grads, ((1,), (1,)))
        new_right[i] = 0.5 * right_stats[i] + 0.5 * rounded_dot(grads, grads, ((0,), (0,)))
        way = rounded_dot(rounded_dot(left_root[i], grads, ((1,), (0,))), right_root[i], ((1,), (0,)))
        master_now = master[i] - 0.5 * way
        new_master[i] = master_now
        new_copy[i] = master_now.astype(BF16)

    @pl.when(pl.program_id(0) == 0)
    def _():
        for came, copy in zip(copies(0), copies(1)):
            came.wait()
            copy.start()

    @pl.when(pl.program_id(0) == pl.num_programs(0) - 1)
    def _():
        for copy in copies(1):
            copy.wait()


def update(raw, window, norm_tile, shift, blocks_in, vectors, vec_accum, output, input_grad):
    per = 3
    blocks = pl.BlockSpec((per, SIDE, SIDE), lambda i: (i, 0, 0))
    anywhere = pl.BlockSpec(memory_space=pltpu.HBM)

    def whole(*shape):
        return pl.BlockSpec(shape, lambda i: (0,) * len(shape))

    f32_blocks = jax.ShapeDtypeStruct((6, SIDE, SIDE), F32)
    f32_vecs = jax.ShapeDtypeStruct((8, NV), F32)
    tokens = jax.ShapeDtypeStruct((TOKENS, D), BF16)
    return pl.pallas_call(
        step_kernel,
        grid=(6 // per,),
        out_shape=[f32_blocks] * 4
        + [jax.ShapeDtypeStruct((6, SIDE, SIDE), BF16)]
        + [f32_vecs] * 3
        + [jax.ShapeDtypeStruct((1, 1), F32)]
        + [tokens] * 2,
        in_specs=[blocks, whole(2, 8, 128), whole(8, 128), pl.BlockSpec(memory_space=pltpu.SMEM)]
        + [blocks] * 5
        + [whole(8, NV)] * 2
        + [anywhere] * 2,
        out_specs=[blocks] * 5 + [whole(8, NV)] * 3 + [whole(1, 1)] + [anywhere] * 2,
        scratch_shapes=[pltpu.VMEM((2, TOKENS, D), BF16), pltpu.SemaphoreType.DMA((4,))],
        compiler_params=pltpu.CompilerParams(vmem_limit_bytes=32 * MIB),
        name="update",
    )(*(in_hbm(a) for a in (raw, window, norm_tile)), shift, *blocks_in, in_hbm(vectors), in_hbm(vec_accum), in_hbm(output), in_hbm(input_grad))


def body(
    patches, keep, cotangent, owner_table, master, left_stats, right_stats, left_root, right_root, vectors, vec_accum,
):
    wide, narrow = lax.axis_index("wide"), lax.axis_index("narrow")
    output, input_grad, raw, window, norm_tile = forward_backward(
        owner_table.reshape(6, 128), jnp.asarray(BLOCK_AT.reshape(6, 128)), master, vectors.T, patches, keep, cotangent
    )
    lane = ((wide % 2) * 8 + narrow) * 8
    shift = jnp.reshape((128 - lane) % 128, (1,)).astype(jnp.int32)
    blocks_in = (master, left_stats, right_stats, left_root, right_root)
    *of_blocks, vec_grads, vec_accum_new, vec_new, grad_norm, output, input_grad = update(
        raw, window, norm_tile, shift, blocks_in, vectors.T, vec_accum.T, output, input_grad
    )
    return (output, input_grad, *of_blocks, vec_grads.T, vec_accum_new.T, vec_new.T, grad_norm.reshape(()))


def solution(mesh):
    rows, blocks, vecs = P(BOTH, None), P(BOTH, None, None), P(None, BOTH)
    return jax.shard_map(
        body,
        mesh=mesh,
        in_specs=(rows, rows, rows, P(), blocks, blocks, blocks, blocks, blocks, vecs, vecs),
        out_specs=(rows, rows, blocks, blocks, blocks, blocks, blocks, vecs, vecs, vecs, P()),
        check_vma=False,
    )
```

```python
import functools
import math

import jax
import jax.numpy as jnp
import numpy as np
from jax import lax
from jax.experimental import pallas as pl
from jax.experimental.pallas import tpu as pltpu
from jax.sharding import PartitionSpec as P

MESH = pl.DeviceIdType.MESH
BOTH = ("wide", "narrow")
F32, BF16 = jnp.float32, jnp.bfloat16
MIB = 2**20

D = 1024
FF = 4096
HEADS = 16
HEAD_DIM = 64
PATCHES = 49
IMAGES = 5
TOKENS = IMAGES * PATCHES
ROWS = 256
SIDE = 128
NBLK = 768
NV = 12
LAYER_EPS = 1e-05
MASKED = -1000000000.0
OUTSIDE = -3.0e38
SCALE = HEAD_DIM**-0.5

ORDERS = ((0, 1, 2), (1, 2, 0), (2, 0, 1))
SHARE = (16, 16, 17)
PART_FROM = (0, 128 * 16, 128 * 32)
ALL_ROWS = 128 * 49
NEXT = (0, 3, 1, 2)

FIRST = (0, 64, 128, 192, 256, 512)
WIDTH = (8, 8, 8, 8, 32, 8)
LEFT_AT = (0, 0, 0, 8, 16, 24)
RIGHT_AT = (0, 8, 16, 24, 32, 64)


def slot_places():
    block_at, vector_at = np.zeros(NBLK, np.int32), np.zeros(128, np.int32)
    for dev in range(128):
        wide, narrow = dev // 8, dev % 8
        core = wide % 2
        pos = (wide // 2 % 2 * 2 + narrow // 4, wide // 4, narrow % 4)
        for p, (a, b, c) in enumerate(ORDERS):
            at = PART_FROM[p] + (((core * 4 + pos[c]) * 4 + pos[b]) * 4 + pos[a]) * SHARE[p]
            block_at[dev * 6 + 2 * p] = at
            block_at[dev * 6 + 2 * p + 1] = at + 8
            if p == 2:
                vector_at[dev] = at + 16
    return block_at, vector_at


BLOCK_AT, VECTOR_AT = slot_places()


def place():
    wide, narrow = lax.axis_index("wide"), lax.axis_index("narrow")
    x = (wide // 2) % 2 * 2 + narrow // 4
    return (x, wide // 4, narrow % 4), wide % 2


def device(pos, core):
    x, y, z = pos
    return ((y * 2 + x // 2) * 2 + core, x % 2 * 4 + z)


def moved(pos, axis, by):
    return tuple((c + by) % 4 if a == axis else c for a, c in enumerate(pos))


def partners():
    pos, core = place()
    plane = [device(moved(moved(pos, 0, i), 1, j), core) for i in range(4) for j in range(4) if i or j]
    column = [
        device(moved(pos, 2, i), core if j == 0 else 1 - core) for j in range(2) for i in range(4) if i or j
    ]
    return plane, column


def neighbours():
    pos, core = place()
    return [device(pos, 1 - core)] + [device(moved(pos, a, s), core) for a in range(3) for s in (1, -1)]


def others():
    pos, core = place()
    plane = [(i, j, 0, 0) for i in range(4) for j in range(4) if i or j]
    column = [(0, 0, i, j) for j in range(2) for i in range(4) if i or j]
    near = [(1, 0, 0, 0), (3, 0, 0, 0), (0, 1, 0, 0), (0, 3, 0, 0), (0, 0, 1, 0), (0, 0, 3, 0), (0, 0, 0, 1)]
    return [
        device(tuple((c + by) % 4 for c, by in zip(pos, steps)), core if turn == 0 else 1 - core)
        for *steps, turn in plane + column
        if (*steps, turn) not in near
    ]


def announce(semaphore, partners):
    for partner in partners:
        pl.semaphore_signal(semaphore, inc=1, device_id=partner, device_id_type=MESH)


def all_announced(semaphore, partners):
    pl.semaphore_wait(semaphore, len(partners))


def loop(count, body, together=1):
    lax.fori_loop(0, count, lambda i, _: (body(i), None)[1], None, unroll=together)


def dot(left, right):
    return jnp.dot(left, right, preferred_element_type=F32)


def dot_nt(left, right):
    return lax.dot_general(left, right, (((1,), (1,)), ((), ())), preferred_element_type=F32)


def dot_tn(left, right):
    return lax.dot_general(left, right, (((0,), (0,)), ((), ())), preferred_element_type=F32)


def gather_weights(master, vectors, loads, g, send_sem, recv_sem, meanwhile):
    pos, core = place()
    twin = device(pos, 1 - core)
    near = {(a, s): device(moved(pos, a, s), core) for a in range(3) for s in (1, -1)}

    for load in loads:
        load.wait()

    for p in range(3):
        a, b, c = (pos[axis] for axis in ORDERS[p])
        start = PART_FROM[p] + (((core * 4 + c) * 4 + b) * 4 + a) * SHARE[p]
        g[pl.ds(start, 16)] = master[2 * p : 2 * p + 2].astype(BF16).reshape(16, 16, SIDE)
        if p == 2:
            wide, narrow = lax.axis_index("wide"), lax.axis_index("narrow")
            first_lane = (lax.rem(wide, 2) * 8 + narrow) * 8
            spread = lax.broadcasted_iota(jnp.int32, (8, 128), 1) == (
                lax.broadcasted_iota(jnp.int32, (8, 128), 0) + first_lane
            )
            tile = dot_tn(vectors[...].astype(BF16), spread.astype(BF16)).astype(BF16)
            g[start + 16] = jnp.concatenate([tile, jnp.zeros((16 - NV, 128), BF16)], 0)

    sends = []

    def copy_of(src, dst, p, slot, to):
        return pltpu.make_async_remote_copy(
            src_ref=src, dst_ref=dst, send_sem=send_sem.at[p, slot],
            recv_sem=recv_sem.at[p, slot], device_id=to, device_id_type=MESH,
        )

    def send(src, dst, p, slot, to):
        copy = copy_of(src, dst, p, slot, to)
        copy.start()
        sends.append(copy)

    def arrived(dst, p, slot):
        copy_of(dst, dst, p, slot, twin).wait_recv()

    def at(p, of_core, c, b, a=0, count=4, skip=0, rows=None):
        start = PART_FROM[p] + (((of_core * 4 + c % 4) * 4 + b % 4) * 4 + a % 4) * SHARE[p] + skip
        return g.at[pl.ds(start, count * SHARE[p] if rows is None else rows)]

    def spot(p):
        a, b, c = ORDERS[p]
        return pos[a], pos[b], pos[c]

    def row(p, ci, bi):
        _, b, c = spot(p)
        return at(p, core, c + ci, b + bi)

    def half_row(p, ci, bi, second):
        _, b, c = spot(p)
        return at(p, core, c + ci, b + bi, 2 if second else 0, 2)

    def chunk(p, ai):
        a, b, c = spot(p)
        return at(p, core, c, b, a + ai, 1)

    def half_chunk(p, ai, second):
        a, b, c = spot(p)
        return at(p, core, c, b, a + ai, 1, 8 if second else 0, SHARE[p] - 8 if second else 8)

    def to_twin(p, ci, bi):
        r = row(p, ci, bi)
        send(r, r, p, 24 + 4 * (ci % 4) + bi % 4, twin)

    def onward(p, base, axis, half):
        first, second = half(False), half(True)
        return (
            lambda: send(first, first, p, base + 2, near[axis, 1]),
            lambda: send(second, second, p, base + 3, near[axis, -1]),
        )

    def both(p, base, axis, src, dst):
        send(src, dst, p, base, near[axis, 1])
        send(src, dst, p, base + 1, near[axis, -1])

    parts = range(3)
    for p in parts:
        both(p, 0, ORDERS[p][0], chunk(p, 0), chunk(p, 0))
    for p in parts:
        axis = ORDERS[p][0]
        arrived(chunk(p, -1), p, 0)
        onward(p, 0, axis, lambda second: half_chunk(p, -1, second))[0]()
        arrived(chunk(p, 1), p, 1)
        onward(p, 0, axis, lambda second: half_chunk(p, 1, second))[1]()
    for p in parts:
        arrived(half_chunk(p, 2, False), p, 2)
        arrived(half_chunk(p, 2, True), p, 3)
        r = row(p, 0, 0)
        both(p, 4, ORDERS[p][1], r, r)
        both(p, 8, ORDERS[p][2], r, r)
        to_twin(p, 0, 0)
    for p in parts:
        for bi, i in ((-1, 1), (1, 2)):
            r = row(p, 0, bi)
            arrived(r, p, 4 + (i - 1))
            onward(p, 4, ORDERS[p][1], lambda second: half_row(p, 0, bi, second))[i - 1]()
            both(p, 8 + 4 * i, ORDERS[p][2], r, r)
            to_twin(p, 0, bi)

    meanwhile()

    def sides(p, i):
        bi = NEXT[i]
        for ci, j in ((-1, 0), (1, 1)):
            arrived(row(p, ci, bi), p, 8 + 4 * i + j)
            onward(p, 8 + 4 * i, ORDERS[p][2], lambda second: half_row(p, ci, bi, second))[j]()
            to_twin(p, ci, bi)

    def opposite(p, i):
        bi = NEXT[i]
        arrived(half_row(p, 2, bi, False), p, 8 + 4 * i + 2)
        arrived(half_row(p, 2, bi, True), p, 8 + 4 * i + 3)
        to_twin(p, 2, bi)

    for p in parts:
        sides(p, 0)
    for p in parts:
        arrived(half_row(p, 0, 2, False), p, 6)
        arrived(half_row(p, 0, 2, True), p, 7)
        r = row(p, 0, 2)
        both(p, 8 + 12, ORDERS[p][2], r, r)
        to_twin(p, 0, 2)
    for p in parts:
        sides(p, 1)
        sides(p, 2)
    for p in parts:
        opposite(p, 0)
    early = len(sends)
    for p in parts:
        sides(p, 3)

    def from_twin(p, which):
        _, b, c = spot(p)
        for ci in range(4):
            for bi in range(4):
                if (ci == 2 or bi == 2) == which:
                    arrived(at(p, 1 - core, c + ci, b + bi), p, 24 + 4 * ci + bi)

    for p in parts:
        opposite(p, 1)
        opposite(p, 2)
        from_twin(p, False)
    for copy in sends[:early]:
        copy.wait_send()
    for p in parts:
        opposite(p, 3)
    for p in parts:
        from_twin(p, True)
    return sends[early:]


def normal(values):
    centre = jnp.mean(values, -1, keepdims=True)
    centred = values - centre
    spread = jnp.mean(centred * centred, -1, keepdims=True)
    scale = lax.rsqrt(spread + LAYER_EPS)
    return centred * scale, scale


def by_eights(values):
    return jnp.sum(values.reshape(values.shape[0] // 8, 8, values.shape[1]), 0)


def pass_kernel(
    owner_in, places_in, master_in, vectors_in, patches, keep_in, cotangent, output, input_grad, master, vec_out,
    g, left, right, flats, q, k, v, att, a_low, probs, w_qkv, w_out, wall, sums, vec,
    vectors, keep, owner, places, made, tables, send_sem, recv_sem, held_sem, ready, ready_too,
):
    tokens, d_mid, d_a, mid = (flats.at[i] for i in range(4))
    loads = [
        pltpu.make_async_copy(src, to, held_sem.at[i])
        for i, (src, to) in enumerate(
            (
                (master_in, master), (vectors_in, vectors), (patches, output), (cotangent, input_grad), (keep_in, keep),
                (owner_in, owner), (places_in, places),
            )
        )
    ]
    for load in loads:
        load.start()

    def block(n):
        return g[pl.ds(tables[lax.div(n, 128), lax.rem(n, 128)], 8)].reshape(SIDE, SIDE)

    def columns(m, j, count):
        rows = (256 if m == 4 else 64 if m < 4 else 256) // WIDTH[m]
        return jnp.concatenate(
            [
                jnp.concatenate([block(FIRST[m] + r * WIDTH[m] + j + i) for i in range(count)], 1)
                for r in range(rows)
            ],
            0,
        )

    def rows_of(m, i, count):
        return jnp.concatenate(
            [
                jnp.concatenate([block(FIRST[m] + (i + r) * WIDTH[m] + c) for c in range(WIDTH[m])], 1)
                for r in range(count)
            ],
            0,
        )

    def lanes(i, width):
        return pl.ds(pl.multiple_of(i * width, width), width)

    def strip(i):
        return pl.ds(pl.multiple_of(i * 32, 32), 32)

    def stack(first, count):
        return jnp.concatenate([right[first + i] for i in range(count)], 1)

    def line(i):
        return vec[i : i + 1, :]

    def add_sums(i, value, where=slice(None)):
        sums[i, :, where] += by_eights(value)

    def first_normal(i):
        n, _ = normal(tokens[strip(i), :])
        d_a[strip(i), :] = n
        cot = d_mid[strip(i), :]
        for c in range(8):
            right[64 + c, strip(i), :] = cot[:, c * 128 : (c + 1) * 128].astype(BF16)
        add_sums(7, cot)

    def make_tables():
        number = owner[...]
        matrix = sum((number >= first).astype(jnp.int32) for first in FIRST[1:])

        def by_matrix(values):
            return sum(jnp.where(matrix == m, value, 0) for m, value in enumerate(values))

        inner = number - by_matrix(FIRST)
        wide_one = matrix == 4
        made[8:14, :] = by_matrix(LEFT_AT) + jnp.where(wide_one, inner >> 5, inner >> 3)
        made[16:22, :] = by_matrix(RIGHT_AT) + jnp.where(wide_one, inner & 31, inner & 7)
        lane = lax.broadcasted_iota(jnp.int32, (128, 128), 1)
        found = [jnp.zeros((8, 128), F32)] * 6
        for i in range(6):
            held_by = jnp.broadcast_to(number[i : i + 1].astype(F32), (128, 128)).T
            lies_at = jnp.broadcast_to(places[i : i + 1, :].astype(F32), (128, 128)).T
            for j in range(6):
                hit = held_by == (lane + 128 * j).astype(F32)
                found[j] = found[j] + by_eights(jnp.where(hit, lies_at, 0.0))
        for j in range(6):
            at = jnp.sum(found[j], 0, keepdims=True).astype(jnp.int32)
            made[j : j + 1, :] = jnp.clip(at, 0, ALL_ROWS - 8)

    def meanwhile():
        for load in loads[5:]:
            load.wait()
        make_tables()
        to_scalars = pltpu.make_async_copy(made, tables, held_sem.at[7])
        to_scalars.start()
        sums[...] = jnp.zeros_like(sums)
        for load in loads[2:5]:
            load.wait()
        for came, to in ((output, tokens), (input_grad, d_mid)):
            to[0:TOKENS, :] = came[...].astype(F32)
            to[TOKENS:ROWS, :] = jnp.zeros((ROWS - TOKENS, D), F32)
        row_at = lax.broadcasted_iota(jnp.int32, (ROWS, ROWS), 0)
        col_at = lax.broadcasted_iota(jnp.int32, (ROWS, ROWS), 1)

        def image(at):
            return sum((at >= PATCHES * (i + 1)).astype(jnp.int32) for i in range(IMAGES))

        spread = (
            lax.broadcasted_iota(jnp.int32, (PATCHES, ROWS), 1)
            - PATCHES * image(lax.broadcasted_iota(jnp.int32, (PATCHES, ROWS), 1))
            == lax.broadcasted_iota(jnp.int32, (PATCHES, ROWS), 0)
        )
        kept = dot(keep[...].astype(F32).astype(BF16), spread.astype(F32).astype(BF16))
        own = lax.broadcasted_iota(jnp.int32, (IMAGES, ROWS), 0) == image(
            lax.broadcasted_iota(jnp.int32, (IMAGES, ROWS), 1)
        )
        dropped = jnp.sum(jnp.where(own & (kept < 0.5), 1.0, 0.0), 0, keepdims=True)
        wall[...] = jnp.where(
            image(row_at) == image(col_at), jnp.broadcast_to(dropped, (ROWS, ROWS)) * MASKED, OUTSIDE
        )
        loop(8, first_normal, 2)
        to_scalars.wait()

    barrier = pltpu.get_barrier_semaphore()
    announce(barrier, neighbours())
    all_announced(barrier, neighbours())
    sends = gather_weights(master, vectors, loads[:2], g, send_sem, recv_sem, meanwhile)

    for w in range(8):
        window = sum(g[int(VECTOR_AT[16 * w + i])].astype(F32) for i in range(16))
        vec[:, w * 128 : (w + 1) * 128] = window

    def first_norm(i):
        a_low[strip(i), :] = (d_a[strip(i), :] * line(0) + line(1)).astype(BF16)

    loop(8, first_norm, 4)

    def project(j):
        left[pl.ds(2 * j, 2)] = a_low[:, lanes(j, 256)].T.reshape(2, 128, ROWS)
        at = lanes(j, 256)
        made = []
        for m in range(3):
            weights = columns(m, 2 * j, 2)
            w_qkv[m, :, at] = weights
            made.append(dot(a_low[...], weights))
        q[:, at] = (made[0] + vec[2:3, at]).astype(BF16)
        k[:, at] = made[1].astype(BF16)
        v[:, at] = (made[2] + vec[3:4, at]).astype(BF16)

    loop(4, project, 4)

    low_half = lax.broadcasted_iota(jnp.int32, (ROWS, 128), 1) < HEAD_DIM

    def split(pair):
        nothing = jnp.zeros_like(pair)
        return jnp.where(low_half, pair, nothing), jnp.where(low_half, nothing, pair)

    def attend(j):
        at = lanes(j, 128)
        kp = k[:, at]
        weights = []
        for h, qh in enumerate(split(q[:, at])):
            raw = dot_nt(qh, kp)
            masked = jnp.where(wall[...] == 0.0, raw * SCALE, wall[...])
            e = jnp.exp(masked - jnp.max(masked, -1, keepdims=True))
            p = e / jnp.sum(e, -1, keepdims=True)
            low = p.astype(BF16)
            probs[2 * j + h] = low
            weights.append(low)
        pair = dot(jnp.concatenate(weights, 1), jnp.concatenate(split(v[:, at]), 0)).astype(BF16)
        att[:, at] = pair
        left[8 + j] = pair.T

    loop(8, attend, 4)

    def to_mid(j):
        at = lanes(j, 256)
        mid[:, at] = tokens[:, at] + (dot(att[...], columns(3, 2 * j, 2)) + vec[4:5, at])

    loop(4, to_mid, 4)

    def second_norm(i):
        n, _ = normal(mid[strip(i), :])
        a_low[strip(i), :] = (n * line(5) + line(6)).astype(BF16)

    loop(8, second_norm, 8)

    def hidden(j):
        pre = dot(a_low[...], columns(4, 2 * j, 2)) + vec[pl.ds(8 + j // 4, 1), lanes(j % 4, 256)]
        half = 0.5 * (1.0 + lax.erf(pre * math.sqrt(0.5)))
        slope = half + pre * (jnp.exp(-0.5 * pre * pre) * (1.0 / math.sqrt(2.0 * math.pi)))
        low = (pre * half).astype(BF16)
        left[pl.ds(24 + 2 * j, 2)] = low.T.reshape(2, 128, ROWS)
        weights = rows_of(5, 2 * j, 2)
        w_out[lanes(j, 256), :] = weights
        d_pre = (dot_nt(stack(64, 8), weights) * slope).astype(BF16)
        right[32 + 2 * j] = d_pre[:, :128]
        right[33 + 2 * j] = d_pre[:, 128:]
        add_sums(8 + j // 4, d_pre.astype(F32), lanes(j % 4, 256))

    loop(16, hidden, 4)

    def second_back(j):
        at = lanes(j, 256)
        left[pl.ds(16 + 2 * j, 2)] = a_low[:, at].T.reshape(2, 128, ROWS)
        d_a[:, at] = dot_nt(stack(32, 32), rows_of(4, 2 * j, 2))

    loop(4, second_back, 4)

    def mid_back(i):
        rows = strip(i)
        n, scale = normal(mid[rows, :])
        d = d_a[rows, :]
        e = d * line(5)
        inner = e - jnp.mean(e, -1, keepdims=True) - n * jnp.mean(e * n, -1, keepdims=True)
        whole = d_mid[rows, :] + inner * scale
        d_mid[rows, :] = whole
        low = whole.astype(BF16)
        for c in range(8):
            right[24 + c, rows, :] = low[:, c * 128 : (c + 1) * 128]
        add_sums(5, d * n)
        add_sums(6, d)
        add_sums(4, low.astype(F32))

    loop(8, mid_back, 8)

    def att_back(j):
        att[:, lanes(j, 256)] = dot_nt(stack(24, 8), rows_of(3, 2 * j, 2)).astype(BF16)

    loop(4, att_back, 4)

    def heads_back(j):
        at = lanes(j, 128)
        vp = v[:, at]
        q_parts, k_parts, da_parts = split(q[:, at]), split(k[:, at]), split(att[:, at])
        d_raws, weights = [], []
        for h in range(2):
            low = probs[2 * j + h]
            p = low.astype(F32)
            d_p = dot_nt(da_parts[h], vp)
            d_m = p * (d_p - jnp.sum(p * d_p, -1, keepdims=True))
            d_raws.append(jnp.where(wall[...] == 0.0, d_m * SCALE, 0.0).astype(BF16))
            weights.append(low)
        d_q = dot(jnp.concatenate(d_raws, 1), jnp.concatenate(k_parts, 0)).astype(BF16)
        d_k = dot_tn(jnp.concatenate(d_raws, 0), jnp.concatenate(q_parts, 0)).astype(BF16)
        d_v = dot_tn(jnp.concatenate(weights, 0), jnp.concatenate(da_parts, 0)).astype(BF16)
        right[j] = d_q
        right[8 + j] = d_k
        right[16 + j] = d_v
        add_sums(2, d_q.astype(F32), at)
        add_sums(3, d_v.astype(F32), at)

    for copy in sends:
        copy.wait_send()
    announce(ready, neighbours())

    def first_back(j):
        at = lanes(j, 256)
        weights = jnp.concatenate([w_qkv[m, at, :] for m in range(3)], 1)
        d_a[:, at] = dot_nt(stack(0, 24), weights)

    def token_back(i):
        rows = strip(i)
        n, scale = normal(tokens[rows, :])
        d = d_a[rows, :]
        e = d * line(0)
        inner = e - jnp.mean(e, -1, keepdims=True) - n * jnp.mean(e * n, -1, keepdims=True)
        d_mid[rows, :] = d_mid[rows, :] + inner * scale
        add_sums(0, d * n)
        add_sums(1, d)

    def input_side(stage):
        if stage < 2:
            loop(2, lambda i: first_back(2 * stage + i), 2)
        else:
            loop(8, token_back, 8)
            input_grad[...] = d_mid[0:TOKENS, :].astype(BF16)
            folded = jnp.sum(sums[...], 1)
            vec_out[0] = folded[:8]
            vec_out[1, 0 : NV - 8] = folded[8:]
            vec_out[1, NV - 8 :] = jnp.zeros((16 - NV, D), F32)

    def output_side(stage):
        fan = left[24 + 8 * stage : 32 + 8 * stage].reshape(D, ROWS)
        mid[...] += dot_tn(fan, w_out[stage * D : (stage + 1) * D, :])
        if stage == 3:
            output[...] = (mid[...] + vec[7:8, :])[:TOKENS].astype(BF16)

    def further():
        announce(ready_too, others())

    return heads_back, input_side, output_side, further


ROUNDS = (
    (2, 2), (2, 1), (1, 2), (3, 2), (2, 3), (1, 1), (3, 1), (0, 2), (2, 0), (1, 3), (3, 3), (0, 1), (1, 0), (3, 0), (0, 3), (0, 0),
)
AHEAD = 1
RING = 2 * AHEAD + 2
OUT_RING = 6
OUT_ROUNDS = tuple(round_ for round_ in ROUNDS if round_[0])


VMEM_LIMIT = 62 * MIB


def in_hbm(array):
    return pltpu.with_memory_space_constraint(array, pltpu.HBM)


class Rows:
    def __init__(self, buffer, first):
        self.buffer, self.first = buffer, first

    def row(self, n):
        return self.buffer.at[pl.ds(64 * (self.first + n), 64)]

    def half(self, n, second):
        return self.buffer.at[pl.ds(64 * (self.first + n) + 32 * second, 32)]

    def get(self, n, ai):
        return self.buffer[pl.ds(64 * (self.first + n) + 16 * ai, 16)].reshape(256, SIDE).astype(F32)

    def put(self, n, ai, value):
        self.buffer[pl.ds(64 * (self.first + n) + 16 * ai, 16)] = value.astype(BF16).reshape(16, 16, SIDE)


def scatter_kernel(
    tables, left, right, vec_in,
    total, window, norm_tile,
    g, kept, a_out, a_in,
    vec_y, vec_y_in, vec_x, vec_x_in, vec_z, vec_z_in, vec_t, tiles,
    tw_send, tw_recv, c_send, c_recv, b_send, b_recv, a_send, a_recv, v_send, v_recv, n_send, n_recv,
    heads_back, between, total_copy,
):
    pos, core = place()
    twin = device(pos, 1 - core)
    axes = [[device(moved(pos, a, s), core) for s in (1, 2, 3)] for a in range(3)]
    plane, column = partners()
    sizes, at = (3 * RING, 3 * RING, 3 * OUT_RING, 24, 12, 9, 6, 3), 0
    places = []
    for size in sizes:
        places.append(Rows(g, at))
        at += size
    tw_out, tw_in, c_out, c_in, c_half, b_out, b_in, b_half = places

    def out_row(p, round_):
        return 3 * (OUT_ROUNDS.index(round_) % OUT_RING) + p

    def pick(options, i):
        value = options[-1]
        for n in range(len(options) - 2, -1, -1):
            value = jnp.where(i == n, options[n], value)
        return value

    def axis_of(p, which):
        return lax.rem(p + which, 3)

    def neighbour(p, which, by):
        axis = axis_of(p, which)
        return tuple(pick([axes[a][by - 1][n] for a in range(3)], axis) for n in range(2))

    adds = (lambda x: 16 * lax.div(x, 2) + 4 * lax.rem(x, 2), lambda y: 32 * y, lambda z: z)
    share = [
        [[adds[axis](lax.rem(pos[axis] + by, 4)) for by in range(4)] for axis in ORDERS[p]] for p in range(3)
    ]

    def row_pairs(k, p, of_core):
        ci, bi = ROUNDS[k]
        base = pick([share[i][2][ci] + share[i][1][bi] for i in range(3)], p) + 8 * of_core
        pairs = []
        for ai in range(4):
            slot = (base + pick([share[i][0][ai] for i in range(3)], p)) * 6 + 2 * p
            made = []
            for i in range(2):
                row, lane = lax.div(slot + i, 128), lax.rem(slot + i, 128)
                made.append(dot(left[tables[8 + row, lane]], right[tables[16 + row, lane]]))
            pairs.append(jnp.concatenate(made, 0))
        return pairs

    def remote(src, dst, send_sem, recv_sem, to):
        return pltpu.make_async_remote_copy(
            src_ref=src, dst_ref=dst, send_sem=send_sem, recv_sem=recv_sem, device_id=to, device_id_type=MESH
        )

    def twin_copy(k, p):
        n = 3 * (k % RING) + p
        return remote(tw_out.row(n), tw_in.row(n), tw_send.at[3 * k + p], tw_recv.at[3 * k + p], twin)

    def for_twin(k, p, pairs=None):
        if k >= len(ROUNDS):
            return
        if k >= RING:
            twin_copy(k - RING, p).wait_send()
        for ai, value in enumerate(pairs or row_pairs(k, p, 1 - core)):
            tw_out.put(3 * (k % RING) + p, ai, value)
        twin_copy(k, p).start()

    def chip_sum(k, p, ai, pairs):
        return pairs[ai] + tw_in.get(3 * (k % RING) + p, ai)

    def c_half_copy(p, bi, second):
        n = p * 4 + bi
        return remote(
            c_out.half(out_row(p, (2, bi)), second), c_half.half(n, second), c_send.at[2 * n + second], c_recv.at[2 * n + second],
            neighbour(p, 2, 3 if second else 1),
        )

    def c_whole_copy(p, bi, leftward):
        n = 12 * leftward + p * 4 + bi
        return remote(
            c_out.row(out_row(p, (1 + 2 * leftward, bi))), c_in.row(n), c_send.at[24 + n], c_recv.at[24 + n], neighbour(p, 2, 3 if leftward else 1)
        )

    def free_out(p, round_):
        before = OUT_ROUNDS.index(round_) - OUT_RING
        if before >= 0:
            left_out(p, OUT_ROUNDS[before])

    def left_out(p, round_):
        ci, bi = round_
        if ci == 2:
            c_half_copy(p, bi, 0).wait_send()
            c_half_copy(p, bi, 1).wait_send()
        else:
            c_whole_copy(p, bi, ci // 2).wait_send()

    def b_half_copy(p, second):
        return remote(
            b_out.half(3 * p, second), b_half.half(p, second), b_send.at[4 * p + second], b_recv.at[4 * p + second],
            neighbour(p, 1, 3 if second else 1),
        )

    def b_whole_copy(p, leftward):
        return remote(
            b_out.row(3 * p + 1 + leftward), b_in.row(2 * p + leftward), b_send.at[4 * p + 2 + leftward],
            b_recv.at[4 * p + 2 + leftward], neighbour(p, 1, 3 if leftward else 1),
        )

    def a_copy(p, by):
        n = 3 * p + by - 1
        return remote(a_out.at[n], a_in.at[n], a_send.at[n], a_recv.at[n], neighbour(p, 0, by))

    def opposite_row(k, p, pairs):
        _, bi = ROUNDS[k]
        free_out(p, ROUNDS[k])
        for ai in range(4):
            c_out.put(out_row(p, ROUNDS[k]), ai, chip_sum(k, p, ai, pairs))
            if ai % 2:
                c_half_copy(p, bi, ai // 2).start()

    def side_row(k, p, pairs):
        ci, bi = ROUNDS[k]
        leftward = ci // 2
        n = p * 4 + bi
        c_half_copy(p, bi, leftward).wait_recv()
        free_out(p, ROUNDS[k])
        for ai in range(4):
            value = chip_sum(k, p, ai, pairs)
            if ai // 2 == leftward:
                value = value + c_half.get(n, ai)
            c_out.put(out_row(p, ROUNDS[k]), ai, value)
        c_whole_copy(p, bi, leftward).start()

    def own_row(k, p, pairs):
        _, bi = ROUNDS[k]
        n = p * 4 + bi
        leftward = bi // 2
        c_whole_copy(p, bi, 0).wait_recv()
        c_whole_copy(p, bi, 1).wait_recv()
        if bi % 2:
            b_half_copy(p, leftward).wait_recv()
        for ai in range(4):
            value = chip_sum(k, p, ai, pairs) + c_in.get(n, ai) + c_in.get(12 + n, ai)
            if bi == 0:
                kept[p, :, ai * 128 : (ai + 1) * 128] = value
                continue
            if bi % 2 and ai // 2 == leftward:
                value = value + b_half.get(p, ai)
            b_out.put(3 * p + (0 if bi == 2 else 1 + leftward), ai, value)
            if bi == 2 and ai % 2:
                b_half_copy(p, ai // 2).start()
        if bi % 2:
            b_whole_copy(p, leftward).start()

    def vec_twin():
        return remote(vec_in.at[1 - core], vec_t.at[0], v_send.at[0], v_recv.at[0], twin)

    def vec_copy(axis, by):
        src, dst = ((vec_x, vec_x_in), (vec_y, vec_y_in), (vec_z, vec_z_in))[axis]
        n = 1 + 3 * axis + by - 1
        there = lax.rem(pos[axis] + by, 4)
        piece = src.at[there] if axis == 1 else src.at[there // 2] if axis == 0 else src
        return remote(piece, dst.at[by - 1], v_send.at[n], v_recv.at[n], axes[axis][by - 1])

    def vec_start(axis):
        for by in (1, 2, 3):
            vec_copy(axis, by).start()

    def vec_sum(axis, whole):
        dst = (vec_x_in, vec_y_in, vec_z_in)[axis]
        for by in (1, 2, 3):
            vec_copy(axis, by).wait_recv()
            whole = whole + dst[by - 1]
        return whole

    def vec_last():
        return remote(window.at[core], window.at[core], v_send.at[10], v_recv.at[10], twin)

    def vec_stage(stage):
        if stage < 0:
            vec_twin().start()
        elif stage == 0:
            vec_twin().wait_recv()
            whole = vec_in[core] + vec_t[0]
            for i in range(4):
                vec_y[i] = whole[:, 256 * i : 256 * i + 256]
            vec_start(1)
        elif stage == 1:
            whole = vec_sum(1, vec_y[pos[1]])
            for i in range(2):
                vec_x[i] = whole[:, 128 * i : 128 * i + 128]
            vec_start(0)
        elif stage == 2:
            vec_z[...] = vec_sum(0, vec_x[pos[0] // 2])
            vec_start(2)
        elif stage == 3:
            window[core] = vec_sum(2, vec_z[...])
            vec_last().start()

    def one_row(k, p, pairs=None):
        pairs = pairs or row_pairs(k, p, core)
        twin_copy(k, p).wait_recv()
        ci = ROUNDS[k][0]
        (own_row if ci == 0 else opposite_row if ci == 2 else side_row)(k, p, pairs)

    x_low = lax.rem(pos[0], 2)

    def class_at(i):
        mine = jnp.where((i == 0) | ((i >= 2) & (i < 5)), x_low, 1 - x_low)
        step = pick([2, 2, 0, 1, 3, 1, 0, 3], i)
        return mine * 4 + lax.rem(pos[2] + step, 4)

    def classes_back(first, count):
        loop(count, lambda i: heads_back(class_at(first + i)), count)

    classes_back(0, 2)
    between(-1, vec_stage)
    loop(2, lambda p: for_twin(0, p))
    classes_back(2, 3)
    for_twin(0, jnp.int32(2))
    loop(2, lambda p: one_row(0, p))
    classes_back(5, 3)
    loop(2, lambda p: for_twin(1, p))
    one_row(0, jnp.int32(2))
    for_twin(1, jnp.int32(2))
    for k in range(1, len(ROUNDS)):

        def one_round(p):
            ahead = row_pairs(k + AHEAD, p, 1 - core) if k + AHEAD < len(ROUNDS) else None
            pairs = row_pairs(k, p, core)
            for_twin(k + AHEAD, p, ahead)
            one_row(k, p, pairs)

        between(k, vec_stage)
        loop(3, one_round)

    def row_sum(p, ai):
        return kept[p, :, ai * 128 : (ai + 1) * 128] + b_in.get(2 * p, ai) + b_in.get(2 * p + 1, ai)

    def last_axis(p):
        b_whole_copy(p, 0).wait_recv()
        b_whole_copy(p, 1).wait_recv()
        for by in (2, 1, 3):
            a_out[3 * p + by - 1] = row_sum(p, by).astype(BF16)
            a_copy(p, by).start()

    loop(3, last_axis)

    wide, narrow = lax.axis_index("wide"), lax.axis_index("narrow")
    remote(window.at[1 - core], window.at[1 - core], v_send.at[10], v_recv.at[10], twin).wait_recv()
    lane = lax.broadcasted_iota(jnp.int32, (8, 128), 1) // 8
    own_lanes = lane == lax.rem(wide, 2) * 8 + narrow
    squares = jnp.zeros((8, 128), F32)
    for i in range(2):
        own = jnp.where(own_lanes, window[i], 0.0)
        squares = squares + own * own

    for p in range(3):
        value = row_sum(p, 0)
        for by in (1, 3, 2):
            a_copy(p, by).wait_recv()
            value = value + a_in[3 * p + by - 1].astype(F32)
        total[2 * p] = value[:128]
        total[2 * p + 1] = value[128:]
        squares = squares + by_eights(value * value)
    total_copy.start()

    def norm_copy(stage, i):
        n = 15 * stage + i
        to = (column if stage else plane)[i]
        return remote(tiles.at[stage], tiles.at[2 + n], n_send.at[n], n_recv.at[n], to)

    def sent(p):
        for k in range(len(ROUNDS) - RING, len(ROUNDS)):
            twin_copy(k, p).wait_send()
        for round_ in OUT_ROUNDS[-OUT_RING:]:
            left_out(p, round_)
        for side in (0, 1):
            b_half_copy(p, side).wait_send()
            b_whole_copy(p, side).wait_send()
        for by in (1, 2, 3):
            a_copy(p, by).wait_send()

    def all_sent():
        loop(3, sent)
        vec_twin().wait_send()
        vec_last().wait_send()
        for axis in range(3):
            for by in (1, 2, 3):
                vec_copy(axis, by).wait_send()

    whole = squares
    for stage, count in ((0, 15), (1, 7)):
        tiles[stage] = whole
        for i in range(count):
            norm_copy(stage, i).start()
        if stage == 0:
            all_sent()
        for i in range(count):
            norm_copy(stage, i).wait_recv()
            whole = whole + tiles[2 + 15 * stage + i]
    norm_tile[...] = whole
    for stage, count in ((0, 15), (1, 7)):
        for i in range(count):
            norm_copy(stage, i).wait_send()


def whole_kernel(
    owner, places, master_in, vectors_in, patches, keep_in, cotangent,
    output_out, input_grad_out, total_out, window, norm_tile, *scratch,
):
    gathered, scattered = scratch[:PASS_SCRATCH], scratch[PASS_SCRATCH:]
    g, left, right, flats = gathered[:4]
    vec_in, output, input_grad, total, out_sem, *scattered = scattered
    ready, ready_too = gathered[-2:]
    results = [
        pltpu.make_async_copy(src, dst, out_sem.at[i])
        for i, (src, dst) in enumerate(((output, output_out), (input_grad, input_grad_out), (total, total_out)))
    ]
    heads_back, input_side, output_side, further = pass_kernel(
        owner, places, master_in, vectors_in, patches, keep_in, cotangent, output, input_grad, total, vec_in, *gathered
    )

    def between(k, vec_stage):
        if k < 0:
            all_announced(ready, neighbours())
        elif 1 <= k <= 3:
            for n in ((), (0,), (1, 2), ())[k]:
                input_side(n)
            if k == 1:
                further()
            if k == 2:
                results[1].start()
            if k == 3:
                vec_stage(-1)
        elif 4 <= k <= 7:
            for n in ((0, 1), (2,), (3,), ())[k - 4]:
                output_side(n)
            if k == 5:
                all_announced(ready_too, others())
            if k == 7:
                results[0].start()
        if k in (5, 7, 9, 11):
            vec_stage((k - 5) // 2)

    scatter_kernel(
        gathered[TABLES], left, right, vec_in, total, window, norm_tile, g, flats, *scattered, heads_back, between, results[2]
    )
    for result in results:
        result.wait()


PASS_SCRATCH, TABLES = 26, 20


def forward_backward(*operands):
    vmem = pl.BlockSpec(memory_space=pltpu.VMEM)
    flat = (ROWS, D)
    dma = pltpu.SemaphoreType.DMA
    pass_scratch = [
        pltpu.VMEM((ALL_ROWS, 16, 128), BF16),
        pltpu.VMEM((56, 128, ROWS), BF16),
        pltpu.VMEM((72, ROWS, 128), BF16),
        pltpu.VMEM((4, *flat), F32),
        *[pltpu.VMEM(flat, BF16)] * 5,
        pltpu.VMEM((HEADS, ROWS, ROWS), BF16),
        pltpu.VMEM((3, D, D), BF16),
        pltpu.VMEM((FF, D), BF16),
        pltpu.VMEM((ROWS, ROWS), F32),
        pltpu.VMEM((NV, 8, D), F32),
        pltpu.VMEM((16, D), F32),
        pltpu.VMEM((8, NV), F32),
        pltpu.VMEM((IMAGES, PATCHES), jnp.int32),
        pltpu.VMEM((6, 128), jnp.int32),
        pltpu.VMEM((6, 128), jnp.int32),
        pltpu.VMEM((24, 128), jnp.int32),
        pltpu.SMEM((24, 128), jnp.int32),
        dma((3, 40)),
        dma((3, 40)),
        dma((8,)),
        pltpu.SemaphoreType.REGULAR,
        pltpu.SemaphoreType.REGULAR,
    ]
    assert len(pass_scratch) == PASS_SCRATCH
    return pl.pallas_call(
        whole_kernel,
        out_shape=[
            jax.ShapeDtypeStruct((TOKENS, D), BF16),
            jax.ShapeDtypeStruct((TOKENS, D), BF16),
            jax.ShapeDtypeStruct((6, SIDE, SIDE), F32),
            jax.ShapeDtypeStruct((2, 8, 128), F32),
            jax.ShapeDtypeStruct((8, 128), F32),
        ],
        in_specs=[pl.BlockSpec(memory_space=pltpu.HBM)] * 7,
        out_specs=[pl.BlockSpec(memory_space=pltpu.HBM)] * 3 + [vmem] * 2,
        scratch_shapes=pass_scratch
        + [
            pltpu.VMEM((2, 8, D), F32),
            pltpu.VMEM((TOKENS, D), BF16),
            pltpu.VMEM((TOKENS, D), BF16),
            pltpu.VMEM((6, SIDE, SIDE), F32),
            dma((3,)),
            pltpu.VMEM((9, 256, 128), BF16),
            pltpu.VMEM((9, 256, 128), BF16),
            pltpu.VMEM((4, 8, 256), F32),
            pltpu.VMEM((3, 8, 256), F32),
            pltpu.VMEM((2, 8, 128), F32),
            pltpu.VMEM((3, 8, 128), F32),
            pltpu.VMEM((8, 128), F32),
            pltpu.VMEM((3, 8, 128), F32),
            pltpu.VMEM((1, 8, D), F32),
            pltpu.VMEM((24, 8, 128), F32),
            dma((48,)), dma((48,)), dma((48,)), dma((48,)), dma((12,)), dma((12,)), dma((9,)), dma((9,)),
            dma((11,)), dma((11,)), dma((22,)), dma((22,)),
        ],
        compiler_params=pltpu.CompilerParams(
            collective_id=0, has_side_effects=True, vmem_limit_bytes=VMEM_LIMIT
        ),
        cost_estimate=pl.CostEstimate(
            flops=19_000_000_000, bytes_accessed=10_000_000, transcendentals=3_000_000
        ),
        name="forward_backward",
    )(*(in_hbm(operand) for operand in operands))


def rounded_dot(left, right, over):
    return lax.dot_general(
        left.astype(BF16), right.astype(BF16), (over, ((), ())), preferred_element_type=F32
    )


def step_kernel(
    raw, window, norm_tile, shift, master, left_stats, right_stats, left_root, right_root, vectors, vec_accum,
    output_in, input_grad_in,
    block_grads, new_left, new_right, new_master, new_copy, vec_grads, vec_accum_new, vec_new, grad_norm,
    output, input_grad, passing, sem,
):
    def copies(way):
        ends = ((output_in, output), (input_grad_in, input_grad))
        return [
            pltpu.make_async_copy(
                passing.at[i] if way else pair[0], pair[1] if way else passing.at[i], sem.at[2 * way + i]
            )
            for i, pair in enumerate(ends)
        ]

    norm = jnp.sqrt(jnp.sum(norm_tile[...], keepdims=True))
    clip = 1.0 / jnp.maximum(norm, 1.0)

    @pl.when(pl.program_id(0) == 0)
    def _():
        for copy in copies(0):
            copy.start()
        grad_norm[...] = norm
        lanes = pltpu.roll(window[...].reshape(16, 128), shift[0], 1)
        grads = clip * lanes.T[:8, :NV]
        vec_grads[...] = grads
        accum = 0.5 * vec_accum[...] + 0.5 * grads * grads
        vec_accum_new[...] = accum
        vec_new[...] = vectors[...] - 0.5 * grads / (jnp.sqrt(accum) + 1e-08)

    for i in range(raw.shape[0]):
        grads = raw[i] * clip
        block_grads[i] = grads
        new_left[i] = 0.5 * left_stats[i] + 0.5 * rounded_dot(grads, grads, ((1,), (1,)))
        new_right[i] = 0.5 * right_stats[i] + 0.5 * rounded_dot(grads, grads, ((0,), (0,)))
        way = rounded_dot(rounded_dot(left_root[i], grads, ((1,), (0,))), right_root[i], ((1,), (0,)))
        master_now = master[i] - 0.5 * way
        new_master[i] = master_now
        new_copy[i] = master_now.astype(BF16)

    @pl.when(pl.program_id(0) == 0)
    def _():
        for came, copy in zip(copies(0), copies(1)):
            came.wait()
            copy.start()

    @pl.when(pl.program_id(0) == pl.num_programs(0) - 1)
    def _():
        for copy in copies(1):
            copy.wait()


def update(raw, window, norm_tile, shift, blocks_in, vectors, vec_accum, output, input_grad):
    per = 3
    blocks = pl.BlockSpec((per, SIDE, SIDE), lambda i: (i, 0, 0))
    anywhere = pl.BlockSpec(memory_space=pltpu.HBM)

    def whole(*shape):
        return pl.BlockSpec(shape, lambda i: (0,) * len(shape))

    f32_blocks = jax.ShapeDtypeStruct((6, SIDE, SIDE), F32)
    f32_vecs = jax.ShapeDtypeStruct((8, NV), F32)
    tokens = jax.ShapeDtypeStruct((TOKENS, D), BF16)
    return pl.pallas_call(
        step_kernel,
        grid=(6 // per,),
        out_shape=[f32_blocks] * 4
        + [jax.ShapeDtypeStruct((6, SIDE, SIDE), BF16)]
        + [f32_vecs] * 3
        + [jax.ShapeDtypeStruct((1, 1), F32)]
        + [tokens] * 2,
        in_specs=[blocks, whole(2, 8, 128), whole(8, 128), pl.BlockSpec(memory_space=pltpu.SMEM)]
        + [blocks] * 5
        + [whole(8, NV)] * 2
        + [anywhere] * 2,
        out_specs=[blocks] * 5 + [whole(8, NV)] * 3 + [whole(1, 1)] + [anywhere] * 2,
        scratch_shapes=[pltpu.VMEM((2, TOKENS, D), BF16), pltpu.SemaphoreType.DMA((4,))],
        compiler_params=pltpu.CompilerParams(vmem_limit_bytes=32 * MIB),
        name="update",
    )(*(in_hbm(a) for a in (raw, window, norm_tile)), shift, *blocks_in, in_hbm(vectors), in_hbm(vec_accum), in_hbm(output), in_hbm(input_grad))


def body(
    patches, keep, cotangent, owner_table, master, left_stats, right_stats, left_root, right_root, vectors, vec_accum,
):
    wide, narrow = lax.axis_index("wide"), lax.axis_index("narrow")
    output, input_grad, raw, window, norm_tile = forward_backward(
        owner_table.reshape(6, 128), jnp.asarray(BLOCK_AT.reshape(6, 128)), master, vectors.T, patches, keep, cotangent
    )
    lane = ((wide % 2) * 8 + narrow) * 8
    shift = jnp.reshape((128 - lane) % 128, (1,)).astype(jnp.int32)
    blocks_in = (master, left_stats, right_stats, left_root, right_root)
    *of_blocks, vec_grads, vec_accum_new, vec_new, grad_norm, output, input_grad = update(
        raw, window, norm_tile, shift, blocks_in, vectors.T, vec_accum.T, output, input_grad
    )
    return (output, input_grad, *of_blocks, vec_grads.T, vec_accum_new.T, vec_new.T, grad_norm.reshape(()))


def solution(mesh):
    rows, blocks, vecs = P(BOTH, None), P(BOTH, None, None), P(None, BOTH)
    return jax.shard_map(
        body,
        mesh=mesh,
        in_specs=(rows, rows, rows, P(), blocks, blocks, blocks, blocks, blocks, vecs, vecs),
        out_specs=(rows, rows, blocks, blocks, blocks, blocks, blocks, vecs, vecs, vecs, P()),
        check_vma=False,
    )
```
